32 devices in a mesh: dp: 8 (over z, y), mp: 4 (over x, core).
Axes of the slice: x: 2, y: 2, z: 4, core: 2. Of those that a mesh axis runs over, the one named last changes fastest.
Arguments:
- latents: bfloat16 [16, 1024, 768], P('dp', 'mp'), may hold values from -6 to 6
- conditions: bfloat16 [16, 768], P('dp'), may hold values from -6 to 6
- cotangent: bfloat16 [16, 1024, 768], P('dp', 'mp'), may hold values from -6 to 6
- counts: int32 [8], P('dp'), may hold values from 1 to 2, as said below
- w_mod: float32 [768, 4608], P('dp'), may hold values from -0.21875 to 0.21875
- mom_mod: float32 [768, 4608], P('dp'), may hold values from -32 to 32
- conv_attn: float32 [9, 768], replicated, may hold values from -2 to 2
- mom_conv_attn: float32 [9, 768], replicated, may hold values from -24 to 24
- w_qkv: float32 [3, 768, 768], P(None, None, 'mp'), may hold values from -0.21875 to 0.21875
- mom_qkv: float32 [3, 768, 768], P(None, None, 'mp'), may hold values from -12 to 12
- err_qkv: float32 [8, 3, 768, 768], P('dp', None, None, 'mp'), may hold values from -32 to 32
- start_qkv: float32 [3, 768, 8], P(None, 'mp'), may hold values from -6 to 6
- w_out: float32 [768, 768], P('mp'), may hold values from -1.75 to 1.75
- mom_out: float32 [768, 768], P('mp'), may hold values from -4 to 4
- err_out: float32 [8, 768, 768], P('dp', 'mp'), may hold values from -12 to 12
- start_out: float32 [768, 8], replicated, may hold values from -6 to 6
- w_fc1: float32 [768, 3072], P(None, 'mp'), may hold values from -0.21875 to 0.21875
- mom_fc1: float32 [768, 3072], P(None, 'mp'), may hold values from -16 to 16
- err_fc1: float32 [8, 768, 3072], P('dp', None, 'mp'), may hold values from -48 to 48
- start_fc1: float32 [3072, 8], P('mp'), may hold values from -6 to 6
- conv_ffn: float32 [9, 3072], P(None, 'mp'), may hold values from -2 to 2
- mom_conv_ffn: float32 [9, 3072], P(None, 'mp'), may hold values from -16 to 16
- w_fc2: float32 [3072, 768], P('mp'), may hold values from -0.109375 to 0.109375
- mom_fc2: float32 [3072, 768], P('mp'), may hold values from -28 to 28
- err_fc2: float32 [8, 3072, 768], P('dp', 'mp'), may hold values from -80 to 80
- start_fc2: float32 [768, 8], replicated, may hold values from -6 to 6
Outputs:
- latents_out: bfloat16 [16, 1024, 768], P('dp', 'mp')
- latents_grad: bfloat16 [16, 1024, 768], P('dp', 'mp')
- w_mod_new: float32 [768, 4608], P('dp')
- mom_mod_new: float32 [768, 4608], P('dp')
- conv_attn_new: float32 [9, 768], replicated
- mom_conv_attn_new: float32 [9, 768], replicated
- w_qkv_new: float32 [3, 768, 768], P(None, None, 'mp')
- mom_qkv_new: float32 [3, 768, 768], P(None, None, 'mp')
- err_qkv_new: float32 [8, 3, 768, 768], P('dp', None, None, 'mp')
- w_out_new: float32 [768, 768], P('mp')
- mom_out_new: float32 [768, 768], P('mp')
- err_out_new: float32 [8, 768, 768], P('dp', 'mp')
- w_fc1_new: float32 [768, 3072], P(None, 'mp')
- mom_fc1_new: float32 [768, 3072], P(None, 'mp')
- err_fc1_new: float32 [8, 768, 3072], P('dp', None, 'mp')
- conv_ffn_new: float32 [9, 3072], P(None, 'mp')
- mom_conv_ffn_new: float32 [9, 3072], P(None, 'mp')
- w_fc2_new: float32 [3072, 768], P('mp')
- mom_fc2_new: float32 [3072, 768], P('mp')
- err_fc2_new: float32 [8, 3072, 768], P('dp', 'mp')
The draws below stay inside these ranges and needn't reach their ends.
Inputs may be any that keep to these rules, and one draw needn't show every extreme that they name: Index d of dp holds live latents in its first counts[d] slots; the others are padding. Some index holds 2 and some holds 1.
All inputs are finite; a program needn't handle non-finite values.
Results may differ from the reference program's by a relative error of at most 0.023.
Values may be sent and summed in bfloat16 or wider, within the bound.
No kernel may reach another device: no remote copies, remote signals or barrier semaphores. Data moves between devices by JAX's collectives and lax.ppermute only.
A program may use at most 320 MiB of HBM per device.

```python
import jax
import jax.numpy as jnp
from jax import lax

D = 768
HEADS = 12
HEAD_DIM = 64
FF = 3072
SIDE = 32
SLOTS = 2
RANK = 8
GROUPS = 8
LATENTS = 16
N_MP = 4


def draw_counts(key, part):
    first_key, second_key = jax.random.split(key)
    drawn = jax.random.randint(first_key, (GROUPS,), 1, SLOTS + 1)
    order = jax.random.permutation(second_key, GROUPS)
    drawn = drawn.at[order[0]].set(SLOTS)
    drawn = drawn.at[order[1]].set(1)
    return drawn.astype(jnp.int32)


def steps_of(rng, dims, cuts, least, top_value):
    gain = 1.0
    for position, parts in cuts:
        steps = jax.random.uniform(jax.random.fold_in(jax.random.fold_in(rng, 6), position), (parts,), jnp.float32, least / len(cuts), top_value / len(cuts))
        gain = gain * jnp.repeat(jnp.exp(steps), dims[position] // parts).reshape((-1,) + (1,) * (len(dims) - 1 - position))
    return gain


def scatter_about(stream_key, extent, spread, limit, cuts=(), held_as=jnp.bfloat16):
    level = steps_of(stream_key, extent, cuts, -0.22, 0.18) if cuts else 1.0
    array = jax.random.normal(stream_key, extent, jnp.float32) * spread * level
    return jnp.minimum(jnp.maximum(array, -limit), limit).astype(held_as)


def setup_inputs(seed: int = 0) -> dict:
    streams_of = jax.random.split(jax.random.key(seed), 27)
    latents = scatter_about(streams_of[0], (LATENTS, SIDE * SIDE, D), 1.0, 6.0, ((0, 8), (1, 4)))
    conditions = scatter_about(streams_of[1], (LATENTS, D), 1.0, 6.0, ((0, 8),))
    cotangent = scatter_about(streams_of[2], (LATENTS, SIDE * SIDE, D), 1.0, 6.0, ((0, 8), (1, 4)))
    counts = draw_counts(jax.random.fold_in(streams_of[26], 71), 0)
    w_mod = scatter_about(streams_of[4], (D, 6 * D), D ** -0.5, 0.21875, ((0, 8),), jnp.float32)
    mom_mod = scatter_about(streams_of[5], (D, 6 * D), (0.5 * SIDE * ((6 * SLOTS + 5) // 10) ** 0.5 * GROUPS ** -0.5), 32.0, ((0, 8),), jnp.float32)
    conv_attn = scatter_about(streams_of[6], (9, D), 9 ** -0.5, 2.0, (), jnp.float32)
    mom_conv_attn = scatter_about(streams_of[7], (9, D), (0.3 * (6 * SLOTS * SIDE * SIDE // 10) ** 0.5 * GROUPS ** -0.5), 24.0, (), jnp.float32)
    w_qkv = scatter_about(streams_of[8], (3, D, D), D ** -0.5, 0.21875, ((2, 4),), jnp.float32)
    mom_qkv = scatter_about(streams_of[9], (3, D, D), (0.15 * (6 * SLOTS * SIDE * SIDE // 10) ** 0.5 * GROUPS ** -0.5), 12.0, ((2, 4),), jnp.float32)
    err_qkv = scatter_about(streams_of[10], (GROUPS, 3, D, D), (0.15 * (6 * SLOTS * SIDE * SIDE // 10) ** 0.5), 32.0, ((0, 8), (3, 4)), jnp.float32)
    start_qkv = scatter_about(streams_of[11], (3, D, RANK), 1.0, 6.0, ((1, 4),), jnp.float32)
    w_out = scatter_about(streams_of[12], (D, D), (max(D // 64, 1)) ** -0.5, 1.75, ((0, 4),), jnp.float32)
    mom_out = scatter_about(streams_of[13], (D, D), (0.06 * (6 * SLOTS * SIDE * SIDE // 10) ** 0.5 * GROUPS ** -0.5), 4.0, ((0, 4),), jnp.float32)
    err_out = scatter_about(streams_of[14], (GROUPS, D, D), (0.06 * (6 * SLOTS * SIDE * SIDE // 10) ** 0.5), 12.0, ((0, 8), (1, 4)), jnp.float32)
    start_out = scatter_about(streams_of[15], (D, RANK), 1.0, 6.0, (), jnp.float32)
    w_fc1 = scatter_about(streams_of[16], (D, FF), D ** -0.5, 0.21875, ((1, 4),), jnp.float32)
    mom_fc1 = scatter_about(streams_of[17], (D, FF), (0.24 * (6 * SLOTS * SIDE * SIDE // 10) ** 0.5 * GROUPS ** -0.5), 16.0, ((1, 4),), jnp.float32)
    err_fc1 = scatter_about(streams_of[18], (GROUPS, D, FF), (0.24 * (6 * SLOTS * SIDE * SIDE // 10) ** 0.5), 48.0, ((0, 8), (2, 4)), jnp.float32)
    start_fc1 = scatter_about(streams_of[19], (FF, RANK), 1.0, 6.0, ((0, 4),), jnp.float32)
    conv_ffn = scatter_about(streams_of[20], (9, FF), 9 ** -0.5, 2.0, ((1, 4),), jnp.float32)
    mom_conv_ffn = scatter_about(streams_of[21], (9, FF), (0.2 * (6 * SLOTS * SIDE * SIDE // 10) ** 0.5 * GROUPS ** -0.5), 16.0, ((1, 4),), jnp.float32)
    w_fc2 = scatter_about(streams_of[22], (FF, D), FF ** -0.5, 0.109375, ((0, 4),), jnp.float32)
    mom_fc2 = scatter_about(streams_of[23], (FF, D), (0.36 * (6 * SLOTS * SIDE * SIDE // 10) ** 0.5 * GROUPS ** -0.5), 28.0, ((0, 4),), jnp.float32)
    err_fc2 = scatter_about(streams_of[24], (GROUPS, FF, D), (0.36 * (6 * SLOTS * SIDE * SIDE // 10) ** 0.5), 80.0, ((0, 8), (1, 4)), jnp.float32)
    start_fc2 = scatter_about(streams_of[25], (D, RANK), 1.0, 6.0, (), jnp.float32)
    return {"latents": latents, "conditions": conditions, "cotangent": cotangent, "counts": counts, "w_mod": w_mod, "mom_mod": mom_mod, "conv_attn": conv_attn, "mom_conv_attn": mom_conv_attn, "w_qkv": w_qkv, "mom_qkv": mom_qkv, "err_qkv": err_qkv, "start_qkv": start_qkv, "w_out": w_out, "mom_out": mom_out, "err_out": err_out, "start_out": start_out, "w_fc1": w_fc1, "mom_fc1": mom_fc1, "err_fc1": err_fc1, "start_fc1": start_fc1, "conv_ffn": conv_ffn, "mom_conv_ffn": mom_conv_ffn, "w_fc2": w_fc2, "mom_fc2": mom_fc2, "err_fc2": err_fc2, "start_fc2": start_fc2}


NORM_EPS = 1e-06
ORTHO_EPS = 1e-06
LEARN_RATE = 0.005
FAST_RATE = 0.025
MOMENTUM = 0.9
HIGHEST = lax.Precision.HIGHEST

@jax.custom_vjp
def low(v):
    return lax.optimization_barrier(v.astype(jnp.bfloat16)).astype(jnp.float32)

@jax.custom_vjp
def low_back(v):
    return v

def low_keep(v):
    return (low(v), None)

def low_pass(kept, grad):
    return (grad,)

def back_keep(v):
    return (v, None)

def back_low(kept, grad):
    return (low(grad),)
low.defvjp(low_keep, low_pass)
low_back.defvjp(back_keep, back_low)

def layer_norm(values):
    centred = values - lax.optimization_barrier(jnp.mean(values, -1, keepdims=True))
    variance = lax.optimization_barrier(jnp.mean(centred * centred, -1, keepdims=True))
    return centred * lax.rsqrt(variance + NORM_EPS)

def conv_grid(values, kernel):
    channels = values.shape[-1]
    padded = jnp.pad(values.reshape(SIDE, SIDE, channels), ((1, 1), (1, 1), (0, 0)))
    summed = jnp.zeros((SIDE, SIDE, channels), jnp.float32)
    for vertical in range(3):
        for lateral in range(3):
            summed = summed + kernel[3 * vertical + lateral] * padded[vertical:vertical + SIDE, lateral:lateral + SIDE]
    return summed.reshape(SIDE * SIDE, channels)

def to_groups(values):
    channels = values.shape[-1]
    shaped = values.reshape(SIDE // 2, 2, SIDE // 2, 2, channels).transpose(1, 3, 0, 2, 4)
    return shaped.reshape(4, (SIDE // 2) ** 2, channels)

def from_groups(values):
    channels = values.shape[-1]
    shaped = values.reshape(2, 2, SIDE // 2, SIDE // 2, channels).transpose(2, 0, 3, 1, 4)
    return shaped.reshape(SIDE * SIDE, channels)

def orthonormal(factor):
    columns = []
    for column in range(factor.shape[-1]):
        current = factor[..., column]
        for earlier in columns:
            current = current - lax.optimization_barrier(jnp.sum(earlier * current, -1, keepdims=True)) * earlier
        current = current * lax.rsqrt(lax.optimization_barrier(jnp.sum(current * current, -1, keepdims=True)) + ORTHO_EPS)
        columns.append(current)
    return jnp.stack(columns, -1)

def split_heads(values):
    return to_groups(values).reshape(4, -1, HEADS, HEAD_DIM)

def attention(query, keyed, valued):
    score_scale = HEAD_DIM ** (-0.5)
    scores = jnp.einsum('aqhe,akhe->ahqk', split_heads(query), split_heads(keyed), precision=HIGHEST) * score_scale
    scores = low_back(scores)
    probs = low(jax.nn.softmax(scores, -1))
    attended = jnp.einsum('ahqk,akhe->aqhe', probs, split_heads(valued), precision=HIGHEST)
    return from_groups(attended.reshape(4, -1, D))

def block_forward(latent, modulation, conv_attn, w_qkv, w_out, w_fc1, conv_ffn, w_fc2):
    shift_one = modulation[0]
    scale_one = modulation[1]
    gate_one = modulation[2]
    shift_two = modulation[3]
    scale_two = modulation[4]
    gate_two = modulation[5]
    token_count = latent.shape[0]
    normed_one = layer_norm(latent)
    conv_low = low(conv_grid(normed_one * (1.0 + scale_one) + shift_one, conv_attn))
    projected = low(low_back(jnp.einsum('ld,tde->tle', conv_low, low(w_qkv), precision=HIGHEST)))
    attended = low(low_back(jax.checkpoint(attention)(projected[0], projected[1], projected[2])))
    attn_parts = jnp.einsum('ljc,jcd->jld', attended.reshape(token_count, N_MP, D // N_MP), low(w_out).reshape(N_MP, D // N_MP, D), precision=HIGHEST)
    attn_out = low_back(lax.optimization_barrier(jnp.sum(low(attn_parts), 0)))
    residual = latent + gate_one * attn_out
    mixed_low = low(layer_norm(residual) * (1.0 + scale_two) + shift_two)
    hidden = low_back(jnp.dot(mixed_low, low(w_fc1), precision=HIGHEST))
    act_low = low(jax.nn.gelu(conv_grid(hidden, conv_ffn), approximate=True))
    ffn_parts = jnp.einsum('ljc,jcd->jld', act_low.reshape(token_count, N_MP, FF // N_MP), low(w_fc2).reshape(N_MP, FF // N_MP, D), precision=HIGHEST)
    ffn_out = low_back(lax.optimization_barrier(jnp.sum(low(ffn_parts), 0)))
    return residual + gate_two * ffn_out

def device_pass(latent_rows, condition_rows, cotangent_rows, live_mask, weights):

    def forward(latents_in, w_mod, conv_attn, w_qkv, w_out, w_fc1, conv_ffn, w_fc2):
        modulation = jnp.dot(low(jax.nn.silu(condition_rows)), low(w_mod), precision=HIGHEST).reshape(-1, 6, D)

        def one_latent(entries):
            return block_forward(entries[0], entries[1], conv_attn, w_qkv, w_out, w_fc1, conv_ffn, w_fc2) * entries[2]
        return lax.map(one_latent, (latents_in, modulation, live_mask))
    outputs, backward = jax.vjp(forward, latent_rows, *weights)
    return (outputs, backward(cotangent_rows))

def momentum_update(weight, moment, gradient, rate):
    new_moment = MOMENTUM * moment + gradient
    return (weight - rate * new_moment, new_moment)

def reference(latents, conditions, cotangent, counts, w_mod, mom_mod, conv_attn, mom_conv_attn, w_qkv, mom_qkv, err_qkv, start_qkv, w_out, mom_out, err_out, start_out, w_fc1, mom_fc1, err_fc1, start_fc1, conv_ffn, mom_conv_ffn, w_fc2, mom_fc2, err_fc2, start_fc2):
    slot_index = jnp.arange(SLOTS, dtype=jnp.int32)
    live_all = (slot_index[None, :] < counts[:, None].astype(jnp.int32)).astype(jnp.float32)
    weights = (w_mod, conv_attn, w_qkv, w_out, w_fc1, conv_ffn, w_fc2)

    def per_device(entries):
        return device_pass(entries[0], entries[1], entries[2], entries[3], weights)
    lat_rows = latents.astype(jnp.float32).reshape(GROUPS, SLOTS, SIDE * SIDE, D)
    cond_rows = conditions.astype(jnp.float32).reshape(GROUPS, SLOTS, D)
    cot_rows = cotangent.astype(jnp.float32).reshape(GROUPS, SLOTS, SIDE * SIDE, D)
    outputs, grads = lax.map(per_device, (lat_rows, cond_rows, cot_rows, live_all))
    latents_out = outputs.reshape(LATENTS, SIDE * SIDE, D).astype(jnp.bfloat16)
    latents_grad = grads[0].reshape(LATENTS, SIDE * SIDE, D).astype(jnp.bfloat16)
    w_mod_new, mom_mod_new = momentum_update(w_mod, mom_mod, lax.optimization_barrier(jnp.sum(grads[1], 0)) / GROUPS, LEARN_RATE)
    conv_attn_new, mom_conv_attn_new = momentum_update(conv_attn, mom_conv_attn, lax.optimization_barrier(jnp.sum(grads[2], 0)) / GROUPS, LEARN_RATE)
    conv_ffn_new, mom_conv_ffn_new = momentum_update(conv_ffn, mom_conv_ffn, lax.optimization_barrier(jnp.sum(grads[6], 0)) / GROUPS, FAST_RATE)
    head_cols = D // N_MP
    unit_cols = FF // N_MP
    merged_qkv = grads[3] + err_qkv
    blocks = merged_qkv.reshape(GROUPS, 3, D, N_MP, head_cols)
    starts = start_qkv.reshape(3, N_MP, head_cols, RANK)
    left = orthonormal(jnp.einsum('ntdjo,tjor->jdr', blocks, starts, precision=HIGHEST) / GROUPS)
    right = jnp.einsum('ntdjo,jdr->tjor', blocks, left, precision=HIGHEST) / GROUPS
    approx_qkv = jnp.einsum('jdr,tjor->tdjo', left, right, precision=HIGHEST).reshape(3, D, D)
    err_qkv_new = merged_qkv - approx_qkv[None]
    w_qkv_new, mom_qkv_new = momentum_update(w_qkv, mom_qkv, approx_qkv, LEARN_RATE)
    merged_out = grads[4] + err_out
    blocks = merged_out.reshape(GROUPS, N_MP, head_cols, D)
    left = orthonormal(jnp.einsum('njcd,dr->jcr', blocks, start_out, precision=HIGHEST) / GROUPS)
    right = jnp.einsum('njcd,jcr->jdr', blocks, left, precision=HIGHEST) / GROUPS
    approx_out = jnp.einsum('jcr,jdr->jcd', left, right, precision=HIGHEST).reshape(D, D)
    err_out_new = merged_out - approx_out[None]
    w_out_new, mom_out_new = momentum_update(w_out, mom_out, approx_out, FAST_RATE)
    merged_fc1 = grads[5] + err_fc1
    blocks = merged_fc1.reshape(GROUPS, D, N_MP, unit_cols)
    starts = start_fc1.reshape(N_MP, unit_cols, RANK)
    left = orthonormal(jnp.einsum('ndjf,jfr->jdr', blocks, starts, precision=HIGHEST) / GROUPS)
    right = jnp.einsum('ndjf,jdr->jfr', blocks, left, precision=HIGHEST) / GROUPS
    approx_fc1 = jnp.einsum('jdr,jfr->djf', left, right, precision=HIGHEST).reshape(D, FF)
    err_fc1_new = merged_fc1 - approx_fc1[None]
    w_fc1_new, mom_fc1_new = momentum_update(w_fc1, mom_fc1, approx_fc1, LEARN_RATE)
    merged_fc2 = grads[7] + err_fc2
    blocks = merged_fc2.reshape(GROUPS, N_MP, unit_cols, D)
    left = orthonormal(jnp.einsum('njfd,dr->jfr', blocks, start_fc2, precision=HIGHEST) / GROUPS)
    right = jnp.einsum('njfd,jfr->jdr', blocks, left, precision=HIGHEST) / GROUPS
    approx_fc2 = jnp.einsum('jfr,jdr->jfd', left, right, precision=HIGHEST).reshape(FF, D)
    err_fc2_new = merged_fc2 - approx_fc2[None]
    w_fc2_new, mom_fc2_new = momentum_update(w_fc2, mom_fc2, approx_fc2, LEARN_RATE)
    return (latents_out, latents_grad, w_mod_new, mom_mod_new, conv_attn_new, mom_conv_attn_new, w_qkv_new, mom_qkv_new, err_qkv_new, w_out_new, mom_out_new, err_out_new, w_fc1_new, mom_fc1_new, err_fc1_new, conv_ffn_new, mom_conv_ffn_new, w_fc2_new, mom_fc2_new, err_fc2_new)
```

```python
import functools

import jax
import jax.numpy as jnp
from jax import lax
from jax.experimental import pallas as pl
from jax.experimental.pallas import tpu as pltpu
from jax.sharding import PartitionSpec as P

HEAD_DIM = 64
SIDE = 32
HALF = SIDE // 2
PHASE = HALF * HALF
TOKENS = SIDE * SIDE
PADDED = PHASE + 2 * HALF
LANES = 256
ROWS = 32

NORM_EPS = 1e-06
ORTHO_EPS = 1e-06
LEARN_RATE = 0.005
FAST_RATE = 0.025
MOMENTUM = 0.9
HIGHEST = lax.Precision.HIGHEST
GELU_C = 0.7978845608
GELU_A = 0.044715

f32 = jnp.float32
bf16 = jnp.bfloat16
VMEM = pl.BlockSpec(memory_space=pltpu.VMEM)
SMEM = pl.BlockSpec(memory_space=pltpu.SMEM)


def params(mib, **more):
    return pltpu.CompilerParams(vmem_limit_bytes=mib << 20, **more)


def cost(flops, nbytes, trans=0):
    return pl.CostEstimate(flops=flops, bytes_accessed=nbytes, transcendentals=trans)


def dot_nn(a, b):
    return lax.dot_general(a, b, (((1,), (0,)), ((), ())), preferred_element_type=f32)


def dot_nt(a, b):
    return lax.dot_general(a, b, (((1,), (1,)), ((), ())), preferred_element_type=f32)


def dot_tn(a, b):
    return lax.dot_general(a, b, (((0,), (0,)), ((), ())), preferred_element_type=f32)


def taps_of(a, b):
    rows = (((1, -1), (0, 0), (1, 0)) if a == 0 else ((0, 0), (1, 0), (0, 1)))
    cols = (((1, True), (0, False), (1, False)) if b == 0 else ((0, False), (1, False), (0, True)))
    return [
        (3 * i + j, 2 * rows[i][0] + cols[j][0], cols[j][1], rows[i][1])
        for i in range(3)
        for j in range(3)
    ]


TAPS = [taps_of(g // 2, g % 2) for g in range(4)]


def shift_columns(values, phase):
    place = lax.broadcasted_iota(jnp.int32, values.shape, 0)
    if phase % 2 == 1:
        return jnp.where(place == 0, 0.0, pltpu.roll(values, 1, 0))
    return jnp.where(place == HALF - 1, 0.0, pltpu.roll(values, HALF - 1, 0))


def zero_edges(*buffers):
    for buffer in buffers:
        lanes = buffer.shape[-1]
        for g in range(4):
            buffer[g, 0:HALF, :] = jnp.zeros((HALF, lanes), f32)
            buffer[g, HALF + PHASE : PADDED, :] = jnp.zeros((HALF, lanes), f32)


def tap_rows(plain, shifted, g, tap, row, lanes):
    _, phase, moved, step = TAPS[g][tap]
    buffer = shifted if moved else plain
    start = pl.multiple_of(HALF + (row + step) * HALF, HALF)
    return buffer[phase, pl.ds(start, HALF), lanes]


def spread_kernel(k_ref, lanes, flip):
    width = lanes.stop - lanes.start
    return [
        jnp.broadcast_to(k_ref[(8 - t if flip else t) : (8 - t if flip else t) + 1, lanes], (8, width))
        for t in range(9)
    ]


def conv_row(plain, shifted, spread, g, row, lanes):
    width = lanes.stop - lanes.start
    total = None
    for t in range(9):
        value = tap_rows(plain, shifted, g, t, row, lanes).reshape(2, 8, width)
        term = spread[t][None] * value
        total = term if total is None else total + term
    return total.reshape(HALF, width)


def kernel_sums(plain, shifted, grads, lanes):
    width = lanes.stop - lanes.start

    def body(row, sums):
        sums = list(sums)
        for g in range(4):
            start = pl.multiple_of(HALF + row * HALF, HALF)
            grad = grads[g, pl.ds(start, HALF), lanes].reshape(2, 8, width)
            for t in range(9):
                value = tap_rows(plain, shifted, g, t, row, lanes).reshape(2, 8, width)
                term = value * grad
                sums[t] = sums[t] + (term[0] + term[1])
        return tuple(sums)

    return lax.fori_loop(0, HALF, body, tuple(jnp.zeros((8, width), f32) for _ in range(9)))


def grid_permutation(inverse):
    size = 8 * SIDE
    token = lax.broadcasted_iota(jnp.int32, (size, size), 0 if inverse else 1)
    place = lax.broadcasted_iota(jnp.int32, (size, size), 1 if inverse else 0)
    r, c = token >> 5, token & 31
    target = ((r & 1) * 2 + (c & 1)) * 64 + (r >> 1) * HALF + (c >> 1)
    return jnp.where(target == place, 1.0, 0.0).astype(bf16)


def enter_kernel(slot_ref, lat_ref, cot_ref, own_l, own_c, snd_l, snd_c):
    perm = grid_permutation(False)
    mine = slot_ref[0]
    other = 1 - mine
    own_l[...] = dot_nn(perm, lat_ref[mine]).astype(bf16)
    snd_l[...] = dot_nn(perm, lat_ref[other]).astype(bf16)
    own_c[...] = dot_nn(perm, cot_ref[mine]).astype(bf16)
    snd_c[...] = dot_nn(perm, cot_ref[other]).astype(bf16)


def enter(slot, latents, cotangent):
    share, width = latents.shape[1:]
    piece = jax.ShapeDtypeStruct((share, width), bf16)
    return pl.pallas_call(
        enter_kernel,
        out_shape=(piece,) * 4,
        in_specs=[SMEM, VMEM, VMEM],
        out_specs=(VMEM,) * 4,
        compiler_params=params(24),
        cost_estimate=cost(4 * 2 * share * share * width, 12 * share * width),
        name="enter",
    )(slot, latents, cotangent)


def pack_attn_kernel(qkv_ref, out_ref, packed):
    local = qkv_ref.shape[2]
    row = lax.broadcasted_iota(jnp.int32, (local, local), 0)
    col = lax.broadcasted_iota(jnp.int32, (local, local), 1)
    eye = jnp.where(row == col, 1.0, 0.0).astype(bf16)
    for t in range(3):
        packed[t * local : (t + 1) * local, :] = dot_nt(eye, qkv_ref[t].astype(bf16)).astype(bf16)
    packed[3 * local : 4 * local, :] = out_ref[...].astype(bf16)


def pack_attn(w_qkv, w_out):
    local, width = w_out.shape
    return pl.pallas_call(
        pack_attn_kernel,
        out_shape=jax.ShapeDtypeStruct((4 * local, width), bf16),
        in_specs=[VMEM, VMEM],
        out_specs=VMEM,
        compiler_params=params(24),
        cost_estimate=cost(6 * local * local * width, 24 * local * width),
        name="pack_attn",
    )(w_qkv, w_out)


def norm_rows(values):
    mean = jnp.mean(values, -1, keepdims=True)
    centred = values - mean
    variance = jnp.mean(centred * centred, -1, keepdims=True)
    scale = lax.rsqrt(variance + NORM_EPS)
    return centred * scale, scale


def place_pieces(midx_ref, pieces, whole):
    for i, piece in enumerate(pieces):
        block = midx_ref[i]
        for g in range(4):
            start = pl.multiple_of(g * PHASE + block * 64, 64)
            whole[pl.ds(start, 64), :] = piece[g * 64 : (g + 1) * 64, :]


def fill_shifted(lat_ref, mod_ref, plain, shifted):
    gain = 1.0 + mod_ref[1:2, :]
    bias = mod_ref[0:1, :]
    for g in range(4):

        def body(j, carry):
            values = lat_ref[pl.ds(pl.multiple_of(g * PHASE + j * ROWS, ROWS), ROWS), :].astype(f32)
            normed, _ = norm_rows(values)
            result = normed * gain + bias
            start = pl.multiple_of(HALF + j * ROWS, HALF)
            plain[g, pl.ds(start, ROWS), :] = result
            for h in range(ROWS // HALF):
                part = result[h * HALF : (h + 1) * HALF]
                shifted[g, pl.ds(start + h * HALF, HALF), :] = shift_columns(part, g)
            return carry

        lax.fori_loop(0, PHASE // ROWS, body, 0)


def first_conv_kernel(midx_ref, p0, p1, p2, p3, mod_ref, k_ref, lat_ref, conv_ref, plain, shifted):
    place_pieces(midx_ref, (p0, p1, p2, p3), lat_ref)
    zero_edges(plain, shifted)
    fill_shifted(lat_ref, mod_ref, plain, shifted)
    for first in range(0, conv_ref.shape[1], LANES):
        lanes = slice(first, first + LANES)
        spread = spread_kernel(k_ref, lanes, False)
        for g in range(4):

            def body(row, carry):
                result = conv_row(plain, shifted, spread, g, row, lanes)
                start = pl.multiple_of(g * PHASE + row * HALF, HALF)
                conv_ref[pl.ds(start, HALF), lanes] = result.astype(bf16)
                return carry

            lax.fori_loop(0, HALF, body, 0)


def first_conv(midx, pieces, mod, kernel):
    width = pieces[0].shape[1]
    whole = jax.ShapeDtypeStruct((TOKENS, width), bf16)
    return pl.pallas_call(
        first_conv_kernel,
        out_shape=(whole, whole),
        in_specs=[SMEM] + [VMEM] * 6,
        out_specs=(VMEM, VMEM),
        scratch_shapes=[pltpu.VMEM((4, PADDED, width), f32)] * 2,
        compiler_params=params(32),
        cost_estimate=cost(30 * TOKENS * width, 6 * TOKENS * width),
        name="first_conv",
    )(midx, *pieces, mod, kernel)


def head_mask(shape, half):
    lane = lax.broadcasted_iota(jnp.int32, shape, 1)
    return (lane < HEAD_DIM) if half == 0 else (lane >= HEAD_DIM)


def attn_forward_kernel(conv_ref, wa_ref, wb_ref, wcat, proj_ref, att_t_ref, lse_ref, part_ref):
    local = wa_ref.shape[0] // 4
    both = 2 * local

    @pl.when(pl.program_id(0) == 0)
    def _():
        for t in range(4):
            wcat[t * both : t * both + local, :] = wa_ref[t * local : (t + 1) * local, :]
            wcat[t * both + local : (t + 1) * both, :] = wb_ref[t * local : (t + 1) * local, :]

    proj_ref[...] = dot_nt(conv_ref[...], wcat[0 : 3 * both, :]).astype(bf16)
    for pair in range(both // 128):
        q = proj_ref[:, pair * 128 : (pair + 1) * 128] * jnp.asarray(HEAD_DIM**-0.5, bf16)
        k = proj_ref[:, both + pair * 128 : both + (pair + 1) * 128]
        v = proj_ref[:, 2 * both + pair * 128 : 2 * both + (pair + 1) * 128]
        v_t = v.T
        for half in range(2):
            q_half = jnp.where(head_mask(q.shape, half), q, jnp.zeros_like(q))
            scores = dot_nt(k, q_half)
            top = jnp.max(scores, 0, keepdims=True)
            weights = jnp.exp(scores - top)
            total = jnp.sum(weights, 0, keepdims=True)
            probs = (weights * (1.0 / total)).astype(bf16)
            head = 2 * pair + half
            lse_ref[head : head + 1, :] = top + jnp.log(total)
            out_t = dot_nn(v_t[half * HEAD_DIM : (half + 1) * HEAD_DIM, :], probs)
            att_t_ref[head * HEAD_DIM : (head + 1) * HEAD_DIM, :] = out_t.astype(bf16)
    part_ref[...] = dot_tn(att_t_ref[...], wcat[3 * both : 4 * both, :]).astype(bf16)


def attn_forward(conv_low, wa, wb):
    rows, width = wa.shape
    both = rows // 2
    block = lambda g: (g, 0)
    fixed = lambda g: (0, 0)
    return pl.pallas_call(
        attn_forward_kernel,
        grid=(4,),
        out_shape=(
            jax.ShapeDtypeStruct((2 * rows, width), bf16),
            jax.ShapeDtypeStruct((TOKENS, 3 * both), bf16),
            jax.ShapeDtypeStruct((4, both, PHASE), bf16),
            jax.ShapeDtypeStruct((4, 8, PHASE), f32),
            jax.ShapeDtypeStruct((TOKENS, width), bf16),
        ),
        in_specs=[
            pl.BlockSpec((PHASE, width), block),
            pl.BlockSpec((rows, width), fixed),
            pl.BlockSpec((rows, width), fixed),
        ],
        out_specs=(
            pl.BlockSpec((2 * rows, width), fixed),
            pl.BlockSpec((PHASE, 3 * both), block),
            pl.BlockSpec((None, both, PHASE), lambda g: (g, 0, 0)),
            pl.BlockSpec((None, 8, PHASE), lambda g: (g, 0, 0)),
            pl.BlockSpec((PHASE, width), block),
        ),
        compiler_params=params(48),
        cost_estimate=cost(8 * TOKENS * both * width + 8 * TOKENS * PHASE * both, 16 << 20),
        name="attn_forward",
    )(conv_low, wa, wb)


def second_norm_kernel(midx_ref, lat_ref, po_ref, pr_ref, c0, c1, c2, c3, mod_ref, mixed, mixed_t, fgl, cot):
    place_pieces(midx_ref, (c0, c1, c2, c3), cot)
    gate_one = mod_ref[2:3, :]
    bias = mod_ref[3:4, :]
    gain = 1.0 + mod_ref[4:5, :]
    gate_two = mod_ref[5:6, :]
    live = mod_ref[6:7, :]

    def body(j, carry):
        rows = pl.ds(pl.multiple_of(j * ROWS, ROWS), ROWS)
        attn = po_ref[rows, :].astype(f32) + pr_ref[rows, :].astype(f32)
        resid = lat_ref[rows, :].astype(f32) + gate_one * attn
        normed, _ = norm_rows(resid)
        mixed[rows, :] = (normed * gain + bias).astype(bf16)
        grad = live * cot[rows, :].astype(f32)
        cot[rows, :] = grad.astype(bf16)
        fgl[rows, :] = (gate_two * grad).astype(bf16)
        return carry

    lax.fori_loop(0, TOKENS // ROWS, body, 0)
    mixed_t[...] = mixed[...].T


def second_norm(midx, lat, own, got, cots, mod):
    width = lat.shape[1]
    whole = jax.ShapeDtypeStruct((TOKENS, width), bf16)
    return pl.pallas_call(
        second_norm_kernel,
        out_shape=(whole, jax.ShapeDtypeStruct((width, TOKENS), bf16), whole, whole),
        in_specs=[SMEM] + [VMEM] * 8,
        out_specs=(VMEM,) * 4,
        compiler_params=params(32),
        cost_estimate=cost(20 * TOKENS * width, 16 * TOKENS * width),
        name="second_norm",
    )(midx, lat, own, got, *cots, mod)


def ffn_kernel(first, mixed, mixed_t, fgl, w1_ref, w2_ref, k_ref, *rest):
    if first:
        ffn_out, mix_out, g1_ref, g2_ref, kg_ref = rest[:5]
        scratch = rest[5:]
    else:
        ffn_in, mix_in, ffn_out, mix_out, g1_ref, g2_ref, kg_ref = rest[:7]
        scratch = rest[7:]
    plain, shifted, grad, grad_shifted, act, hidden_grad, ffn_acc, mix_acc = scratch
    step = pl.program_id(0)
    lanes = slice(0, w1_ref.shape[1])

    @pl.when(step == 0)
    def _():
        zero_edges(plain, shifted, grad, grad_shifted)
        if first:
            ffn_acc[...] = jnp.zeros_like(ffn_acc)
            mix_acc[...] = jnp.zeros_like(mix_acc)
        else:
            ffn_acc[...] = ffn_in[...].astype(f32)
            mix_acc[...] = mix_in[...].astype(f32)

    for g in range(4):
        rows = slice(g * PHASE, (g + 1) * PHASE)
        plain[g, HALF : HALF + PHASE, :] = dot_nn(mixed[rows, :], w1_ref[...])
        grad[g, HALF : HALF + PHASE, :] = dot_nt(fgl[rows, :], w2_ref[...])
    for g in range(4):

        def shift_body(row, carry):
            rows = pl.ds(pl.multiple_of(HALF + row * HALF, HALF), HALF)
            shifted[g, rows, :] = shift_columns(plain[g, rows, :], g)
            return carry

        lax.fori_loop(0, HALF, shift_body, 0)
    spread = spread_kernel(k_ref, lanes, False)
    for g in range(4):

        def act_body(row, carry):
            pre = conv_row(plain, shifted, spread, g, row, lanes)
            square = pre * pre
            tanh = jnp.tanh(pre * (GELU_C + (GELU_C * GELU_A) * square))
            half = 0.5 + 0.5 * tanh
            rows = pl.ds(pl.multiple_of(g * PHASE + row * HALF, HALF), HALF)
            act[rows, :] = (pre * half).astype(bf16)
            slope = half + (0.5 * pre) * (1.0 - tanh * tanh) * (
                GELU_C + (3.0 * GELU_C * GELU_A) * square
            )
            padded = pl.ds(pl.multiple_of(HALF + row * HALF, HALF), HALF)
            result = grad[g, padded, :] * slope
            grad[g, padded, :] = result
            grad_shifted[g, padded, :] = shift_columns(result, g)
            return carry

        lax.fori_loop(0, HALF, act_body, 0)
    flipped = spread_kernel(k_ref, lanes, True)
    for g in range(4):

        def back_body(row, carry):
            result = conv_row(grad, grad_shifted, flipped, g, row, lanes)
            rows = pl.ds(pl.multiple_of(g * PHASE + row * HALF, HALF), HALF)
            hidden_grad[rows, :] = result.astype(bf16)
            return carry

        lax.fori_loop(0, HALF, back_body, 0)
    sums = kernel_sums(plain, shifted, grad, lanes)
    for t in range(9):
        kg_ref[t : t + 1, :] = jnp.sum(sums[t], 0, keepdims=True)
    g2_ref[...] = dot_tn(act[...], fgl[...]).astype(g2_ref.dtype)
    g1_ref[...] = dot_nn(mixed_t[...], hidden_grad[...]).astype(g1_ref.dtype)
    for g in range(4):
        rows = slice(g * PHASE, (g + 1) * PHASE)
        ffn_acc[rows, :] += dot_nn(act[rows, :], w2_ref[...])
        mix_acc[rows, :] += dot_nt(hidden_grad[rows, :], w1_ref[...])

    @pl.when(step == pl.num_programs(0) - 1)
    def _():
        ffn_out[...] = ffn_acc[...].astype(ffn_out.dtype)
        mix_out[...] = mix_acc[...].astype(mix_out.dtype)


def ffn(mixed, mixed_t, fgl, w1, w2, kernel, before, grad_type):
    width, units = w1.shape
    first = before is None
    fixed = lambda i: (0, 0)
    whole = pl.BlockSpec((TOKENS, width), fixed)
    part_type = f32 if first else bf16
    padded = pltpu.VMEM((4, PADDED, LANES), f32)
    in_specs = [
        whole,
        pl.BlockSpec((width, TOKENS), fixed),
        whole,
        pl.BlockSpec((width, LANES), lambda i: (0, i)),
        pl.BlockSpec((LANES, width), lambda i: (i, 0)),
        pl.BlockSpec((9, LANES), lambda i: (0, i)),
    ]
    operands = [mixed, mixed_t, fgl, w1, w2, kernel]
    if not first:
        in_specs += [whole, whole]
        operands += list(before)
    return pl.pallas_call(
        functools.partial(ffn_kernel, first),
        grid=(units // LANES,),
        out_shape=(
            jax.ShapeDtypeStruct((TOKENS, width), part_type),
            jax.ShapeDtypeStruct((TOKENS, width), part_type),
            jax.ShapeDtypeStruct((width, units), grad_type),
            jax.ShapeDtypeStruct((units, width), grad_type),
            jax.ShapeDtypeStruct((9, units), f32),
        ),
        in_specs=in_specs,
        out_specs=(
            whole,
            whole,
            pl.BlockSpec((width, LANES), lambda i: (0, i)),
            pl.BlockSpec((LANES, width), lambda i: (i, 0)),
            pl.BlockSpec((9, LANES), lambda i: (0, i)),
        ),
        scratch_shapes=[padded] * 4
        + [pltpu.VMEM((TOKENS, LANES), bf16)] * 2
        + [pltpu.VMEM((TOKENS, width), f32)] * 2,
        compiler_params=params(58),
        cost_estimate=cost(12 * TOKENS * width * units, 20 << 20),
        name="ffn",
    )(*operands)


def attn_backward_kernel(
    lat_ref, po_ref, pr_ref, cot_ref, mo_ref, mr_ref, mod_ref, conv_ref, proj_ref, att_t_ref, lse_ref, wcat,
    part_ref, resid_ref, mine_ref, send_ref, sums_ref,
    low, proj_t, grads, sums,
):
    step = pl.program_id(0)
    both = wcat.shape[0] // 4
    local = both // 2
    width = wcat.shape[1]

    @pl.when(step == 0)
    def _():
        grads[...] = jnp.zeros_like(grads)
        sums[...] = jnp.zeros_like(sums)

    gate_one = mod_ref[2:3, :]
    gain = 1.0 + mod_ref[4:5, :]

    def fold(values):
        return jnp.sum(values.reshape(ROWS // 8, 8, width), 0)

    def body(j, carry):
        rows = pl.ds(pl.multiple_of(j * ROWS, ROWS), ROWS)
        attn = po_ref[rows, :].astype(f32) + pr_ref[rows, :].astype(f32)
        resid = lat_ref[rows, :].astype(f32) + gate_one * attn
        normed, scale = norm_rows(resid)
        mixed = mo_ref[rows, :].astype(f32) + mr_ref[rows, :].astype(f32)
        u = mixed * gain
        mean_u = jnp.mean(u, -1, keepdims=True)
        mean_un = jnp.mean(u * normed, -1, keepdims=True)
        grad = cot_ref[rows, :].astype(f32) + scale * (u - mean_u - normed * mean_un)
        resid_ref[rows, :] = grad
        low[rows, :] = (gate_one * grad).astype(bf16)
        sums[0] += fold(attn * grad)
        sums[1] += fold(mixed)
        sums[2] += fold(mixed * normed)
        return carry

    lax.fori_loop(0, PHASE // ROWS, body, 0)
    w_out = wcat[3 * both : 4 * both, :]
    d_att = dot_nt(low[...], w_out).astype(bf16)
    d_att_t = dot_nt(w_out, low[...]).astype(bf16)
    scale = HEAD_DIM**-0.5
    for pair in range(both // 128):
        q = proj_ref[:, pair * 128 : (pair + 1) * 128] * jnp.asarray(scale, bf16)
        k = proj_ref[:, both + pair * 128 : both + (pair + 1) * 128]
        v = proj_ref[:, 2 * both + pair * 128 : 2 * both + (pair + 1) * 128]
        d_out = d_att[:, pair * 128 : (pair + 1) * 128]
        q_t = q.T
        k_t = k.T
        for half in range(2):
            head = 2 * pair + half
            own = slice(half * HEAD_DIM, (half + 1) * HEAD_DIM)
            mask = head_mask(q.shape, half)
            scores = dot_nt(k, jnp.where(mask, q, jnp.zeros_like(q)))
            probs = jnp.exp(scores - lse_ref[head : head + 1, :])
            prob_grad = dot_nt(v, jnp.where(mask, d_out, jnp.zeros_like(d_out)))
            mean = jnp.sum(probs * prob_grad, 0, keepdims=True)
            score_grad = (probs * (prob_grad - mean)).astype(bf16)
            low_probs = probs.astype(bf16)
            d_head = d_att_t[head * HEAD_DIM : (head + 1) * HEAD_DIM, :]
            at = head * HEAD_DIM
            proj_t[at : at + HEAD_DIM, :] = (dot_nn(k_t[own, :], score_grad) * scale).astype(bf16)
            proj_t[both + at : both + at + HEAD_DIM, :] = dot_nt(q_t[own, :], score_grad).astype(bf16)
            proj_t[2 * both + at : 2 * both + at + HEAD_DIM, :] = dot_nt(d_head, low_probs).astype(bf16)
    part_ref[...] = dot_tn(proj_t[...], wcat[0 : 3 * both, :]).astype(bf16)
    grads[0 : 3 * both, :] += dot_nn(proj_t[...], conv_ref[...])
    grads[3 * both : 4 * both, :] += dot_nn(att_t_ref[...], low[...])

    @pl.when(step == pl.num_programs(0) - 1)
    def _():
        for t in range(4):
            mine_ref[t * local : (t + 1) * local, :] = grads[t * both : t * both + local, :]
            send_ref[t * local : (t + 1) * local, :] = grads[t * both + local : (t + 1) * both, :].astype(bf16)
        for t in range(3):
            sums_ref[t : t + 1, :] = jnp.sum(sums[t], 0, keepdims=True)
        sums_ref[3:8, :] = jnp.zeros((5, width), f32)


def attn_backward(lat, part_own, part_got, cot, mix_own, mix_got, mod, conv_low, proj, att_t, lse, wcat):
    both = wcat.shape[0] // 4
    width = lat.shape[1]
    block = lambda g: (g, 0)
    fixed = lambda g: (0, 0)
    token = pl.BlockSpec((PHASE, width), block)
    return pl.pallas_call(
        attn_backward_kernel,
        grid=(4,),
        out_shape=(
            jax.ShapeDtypeStruct((TOKENS, width), bf16),
            jax.ShapeDtypeStruct((TOKENS, width), f32),
            jax.ShapeDtypeStruct((2 * both, width), f32),
            jax.ShapeDtypeStruct((2 * both, width), bf16),
            jax.ShapeDtypeStruct((8, width), f32),
        ),
        in_specs=[token] * 6
        + [
            pl.BlockSpec((8, width), fixed),
            token,
            pl.BlockSpec((PHASE, 3 * both), block),
            pl.BlockSpec((None, both, PHASE), lambda g: (g, 0, 0)),
            pl.BlockSpec((None, 8, PHASE), lambda g: (g, 0, 0)),
            pl.BlockSpec((4 * both, width), fixed),
        ],
        out_specs=(
            token,
            token,
            pl.BlockSpec((2 * both, width), fixed),
            pl.BlockSpec((2 * both, width), fixed),
            pl.BlockSpec((8, width), fixed),
        ),
        scratch_shapes=[
            pltpu.VMEM((PHASE, width), bf16),
            pltpu.VMEM((3 * both, PHASE), bf16),
            pltpu.VMEM((4 * both, width), f32),
            pltpu.VMEM((3, 8, width), f32),
        ],
        compiler_params=params(58),
        cost_estimate=cost(20 * TOKENS * both * width + 20 * TOKENS * PHASE * both, 30 << 20),
        name="attn_backward",
    )(lat, part_own, part_got, cot, mix_own, mix_got, mod, conv_low, proj, att_t, lse, wcat)


def tail_kernel(
    midx_ref, lat_ref, po_ref, pr_ref, fo_ref, fr_ref, co_ref, cr_ref, cot_ref, resid_ref, mod_ref, k_ref,
    own_ref, send_ref, kg_ref, sums_ref,
    plain, shifted, grad, grad_shifted, out_low, sums,
):
    width = lat_ref.shape[1]
    zero_edges(plain, shifted, grad, grad_shifted)
    fill_shifted(lat_ref, mod_ref, plain, shifted)
    for g in range(4):

        def grad_body(row, carry):
            rows = pl.ds(pl.multiple_of(g * PHASE + row * HALF, HALF), HALF)
            values = co_ref[rows, :].astype(f32) + cr_ref[rows, :].astype(f32)
            padded = pl.ds(pl.multiple_of(HALF + row * HALF, HALF), HALF)
            grad[g, padded, :] = values
            grad_shifted[g, padded, :] = shift_columns(values, g)
            return carry

        lax.fori_loop(0, HALF, grad_body, 0)
    for first in range(0, width, LANES):
        lanes = slice(first, first + LANES)
        totals = kernel_sums(plain, shifted, grad, lanes)
        for t in range(9):
            kg_ref[t : t + 1, lanes] = jnp.sum(totals[t], 0, keepdims=True)
    for first in range(0, width, LANES):
        lanes = slice(first, first + LANES)
        flipped = spread_kernel(k_ref, lanes, True)
        for g in range(4):

            def back_body(row, carry):
                padded = pl.ds(pl.multiple_of(HALF + row * HALF, HALF), HALF)
                plain[g, padded, lanes] = conv_row(grad, grad_shifted, flipped, g, row, lanes)
                return carry

            lax.fori_loop(0, HALF, back_body, 0)
    sums[...] = jnp.zeros_like(sums)
    gate_one = mod_ref[2:3, :]
    gate_two = mod_ref[5:6, :]
    live = mod_ref[6:7, :]
    gain = 1.0 + mod_ref[1:2, :]

    def fold(values):
        return jnp.sum(values.reshape(ROWS // 8, 8, width), 0)

    for g in range(4):

        def body(j, carry):
            rows = pl.ds(pl.multiple_of(g * PHASE + j * ROWS, ROWS), ROWS)
            latent = lat_ref[rows, :].astype(f32)
            attn = po_ref[rows, :].astype(f32) + pr_ref[rows, :].astype(f32)
            ffn_out = fo_ref[rows, :].astype(f32) + fr_ref[rows, :].astype(f32)
            out = live * (latent + gate_one * attn + gate_two * ffn_out)
            out_low[0, rows, :] = out.astype(bf16)
            sums[2] += fold(ffn_out * cot_ref[rows, :].astype(f32))
            normed, scale = norm_rows(latent)
            back = plain[g, pl.ds(pl.multiple_of(HALF + j * ROWS, HALF), ROWS), :]
            u = back * gain
            mean_u = jnp.mean(u, -1, keepdims=True)
            mean_un = jnp.mean(u * normed, -1, keepdims=True)
            result = resid_ref[rows, :] + scale * (u - mean_u - normed * mean_un)
            out_low[1, rows, :] = result.astype(bf16)
            sums[0] += fold(back)
            sums[1] += fold(back * normed)
            return carry

        lax.fori_loop(0, PHASE // ROWS, body, 0)
    for t in range(3):
        sums_ref[t : t + 1, :] = jnp.sum(sums[t], 0, keepdims=True)
    sums_ref[3:8, :] = jnp.zeros((5, width), f32)
    perm = grid_permutation(True)
    for i, target in ((0, own_ref), (1, send_ref)):
        block = midx_ref[i]
        for which in range(2):
            values = jnp.concatenate(
                [
                    out_low[which, pl.ds(pl.multiple_of(g * PHASE + block * 64, 64), 64), :]
                    for g in range(4)
                ],
                0,
            )
            target[which] = dot_nn(perm, values).astype(bf16)


def tail(midx, lat, part_own, part_got, ffn_own, ffn_got, conv_own, conv_got, cot, resid, mod, kernel):
    width = lat.shape[1]
    share = jax.ShapeDtypeStruct((2, TOKENS // 4, width), bf16)
    padded = pltpu.VMEM((4, PADDED, width), f32)
    return pl.pallas_call(
        tail_kernel,
        out_shape=(
            share,
            share,
            jax.ShapeDtypeStruct((9, width), f32),
            jax.ShapeDtypeStruct((8, width), f32),
        ),
        in_specs=[SMEM] + [VMEM] * 11,
        out_specs=(VMEM,) * 4,
        scratch_shapes=[padded] * 4 + [pltpu.VMEM((2, TOKENS, width), bf16), pltpu.VMEM((3, 8, width), f32)],
        compiler_params=params(58),
        cost_estimate=cost(80 * TOKENS * width, 24 * TOKENS * width),
        name="tail",
    )(midx, lat, part_own, part_got, ffn_own, ffn_got, conv_own, conv_got, cot, resid, mod, kernel)


def ortho_kernel(inverse, left_ref, basis_ref):
    for block in range(left_ref.shape[0] // 8):
        rows = slice(8 * block, 8 * block + 8)
        factor = left_ref[rows, :] * inverse
        place = lax.broadcasted_iota(jnp.int32, (8, 1), 0)
        for k in range(8):
            products = jnp.sum(factor * factor[k : k + 1, :], -1, keepdims=True)
            scale = lax.rsqrt(products[k : k + 1, :] + ORTHO_EPS)
            column = factor[k : k + 1, :] * scale
            weight = jnp.where(place > k, products * scale, 0.0)
            factor = jnp.where(place == k, column, factor - weight * column)
        basis_ref[rows, :] = factor


def ortho(left, count):
    return pl.pallas_call(
        functools.partial(ortho_kernel, 1.0 / count),
        out_shape=jax.ShapeDtypeStruct(left.shape, f32),
        in_specs=[VMEM],
        out_specs=VMEM,
        compiler_params=params(16),
        cost_estimate=cost(left.size * 40, left.size * 8),
        name="ortho",
    )(left)


def momentum_update(weight, moment, gradient, rate):
    new_moment = MOMENTUM * moment + gradient
    return (weight - rate * new_moment, new_moment)


def per_device(
    latents, conditions, cotangent, counts, w_mod, mom_mod, conv_attn, mom_conv_attn,
    w_qkv, mom_qkv, err_qkv, start_qkv, w_out, mom_out, err_out, start_out,
    w_fc1, mom_fc1, err_fc1, start_fc1, conv_ffn, mom_conv_ffn, w_fc2, mom_fc2, err_fc2, start_fc2,
):
    slots, share, width = latents.shape
    local = w_out.shape[0]
    rank = start_out.shape[1]
    mp_count = lax.axis_size("mp")
    dp_count = lax.axis_size("dp")
    mp = lax.axis_index("mp")
    dp = lax.axis_index("dp")
    chip, core = mp // 2, mp % 2

    def swap_chip(values):
        return lax.ppermute(values, "mp", [(i, i ^ 2) for i in range(mp_count)])

    def swap_core(values):
        return lax.ppermute(values, "mp", [(i, i ^ 1) for i in range(mp_count)])

    def swap_dp(values, bit):
        return lax.ppermute(values, "dp", [(i, i ^ bit) for i in range(dp_count)])

    bits = [1 << b for b in range(dp_count.bit_length() - 1)]

    def sum_dp(values):
        for bit in bits:
            values = values + swap_dp(values, bit)
        return values

    slot = jnp.reshape(chip, (1,)).astype(jnp.int32)
    midx = jnp.stack(
        [2 * chip + core, 2 * (1 - chip) + core, 2 * chip + 1 - core, 2 * (1 - chip) + 1 - core]
    ).astype(jnp.int32)

    own_l, own_c, snd_l, snd_c = enter(slot, latents, cotangent)
    got_l = swap_chip(snd_l)
    sib_own_l = swap_core(own_l)
    sib_got_l = swap_core(got_l)
    lat_pieces = (own_l, got_l, sib_own_l, sib_got_l)

    silu_own = jax.nn.silu(conditions.astype(f32)).astype(bf16)
    silu_all = lax.all_to_all(silu_own, "dp", split_axis=1, concat_axis=0, tiled=True)
    silu_all = silu_all.reshape(dp_count, slots, -1)
    silu_slot = lax.dynamic_index_in_dim(silu_all, chip, 1, keepdims=False)
    partial = jnp.dot(silu_slot, w_mod.astype(bf16), preferred_element_type=f32)
    gathered = lax.all_to_all(partial, "dp", split_axis=0, concat_axis=0, tiled=True)
    modulation = jnp.sum(gathered, 0).reshape(6, width)
    live = (counts[0] > chip).astype(f32)
    mod = jnp.concatenate([modulation, jnp.full((2, width), live, f32)], 0)

    def fetch(shard):
        rows = shard.shape[0] // 2
        place = dp % 2
        half = lax.dynamic_slice_in_dim(shard, place * rows, rows, 0)
        near = swap_chip(half)
        far = swap_dp(near, 1)
        return jnp.where(place == 0, jnp.concatenate([near, far], 0), jnp.concatenate([far, near], 0))

    attn_a = pack_attn(w_qkv, w_out)
    attn_b = fetch(attn_a)
    fc1_a, fc2_a = w_fc1.astype(bf16), w_fc2.astype(bf16)
    got_c = swap_chip(snd_c)
    sib_own_c = swap_core(own_c)
    sib_got_c = swap_core(got_c)
    cot_pieces = (own_c, got_c, sib_own_c, sib_got_c)
    both_b = fetch(jnp.concatenate([fc1_a, fc2_a], 0))
    fc1_b, fc2_b = both_b[: fc1_a.shape[0]], both_b[fc1_a.shape[0] :]
    conv_ffn_b = swap_chip(conv_ffn)

    lat, conv_low = first_conv(midx, lat_pieces, mod, conv_attn)
    wcat, proj, att_t, lse, part = attn_forward(conv_low, attn_a, attn_b)
    part_got = swap_core(part)
    mixed, mixed_t, fgl, cot = second_norm(midx, lat, part, part_got, cot_pieces, mod)
    ffn_a, mix_a, grad_fc1, grad_fc2, kgrad_a = ffn(mixed, mixed_t, fgl, fc1_a, fc2_a, conv_ffn, None, f32)
    ffn_part, mix_part, snd_fc1, snd_fc2, kgrad_b = ffn(
        mixed, mixed_t, fgl, fc1_b, fc2_b, conv_ffn_b, (ffn_a, mix_a), bf16
    )
    mix_got = swap_core(mix_part)
    ffn_got = swap_core(ffn_part)
    got_fc2 = swap_chip(snd_fc2)
    got_fc1 = swap_chip(snd_fc1)
    kgrad_got = swap_chip(kgrad_b)
    conv_part, resid_grad, grad_attn, snd_attn, sums_two = attn_backward(
        lat, part, part_got, cot, mix_part, mix_got, mod, conv_low, proj, att_t, lse, wcat
    )
    got_attn = swap_chip(snd_attn)
    conv_got = swap_core(conv_part)
    own_out, snd_out, kgrad_attn, sums_one = tail(
        midx, lat, part, part_got, ffn_part, ffn_got, conv_part, conv_got, cot, resid_grad, mod, conv_attn
    )
    got_out = swap_chip(snd_out)
    outs = jnp.where(chip == 0, jnp.stack([own_out, got_out], 1), jnp.stack([got_out, own_out], 1))

    mod_total = jnp.concatenate([sums_one[0:2], sums_two[0:3], sums_one[2:3]], 0).reshape(1, -1)
    for bit in bits:
        mod_total = jnp.concatenate([mod_total, swap_dp(mod_total, bit)], 0)
    other_total = swap_chip(mod_total)
    count = jnp.arange(dp_count)
    pick = ((dp ^ count)[:, None] == count[None, :]).astype(bf16)
    silu_order = jnp.dot(pick, silu_all.reshape(dp_count, -1)).reshape(silu_all.shape)
    totals = jnp.where(
        chip == 0, jnp.concatenate([mod_total, other_total], 0), jnp.concatenate([other_total, mod_total], 0)
    )
    mod_mean = (
        jnp.dot(
            jnp.concatenate([silu_order[:, s] for s in range(slots)], 0).astype(f32).T,
            totals,
            precision=HIGHEST,
            preferred_element_type=f32,
        )
        / dp_count
    )
    w_mod_new, mom_mod_new = momentum_update(w_mod, mom_mod, mod_mean, LEARN_RATE)

    merged_attn = grad_attn + got_attn.astype(f32)
    merged_qkv = merged_attn[: 3 * local].reshape(3, local, width).transpose(0, 2, 1) + err_qkv[0]
    merged_out = merged_attn[3 * local :] + err_out[0]
    merged_fc1 = grad_fc1 + got_fc1.astype(f32) + err_fc1[0]
    merged_fc2 = grad_fc2 + got_fc2.astype(f32) + err_fc2[0]
    left_qkv = jnp.einsum("tdo,tor->rd", merged_qkv, start_qkv, precision=HIGHEST)
    left_out = jnp.einsum("cd,dr->rc", merged_out, start_out, precision=HIGHEST)
    left_fc1 = jnp.einsum("df,fr->rd", merged_fc1, start_fc1, precision=HIGHEST)
    left_fc2 = jnp.einsum("fd,dr->rf", merged_fc2, start_fc2, precision=HIGHEST)
    left = jnp.concatenate(
        [left_qkv, left_fc1, left_fc2, jnp.pad(left_out, ((0, 0), (0, width - local)))], 0
    )
    left = sum_dp(left)
    basis = ortho(left, dp_count)
    basis_qkv, basis_fc1, basis_fc2 = basis[:rank], basis[rank : 2 * rank], basis[2 * rank : 3 * rank]
    basis_out = basis[3 * rank :, :local]
    right_qkv = jnp.einsum("tdo,rd->tro", merged_qkv, basis_qkv, precision=HIGHEST)
    right_out = jnp.einsum("cd,rc->rd", merged_out, basis_out, precision=HIGHEST)
    right_fc1 = jnp.einsum("df,rd->rf", merged_fc1, basis_fc1, precision=HIGHEST)
    right_fc2 = jnp.einsum("fd,rf->rd", merged_fc2, basis_fc2, precision=HIGHEST)
    kgrad_chip = kgrad_attn + swap_chip(kgrad_attn)
    rights = jnp.concatenate(
        [
            right_out,
            right_fc1,
            right_fc2,
            jnp.pad(right_qkv.transpose(1, 0, 2).reshape(rank, -1), ((0, 0), (0, width - 3 * local))),
            kgrad_chip,
            kgrad_a + kgrad_got,
        ],
        0,
    )
    rights = sum_dp(rights) / dp_count
    right_out, right_fc1, right_fc2 = rights[:rank], rights[rank : 2 * rank], rights[2 * rank : 3 * rank]
    right_qkv = rights[3 * rank : 4 * rank, : 3 * local].reshape(rank, 3, local)
    conv_attn_new, mom_conv_attn_new = momentum_update(
        conv_attn, mom_conv_attn, rights[4 * rank : 4 * rank + 9], LEARN_RATE
    )
    conv_ffn_new, mom_conv_ffn_new = momentum_update(
        conv_ffn, mom_conv_ffn, rights[4 * rank + 9 : 4 * rank + 18], FAST_RATE
    )
    approx_qkv = jnp.einsum("rd,rto->tdo", basis_qkv, right_qkv, precision=HIGHEST)
    approx_out = jnp.einsum("rc,rd->cd", basis_out, right_out, precision=HIGHEST)
    approx_fc1 = jnp.einsum("rd,rf->df", basis_fc1, right_fc1, precision=HIGHEST)
    approx_fc2 = jnp.einsum("rf,rd->fd", basis_fc2, right_fc2, precision=HIGHEST)
    w_qkv_new, mom_qkv_new = momentum_update(w_qkv, mom_qkv, approx_qkv, LEARN_RATE)
    w_out_new, mom_out_new = momentum_update(w_out, mom_out, approx_out, FAST_RATE)
    w_fc1_new, mom_fc1_new = momentum_update(w_fc1, mom_fc1, approx_fc1, LEARN_RATE)
    w_fc2_new, mom_fc2_new = momentum_update(w_fc2, mom_fc2, approx_fc2, LEARN_RATE)
    return (
        outs[0], outs[1], w_mod_new, mom_mod_new, conv_attn_new, mom_conv_attn_new,
        w_qkv_new, mom_qkv_new, (merged_qkv - approx_qkv)[None],
        w_out_new, mom_out_new, (merged_out - approx_out)[None],
        w_fc1_new, mom_fc1_new, (merged_fc1 - approx_fc1)[None],
        conv_ffn_new, mom_conv_ffn_new,
        w_fc2_new, mom_fc2_new, (merged_fc2 - approx_fc2)[None],
    )


def solution(mesh):
    token = P("dp", "mp", None)
    rows = P("mp", None)
    columns = P(None, "mp")
    placed = (
        token, P("dp", None), token, P("dp"), P("dp", None), P("dp", None), P(), P(),
        P(None, None, "mp"), P(None, None, "mp"), P("dp", None, None, "mp"), P(None, "mp", None),
        rows, rows, P("dp", "mp", None), P(),
        columns, columns, P("dp", None, "mp"), rows,
        columns, columns,
        rows, rows, P("dp", "mp", None), P(),
    )
    results = (
        token, token, P("dp", None), P("dp", None), P(), P(),
        P(None, None, "mp"), P(None, None, "mp"), P("dp", None, None, "mp"),
        rows, rows, P("dp", "mp", None),
        columns, columns, P("dp", None, "mp"),
        columns, columns,
        rows, rows, P("dp", "mp", None),
    )
    return jax.shard_map(per_device, mesh=mesh, in_specs=placed, out_specs=results, check_vma=False)
```

```python
import functools

import jax
import jax.numpy as jnp
from jax import lax
from jax.experimental import pallas as pl
from jax.experimental.pallas import tpu as pltpu
from jax.sharding import PartitionSpec as P

HEAD_DIM = 64
SIDE = 32
HALF = SIDE // 2
PHASE = HALF * HALF
TOKENS = SIDE * SIDE
PADDED = PHASE + 2 * HALF
LANES = 256
ROWS = 64
CHEAP = 4
FINAL_MIB = 58
UNROLL = 4

NORM_EPS = 1e-06
ORTHO_EPS = 1e-06
LEARN_RATE = 0.005
FAST_RATE = 0.025
MOMENTUM = 0.9
GELU_C = 0.7978845608
GELU_A = 0.044715

f32 = jnp.float32
bf16 = jnp.bfloat16
VMEM = pl.BlockSpec(memory_space=pltpu.VMEM)
SMEM = pl.BlockSpec(memory_space=pltpu.SMEM)


def params(mib, **more):
    return pltpu.CompilerParams(vmem_limit_bytes=mib << 20, **more)


def cost(flops, nbytes, trans=0):
    return pl.CostEstimate(flops=flops // CHEAP, bytes_accessed=nbytes // CHEAP, transcendentals=trans)


def dot_nn(a, b):
    return lax.dot_general(a, b, (((1,), (0,)), ((), ())), preferred_element_type=f32)


def dot_nt(a, b):
    return lax.dot_general(a, b, (((1,), (1,)), ((), ())), preferred_element_type=f32)


def dot_tn(a, b):
    return lax.dot_general(a, b, (((0,), (0,)), ((), ())), preferred_element_type=f32)


def taps_of(a, b):
    rows = (((1, -1), (0, 0), (1, 0)) if a == 0 else ((0, 0), (1, 0), (0, 1)))
    cols = (((1, True), (0, False), (1, False)) if b == 0 else ((0, False), (1, False), (0, True)))
    return [
        (3 * i + j, 2 * rows[i][0] + cols[j][0], cols[j][1], rows[i][1])
        for i in range(3)
        for j in range(3)
    ]


TAPS = [taps_of(g // 2, g % 2) for g in range(4)]


def shift_columns(values, phase):
    place = lax.broadcasted_iota(jnp.int32, values.shape, 0)
    if phase % 2 == 1:
        return jnp.where(place == 0, 0.0, pltpu.roll(values, 1, 0))
    return jnp.where(place == HALF - 1, 0.0, pltpu.roll(values, HALF - 1, 0))


def zero_edges(*buffers):
    for buffer in buffers:
        lanes = buffer.shape[-1]
        for g in range(4):
            buffer[g, 0:HALF, :] = jnp.zeros((HALF, lanes), f32)
            buffer[g, HALF + PHASE : PADDED, :] = jnp.zeros((HALF, lanes), f32)


def tap_rows(plain, shifted, g, tap, row, lanes):
    _, phase, moved, step = TAPS[g][tap]
    buffer = shifted if moved else plain
    start = pl.multiple_of(HALF + (row + step) * HALF, HALF)
    return buffer[phase, pl.ds(start, HALF), lanes]


def spread_kernel(k_ref, lanes, flip):
    width = lanes.stop - lanes.start
    return [
        jnp.broadcast_to(k_ref[(8 - t if flip else t) : (8 - t if flip else t) + 1, lanes], (8, width))
        for t in range(9)
    ]


def conv_row(plain, shifted, spread, g, row, lanes):
    width = lanes.stop - lanes.start
    total = None
    for t in range(9):
        value = tap_rows(plain, shifted, g, t, row, lanes).reshape(2, 8, width)
        term = spread[t][None] * value
        total = term if total is None else total + term
    return total.reshape(HALF, width)


def kernel_sums(plain, shifted, grads, lanes):
    width = lanes.stop - lanes.start

    def body(row, sums):
        sums = list(sums)
        for g in range(4):
            start = pl.multiple_of(HALF + row * HALF, HALF)
            grad = grads[g, pl.ds(start, HALF), lanes].reshape(2, 8, width)
            for t in range(9):
                value = tap_rows(plain, shifted, g, t, row, lanes).reshape(2, 8, width)
                term = value * grad
                sums[t] = sums[t] + (term[0] + term[1])
        return tuple(sums)

    return lax.fori_loop(0, HALF, body, tuple(jnp.zeros((8, width), f32) for _ in range(9)), unroll=2)


def grid_permutation(inverse):
    size = 8 * SIDE
    token = lax.broadcasted_iota(jnp.int32, (size, size), 0 if inverse else 1)
    place = lax.broadcasted_iota(jnp.int32, (size, size), 1 if inverse else 0)
    r, c = token >> 5, token & 31
    target = ((r & 1) * 2 + (c & 1)) * 64 + (r >> 1) * HALF + (c >> 1)
    return jnp.where(target == place, 1.0, 0.0).astype(bf16)


def enter_kernel(slot_ref, lat_ref, cot_ref, own_l, own_c, snd_l, snd_c):
    perm = grid_permutation(False)
    mine = slot_ref[0]
    other = 1 - mine
    own_l[...] = dot_nn(perm, lat_ref[mine]).astype(bf16)
    snd_l[...] = dot_nn(perm, lat_ref[other]).astype(bf16)
    own_c[...] = dot_nn(perm, cot_ref[mine]).astype(bf16)
    snd_c[...] = dot_nn(perm, cot_ref[other]).astype(bf16)


def enter(slot, latents, cotangent):
    share, width = latents.shape[1:]
    piece = jax.ShapeDtypeStruct((share, width), bf16)
    return pl.pallas_call(
        enter_kernel,
        out_shape=(piece,) * 4,
        in_specs=[SMEM, VMEM, VMEM],
        out_specs=(VMEM,) * 4,
        compiler_params=params(24),
        cost_estimate=cost(4 * 2 * share * share * width, 12 * share * width),
        name="enter",
    )(slot, latents, cotangent)


def place_quarters(place, quarters, store):
    store(2 * place, quarters[0])
    store(2 * place + 1, quarters[1])
    store(2 * (1 - place), quarters[2])
    store(2 * (1 - place) + 1, quarters[3])


def norm_rows(values):
    mean = jnp.mean(values, -1, keepdims=True)
    centred = values - mean
    variance = jnp.mean(centred * centred, -1, keepdims=True)
    scale = lax.rsqrt(variance + NORM_EPS)
    return centred * scale, scale


def place_pieces(midx_ref, pieces, whole):
    for i, piece in enumerate(pieces):
        block = midx_ref[i]
        for g in range(4):
            start = pl.multiple_of(g * PHASE + block * 64, 64)
            whole[pl.ds(start, 64), :] = piece[g * 64 : (g + 1) * 64, :]


def fill_shifted(lat_ref, mod_ref, plain, shifted):
    if mod_ref is not None:
        gain = 1.0 + mod_ref[1:2, :]
        bias = mod_ref[0:1, :]
    for g in range(4):

        def body(j, carry):
            values = lat_ref[pl.ds(pl.multiple_of(g * PHASE + j * ROWS, ROWS), ROWS), :].astype(f32)
            result, _ = norm_rows(values)
            if mod_ref is not None:
                result = result * gain + bias
            start = pl.multiple_of(HALF + j * ROWS, HALF)
            plain[g, pl.ds(start, ROWS), :] = result
            for h in range(ROWS // HALF):
                part = result[h * HALF : (h + 1) * HALF]
                shifted[g, pl.ds(start + h * HALF, HALF), :] = shift_columns(part, g)
            return carry

        lax.fori_loop(0, PHASE // ROWS, body, 0, unroll=UNROLL)


def first_conv_kernel(idx_ref, p0, p1, p2, p3, k_ref, lat_ref, conv_ref, plain, shifted):
    place_pieces(idx_ref, (p0, p1, p2, p3), lat_ref)
    zero_edges(plain, shifted)
    fill_shifted(lat_ref, None, plain, shifted)
    for first in range(0, conv_ref.shape[1], LANES):
        lanes = slice(first, first + LANES)
        spread = spread_kernel(k_ref, lanes, False)

        def body(row, carry):
            for g in range(4):
                start = pl.multiple_of(g * PHASE + row * HALF, HALF)
                conv_ref[pl.ds(start, HALF), lanes] = conv_row(plain, shifted, spread, g, row, lanes)
            return carry

        lax.fori_loop(0, HALF, body, 0, unroll=2)


def first_conv(idx, pieces, kernel):
    width = pieces[0].shape[1]
    return pl.pallas_call(
        first_conv_kernel,
        out_shape=(jax.ShapeDtypeStruct((TOKENS, width), bf16), jax.ShapeDtypeStruct((TOKENS, width), f32)),
        in_specs=[SMEM] + [VMEM] * 5,
        out_specs=(VMEM, VMEM),
        scratch_shapes=[pltpu.VMEM((4, PADDED, width), f32)] * 2,
        compiler_params=params(12),
        cost_estimate=cost(30 * TOKENS * width, 8 * TOKENS * width),
        name="first_conv",
    )(idx, *pieces, kernel)


def modulate(conv_ref, mod_ref, k_ref, low_ref):
    gain = 1.0 + mod_ref[1:2, :]
    bias = mod_ref[0:1, :]
    taps = [k_ref[t : t + 1, :] for t in range(9)]
    width = conv_ref.shape[1]
    for g in range(4):
        a, b = g // 2, g % 2
        inner = [bias * (taps[j] + taps[3 + j] + taps[6 + j]) for j in range(3)]
        edge = [bias * (taps[3 + j] + (taps[6 + j] if a == 0 else taps[j])) for j in range(3)]
        side = 0 if b == 0 else 2
        place = lax.broadcasted_iota(jnp.int32, (HALF, width), 0)
        inside = place != (0 if b == 0 else HALF - 1)

        def body(row, carry):
            outer = row == (0 if a == 0 else HALF - 1)
            sums = [jnp.where(outer, e, i) for e, i in zip(edge, inner)]
            base = sums[1] + sums[2 - side]
            rows = pl.ds(pl.multiple_of(g * PHASE + row * HALF, HALF), HALF)
            value = conv_ref[rows, :] * gain + base + jnp.where(inside, sums[side], 0.0)
            low_ref[rows, :] = value.astype(bf16)
            return carry

        lax.fori_loop(0, HALF, body, 0, unroll=4)


def head_mask(shape, half):
    lane = lax.broadcasted_iota(jnp.int32, shape, 1)
    return (lane < HEAD_DIM) if half == 0 else (lane >= HEAD_DIM)


def attn_forward_kernel(
    idx_ref, conv_ref, mod_ref, k_ref, wa_ref, q0, q1, q2, q3,
    wcat, low_ref, proj_ref, att_t_ref, lse_ref,
):
    local = wa_ref.shape[0] // 3
    both = 2 * local
    for t in range(3):
        wcat[t * both : t * both + local, :] = wa_ref[t * local : (t + 1) * local, :]
    step = local // 4

    def store(index, quarter):
        for j in range(3):
            chunk = 3 * index + j
            start = (chunk >> 2) * both + local + (chunk & 3) * step
            wcat[pl.ds(pl.multiple_of(start, 16), step), :] = quarter[j * step : (j + 1) * step, :]

    place_quarters(idx_ref[5], (q0, q1, q2, q3), store)
    modulate(conv_ref, mod_ref, k_ref, low_ref)

    def body(g, carry):
        rows = pl.ds(pl.multiple_of(g * PHASE, PHASE), PHASE)
        proj_ref[rows, :] = dot_nt(low_ref[rows, :], wcat[...]).astype(bf16)
        for pair in range(both // 128):
            q = proj_ref[rows, pair * 128 : (pair + 1) * 128] * jnp.asarray(HEAD_DIM**-0.5, bf16)
            k = proj_ref[rows, both + pair * 128 : both + (pair + 1) * 128]
            v = proj_ref[rows, 2 * both + pair * 128 : 2 * both + (pair + 1) * 128]
            v_t = v.T
            for half in range(2):
                q_half = jnp.where(head_mask(q.shape, half), q, jnp.zeros_like(q))
                scores = dot_nt(k, q_half)
                top = jnp.max(scores, 0, keepdims=True)
                weights = jnp.exp(scores - top)
                total = jnp.sum(weights, 0, keepdims=True)
                probs = (weights * (1.0 / total)).astype(bf16)
                head = 2 * pair + half
                lse_ref[g, head : head + 1, :] = top + jnp.log(total)
                out_t = dot_nn(v_t[half * HEAD_DIM : (half + 1) * HEAD_DIM, :], probs)
                att_t_ref[g, head * HEAD_DIM : (head + 1) * HEAD_DIM, :] = out_t.astype(bf16)
        return carry

    lax.fori_loop(0, 4, body, 0)


def attn_forward(idx, conv, mod, kernel, wa, quarters):
    rows, width = wa.shape
    both = 2 * rows // 3
    return pl.pallas_call(
        attn_forward_kernel,
        out_shape=(
            jax.ShapeDtypeStruct((2 * rows, width), bf16),
            jax.ShapeDtypeStruct((TOKENS, width), bf16),
            jax.ShapeDtypeStruct((TOKENS, 3 * both), bf16),
            jax.ShapeDtypeStruct((4, both, PHASE), bf16),
            jax.ShapeDtypeStruct((4, 8, PHASE), f32),
        ),
        in_specs=[SMEM] + [VMEM] * 8,
        out_specs=(VMEM,) * 5,
        compiler_params=params(16),
        cost_estimate=cost(8 * TOKENS * both * width + 8 * TOKENS * PHASE * both, 12 << 20),
        name="attn_forward",
    )(idx, conv, mod, kernel, wa, *quarters)


def second_norm_kernel(
    idx_ref, lat_ref, own_ref, sib_ref, oa, ob, sa, sb, c0, c1, c2, c3, mod_ref,
    attn_ref, mixed, mixed_t, fgl, cot, wo, heads,
):
    place_pieces(idx_ref, (c0, c1, c2, c3), cot)
    local = oa.shape[0]
    core = idx_ref[4]
    mine = pl.multiple_of(core * 2 * local, local)
    theirs = pl.multiple_of((1 - core) * 2 * local, local)
    wo[pl.ds(mine, local), :] = oa[...]
    wo[pl.ds(mine + local, local), :] = ob[...]
    wo[pl.ds(theirs, local), :] = sa[...]
    wo[pl.ds(theirs + local, local), :] = sb[...]
    for g in range(4):
        heads[pl.ds(mine, 2 * local), :] = own_ref[g]
        heads[pl.ds(theirs, 2 * local), :] = sib_ref[g]
        attn_ref[g * PHASE : (g + 1) * PHASE, :] = dot_tn(heads[...], wo[...]).astype(bf16)
    gate_one = mod_ref[2:3, :]
    bias = mod_ref[3:4, :]
    gain = 1.0 + mod_ref[4:5, :]
    gate_two = mod_ref[5:6, :]
    live = mod_ref[6:7, :]

    def body(j, carry):
        rows = pl.ds(pl.multiple_of(j * ROWS, ROWS), ROWS)
        resid = lat_ref[rows, :].astype(f32) + gate_one * attn_ref[rows, :].astype(f32)
        normed, _ = norm_rows(resid)
        mixed[rows, :] = (normed * gain + bias).astype(bf16)
        grad = live * cot[rows, :].astype(f32)
        cot[rows, :] = grad.astype(bf16)
        fgl[rows, :] = (gate_two * grad).astype(bf16)
        return carry

    lax.fori_loop(0, TOKENS // ROWS, body, 0, unroll=UNROLL)
    mixed_t[...] = mixed[...].T


def second_norm(idx, lat, own, sib, outs, cots, mod):
    width = lat.shape[1]
    whole = jax.ShapeDtypeStruct((TOKENS, width), bf16)
    return pl.pallas_call(
        second_norm_kernel,
        out_shape=(whole, whole, jax.ShapeDtypeStruct((width, TOKENS), bf16), whole, whole),
        in_specs=[SMEM] + [VMEM] * 12,
        out_specs=(VMEM,) * 5,
        scratch_shapes=[pltpu.VMEM((width, width), bf16), pltpu.VMEM((width, PHASE), bf16)],
        compiler_params=params(16),
        cost_estimate=cost(2 * TOKENS * width * width, 16 * TOKENS * width),
        name="second_norm",
    )(idx, lat, own, sib, *outs, *cots, mod)


def ffn_kernel(first, *refs):
    if first:
        idx_ref, mixed, mixed_t, fgl, near, far_y, far_z, diag_one, diag_two, k_ref = refs[:10]
        ffn_out, mix_out, soon_ref, mid_ref, late_ref, kg_ref = refs[10:16]
        size = diag_one.shape[0]
        w1, w2 = refs[-2:]
        quarter = idx_ref[6]
        for index, one, two in (
            (quarter, near[0:size, :], near[size : 2 * size, :]),
            (quarter ^ 1, far_y[0:size, :], far_y[size : 2 * size, :]),
            (quarter ^ 2, far_z[0:size, :], far_z[size : 2 * size, :]),
            (quarter ^ 3, diag_one[...], diag_two[...]),
        ):
            start = pl.multiple_of(index * size, 64)
            w1[pl.ds(start, size), :] = one
            w2[pl.ds(start, size), :] = two
    else:
        mixed, mixed_t, fgl, w1_ref, w2_ref, k_ref, ffn_in, mix_in = refs[:8]
        ffn_out, mix_out, grads_ref, kg_ref = refs[8:12]
        w1, w2 = refs[-2:]
        w1[...] = w1_ref[...].astype(bf16)
        w2[...] = w2_ref[...].astype(bf16)
    plain, shifted, grad, grad_shifted, act, hidden_grad = refs[-8:-2]
    width = mixed.shape[1]
    kg_ref[9:16, :] = jnp.zeros((7, kg_ref.shape[1]), f32)
    zero_edges(plain, shifted, grad, grad_shifted)
    here = slice(0, LANES)
    for first_lane in range(0, w1.shape[1], LANES):
        lanes = slice(first_lane, first_lane + LANES)
        for g in range(4):
            rows = slice(g * PHASE, (g + 1) * PHASE)
            plain[g, HALF : HALF + PHASE, :] = dot_nn(mixed[rows, :], w1[:, lanes])
            grad[g, HALF : HALF + PHASE, :] = dot_nt(fgl[rows, :], w2[lanes, :])

        def shift_body(row, carry):
            rows = pl.ds(pl.multiple_of(HALF + row * HALF, HALF), HALF)
            for g in range(4):
                shifted[g, rows, :] = shift_columns(plain[g, rows, :], g)
            return carry

        lax.fori_loop(0, HALF, shift_body, 0, unroll=4)
        spread = [
            jnp.broadcast_to(k_ref[t : t + 1, lanes], (8, LANES)) for t in range(9)
        ]

        def act_body(row, carry):
            padded = pl.ds(pl.multiple_of(HALF + row * HALF, HALF), HALF)
            for g in range(4):
                pre = conv_row(plain, shifted, spread, g, row, here)
                square = pre * pre
                tanh = jnp.tanh(pre * (GELU_C + (GELU_C * GELU_A) * square))
                half = 0.5 + 0.5 * tanh
                rows = pl.ds(pl.multiple_of(g * PHASE + row * HALF, HALF), HALF)
                act[rows, lanes] = (pre * half).astype(bf16)
                slope = half + (0.5 * pre) * (1.0 - tanh * tanh) * (
                    GELU_C + (3.0 * GELU_C * GELU_A) * square
                )
                result = grad[g, padded, :] * slope
                grad[g, padded, :] = result
                grad_shifted[g, padded, :] = shift_columns(result, g)
            return carry

        lax.fori_loop(0, HALF, act_body, 0, unroll=2)
        flipped = spread[::-1]

        def back_body(row, carry):
            for g in range(4):
                rows = pl.ds(pl.multiple_of(g * PHASE + row * HALF, HALF), HALF)
                hidden_grad[rows, lanes] = conv_row(grad, grad_shifted, flipped, g, row, here).astype(bf16)
            return carry

        lax.fori_loop(0, HALF, back_body, 0, unroll=2)
        sums = kernel_sums(plain, shifted, grad, here)
        for t in range(9):
            kg_ref[t : t + 1, lanes] = jnp.sum(sums[t], 0, keepdims=True)
        second = dot_tn(act[:, lanes], fgl[...])
        one = dot_nn(mixed_t[...], hidden_grad[:, lanes])
        if first:
            mid_ref[:, lanes] = one.astype(bf16)
            if lanes.stop <= soon_ref.shape[0]:
                soon_ref[lanes, :] = second.astype(bf16)
            else:
                at = lanes.start - soon_ref.shape[0]
                late_ref[at : at + LANES, :] = second.astype(bf16)
        else:
            grads_ref[0:width, lanes] = one
            grads_ref[width + lanes.start : width + lanes.stop, :] = second
    for g in range(4):
        rows = slice(g * PHASE, (g + 1) * PHASE)
        ffn_part = dot_nn(act[rows, :], w2[...])
        mix_part = dot_nt(hidden_grad[rows, :], w1[...])
        if not first:
            ffn_part = ffn_part + ffn_in[rows, :].astype(f32)
            mix_part = mix_part + mix_in[rows, :].astype(f32)
        ffn_out[rows, :] = ffn_part.astype(bf16)
        mix_out[rows, :] = mix_part.astype(bf16)


def ffn(mixed, mixed_t, fgl, kernel, idx=None, pieces=None, weights=None, before=None):
    width = mixed.shape[1]
    units = kernel.shape[1]
    first = before is None
    padded = pltpu.VMEM((4, PADDED, LANES), f32)
    if first:
        operands = [idx, mixed, mixed_t, fgl, *pieces, kernel]
        in_specs = [SMEM] + [VMEM] * 9
        soon = 2 * LANES
        grads = [
            jax.ShapeDtypeStruct((soon, width), bf16),
            jax.ShapeDtypeStruct((width, units), bf16),
            jax.ShapeDtypeStruct((units - soon, width), bf16),
        ]
    else:
        operands = [mixed, mixed_t, fgl, *weights, kernel, *before]
        in_specs = [VMEM] * 8
        grads = [jax.ShapeDtypeStruct((width + units, width), f32)]
    return pl.pallas_call(
        functools.partial(ffn_kernel, first),
        out_shape=(
            jax.ShapeDtypeStruct((TOKENS, width), bf16),
            jax.ShapeDtypeStruct((TOKENS, width), bf16),
            *grads,
            jax.ShapeDtypeStruct((16, units), f32),
        ),
        in_specs=in_specs,
        out_specs=(VMEM,) * (3 + len(grads)),
        scratch_shapes=[padded] * 4
        + [pltpu.VMEM((TOKENS, units), bf16)] * 2
        + [pltpu.VMEM((width, units), bf16), pltpu.VMEM((units, width), bf16)],
        compiler_params=params(20),
        cost_estimate=pl.CostEstimate(flops=1, bytes_accessed=1, transcendentals=0),
        name="ffn_other" if first else "ffn_own",
    )(*operands)


def attn_backward_kernel(
    lat_ref, attn_ref, cot_ref, mo_ref, mr_ref, mod_ref, conv_ref, proj_ref, att_t_ref, lse_ref, wcat, oa, ob,
    part_ref, resid_ref, mine_ref, send_ref, send_out_ref, sums_ref,
    low, proj_t, grads, sums, wo,
):
    both = wcat.shape[0] // 3
    local = both // 2
    width = wcat.shape[1]
    wo[0:local, :] = oa[...]
    wo[local:both, :] = ob[...]
    sums[...] = jnp.zeros_like(sums)
    gate_one = mod_ref[2:3, :]
    gain = 1.0 + mod_ref[4:5, :]

    def fold(values):
        return jnp.sum(values.reshape(ROWS // 8, 8, width), 0)

    def norm_body(j, carry):
        rows = pl.ds(pl.multiple_of(j * ROWS, ROWS), ROWS)
        attn = attn_ref[rows, :].astype(f32)
        resid = lat_ref[rows, :].astype(f32) + gate_one * attn
        normed, scale = norm_rows(resid)
        mixed = mo_ref[rows, :].astype(f32) + mr_ref[rows, :].astype(f32)
        u = mixed * gain
        mean_u = jnp.mean(u, -1, keepdims=True)
        mean_un = jnp.mean(u * normed, -1, keepdims=True)
        grad = cot_ref[rows, :].astype(f32) + scale * (u - mean_u - normed * mean_un)
        resid_ref[rows, :] = grad
        low[rows, :] = (gate_one * grad).astype(bf16)
        sums[0] += fold(attn * grad)
        sums[1] += fold(mixed)
        sums[2] += fold(mixed * normed)
        return carry

    lax.fori_loop(0, TOKENS // ROWS, norm_body, 0, unroll=UNROLL)
    for t in range(3):
        sums_ref[t : t + 1, :] = jnp.sum(sums[t], 0, keepdims=True)
    sums_ref[3:8, :] = jnp.zeros((5, width), f32)
    scale = HEAD_DIM**-0.5

    def body(g, carry):
        rows = pl.ds(pl.multiple_of(g * PHASE, PHASE), PHASE)
        d_att = dot_nt(low[rows, :], wo[...]).astype(bf16)
        d_att_t = dot_nt(wo[...], low[rows, :]).astype(bf16)
        for pair in range(both // 128):
            q = proj_ref[rows, pair * 128 : (pair + 1) * 128] * jnp.asarray(scale, bf16)
            k = proj_ref[rows, both + pair * 128 : both + (pair + 1) * 128]
            v = proj_ref[rows, 2 * both + pair * 128 : 2 * both + (pair + 1) * 128]
            d_out = d_att[:, pair * 128 : (pair + 1) * 128]
            q_t = q.T
            k_t = k.T
            for half in range(2):
                head = 2 * pair + half
                own = slice(half * HEAD_DIM, (half + 1) * HEAD_DIM)
                mask = head_mask(q.shape, half)
                scores = dot_nt(k, jnp.where(mask, q, jnp.zeros_like(q)))
                probs = jnp.exp(scores - lse_ref[g, head : head + 1, :])
                prob_grad = dot_nt(v, jnp.where(mask, d_out, jnp.zeros_like(d_out)))
                mean = jnp.sum(probs * prob_grad, 0, keepdims=True)
                score_grad = (probs * (prob_grad - mean)).astype(bf16)
                low_probs = probs.astype(bf16)
                d_head = d_att_t[head * HEAD_DIM : (head + 1) * HEAD_DIM, :]
                at = head * HEAD_DIM
                proj_t[g, at : at + HEAD_DIM, :] = (dot_nn(k_t[own, :], score_grad) * scale).astype(bf16)
                proj_t[g, both + at : both + at + HEAD_DIM, :] = dot_nt(q_t[own, :], score_grad).astype(bf16)
                proj_t[g, 2 * both + at : 2 * both + at + HEAD_DIM, :] = dot_nt(d_head, low_probs).astype(bf16)
        part_ref[rows, :] = dot_tn(proj_t[g], wcat[...]).astype(bf16)
        return carry

    lax.fori_loop(0, 4, body, 0)

    def total(rows_of, other):
        result = None
        for g in range(4):
            term = dot_nn(rows_of(g), other[g * PHASE : (g + 1) * PHASE, :])
            result = term if result is None else result + term
        return result

    for t in range(4):
        for side in range(2):
            if t < 3:
                first = t * both + side * local
                value = total(lambda g: proj_t[g, first : first + local, :], conv_ref)
            else:
                value = total(lambda g: att_t_ref[g, side * local : (side + 1) * local, :], low)
            if side == 0:
                mine_ref[t * local : (t + 1) * local, :] = value
            elif t < 3:
                send_ref[t * local : (t + 1) * local, :] = value.astype(bf16)
            else:
                send_out_ref[...] = value.astype(bf16)


def attn_backward(lat, attn, cot, mix_own, mix_got, mod, conv_low, proj, att_t, lse, wcat, out_a, out_b):
    both = wcat.shape[0] // 3
    width = lat.shape[1]
    return pl.pallas_call(
        attn_backward_kernel,
        out_shape=(
            jax.ShapeDtypeStruct((TOKENS, width), bf16),
            jax.ShapeDtypeStruct((TOKENS, width), f32),
            jax.ShapeDtypeStruct((2 * both, width), f32),
            jax.ShapeDtypeStruct((3 * both // 2, width), bf16),
            jax.ShapeDtypeStruct((both // 2, width), bf16),
            jax.ShapeDtypeStruct((8, width), f32),
        ),
        in_specs=[VMEM] * 13,
        out_specs=(VMEM,) * 6,
        scratch_shapes=[
            pltpu.VMEM((TOKENS, width), bf16),
            pltpu.VMEM((4, 3 * both, PHASE), bf16),
            pltpu.VMEM((8, 128), f32),
            pltpu.VMEM((3, 8, width), f32),
            pltpu.VMEM((both, width), bf16),
        ],
        compiler_params=params(20),
        cost_estimate=pl.CostEstimate(flops=1, bytes_accessed=1, transcendentals=0),
        name="attn_backward",
    )(lat, attn, cot, mix_own, mix_got, mod, conv_low, proj, att_t, lse, wcat, out_a, out_b)


def tail_kernel(
    midx_ref, lat_ref, attn_ref, fo_ref, fr_ref, co_ref, cr_ref, cot_ref, resid_ref, two_ref, mod_ref, k_ref,
    own_ref, send_ref, kg_ref, rows_ref,
    plain, shifted, grad, grad_shifted, out_low, sums,
):
    width = lat_ref.shape[1]
    zero_edges(plain, shifted, grad, grad_shifted)
    fill_shifted(lat_ref, mod_ref, plain, shifted)
    def grad_body(row, carry):
        padded = pl.ds(pl.multiple_of(HALF + row * HALF, HALF), HALF)
        for g in range(4):
            rows = pl.ds(pl.multiple_of(g * PHASE + row * HALF, HALF), HALF)
            values = co_ref[rows, :].astype(f32) + cr_ref[rows, :].astype(f32)
            grad[g, padded, :] = values
            grad_shifted[g, padded, :] = shift_columns(values, g)
        return carry

    lax.fori_loop(0, HALF, grad_body, 0, unroll=2)
    for first in range(0, width, LANES):
        lanes = slice(first, first + LANES)
        totals = kernel_sums(plain, shifted, grad, lanes)
        for t in range(9):
            kg_ref[t : t + 1, lanes] = jnp.sum(totals[t], 0, keepdims=True)
    for first in range(0, width, LANES):
        lanes = slice(first, first + LANES)
        flipped = spread_kernel(k_ref, lanes, True)

        def back_body(row, carry):
            padded = pl.ds(pl.multiple_of(HALF + row * HALF, HALF), HALF)
            for g in range(4):
                plain[g, padded, lanes] = conv_row(grad, grad_shifted, flipped, g, row, lanes)
            return carry

        lax.fori_loop(0, HALF, back_body, 0, unroll=2)
    sums[...] = jnp.zeros_like(sums)
    gate_one = mod_ref[2:3, :]
    gate_two = mod_ref[5:6, :]
    live = mod_ref[6:7, :]
    gain = 1.0 + mod_ref[1:2, :]

    def fold(values):
        return jnp.sum(values.reshape(ROWS // 8, 8, width), 0)

    for g in range(4):

        def body(j, carry):
            rows = pl.ds(pl.multiple_of(g * PHASE + j * ROWS, ROWS), ROWS)
            latent = lat_ref[rows, :].astype(f32)
            attn = attn_ref[rows, :].astype(f32)
            ffn_out = fo_ref[rows, :].astype(f32) + fr_ref[rows, :].astype(f32)
            out = live * (latent + gate_one * attn + gate_two * ffn_out)
            out_low[0, rows, :] = out.astype(bf16)
            sums[2] += fold(ffn_out * cot_ref[rows, :].astype(f32))
            normed, scale = norm_rows(latent)
            back = plain[g, pl.ds(pl.multiple_of(HALF + j * ROWS, HALF), ROWS), :]
            u = back * gain
            mean_u = jnp.mean(u, -1, keepdims=True)
            mean_un = jnp.mean(u * normed, -1, keepdims=True)
            result = resid_ref[rows, :] + scale * (u - mean_u - normed * mean_un)
            out_low[1, rows, :] = result.astype(bf16)
            sums[0] += fold(back)
            sums[1] += fold(back * normed)
            return carry

        lax.fori_loop(0, PHASE // ROWS, body, 0, unroll=UNROLL)
    for t, row in enumerate((0, 1, 5)):
        rows_ref[row : row + 1, :] = jnp.sum(sums[t], 0, keepdims=True)
    rows_ref[2:5, :] = two_ref[0:3, :]
    rows_ref[6:8, :] = jnp.zeros((2, width), f32)
    kg_ref[9:16, :] = jnp.zeros((7, width), f32)
    perm = grid_permutation(True)
    for i, target in ((0, own_ref), (1, send_ref)):
        block = midx_ref[i]
        for which in range(2):
            values = jnp.concatenate(
                [
                    out_low[which, pl.ds(pl.multiple_of(g * PHASE + block * 64, 64), 64), :]
                    for g in range(4)
                ],
                0,
            )
            target[which] = dot_nn(perm, values).astype(bf16)


def tail(midx, lat, attn, ffn_own, ffn_got, conv_own, conv_got, cot, resid, two, mod, kernel):
    width = lat.shape[1]
    share = jax.ShapeDtypeStruct((2, TOKENS // 4, width), bf16)
    padded = pltpu.VMEM((4, PADDED, width), f32)
    return pl.pallas_call(
        tail_kernel,
        out_shape=(
            share,
            share,
            jax.ShapeDtypeStruct((16, width), f32),
            jax.ShapeDtypeStruct((8, width), f32),
        ),
        in_specs=[SMEM] + [VMEM] * 11,
        out_specs=(VMEM,) * 4,
        scratch_shapes=[padded] * 4 + [pltpu.VMEM((2, TOKENS, width), bf16), pltpu.VMEM((3, 8, width), f32)],
        compiler_params=params(30),
        cost_estimate=pl.CostEstimate(flops=1, bytes_accessed=1, transcendentals=0),
        name="tail",
    )(midx, lat, attn, ffn_own, ffn_got, conv_own, conv_got, cot, resid, two, mod, kernel)


def split_rows(values):
    high = values.astype(bf16).astype(f32)
    return jnp.concatenate([high, values - high], 0).astype(bf16)


def thin(product, rows, matrix):
    both = split_rows(rows)
    if matrix.dtype == bf16:
        result = product(both, matrix)
        return result[0:8] + result[8:16]
    high = matrix.astype(bf16)
    low = (matrix - high.astype(f32)).astype(bf16)
    first, second = product(both, high), product(both, low)
    return (first[0:8] + first[8:16]) + (second[0:8] + second[8:16])


def merge_ffn_kernel(grads_ref, soon_ref, mid_ref, late_ref, err1_ref, err2_ref, start1_ref, start2_ref, merged_ref, left_ref):
    width = err1_ref.shape[0]
    for first in range(0, width, 256):
        rows = slice(first, first + 256)
        one = grads_ref[rows, :] + mid_ref[rows, :].astype(f32) + err1_ref[rows, :]
        merged_ref[rows, :] = one
        left_ref[0:8, rows] = thin(dot_nt, start1_ref[...], one)
        below = slice(width + first, width + first + 256)
        soon = soon_ref.shape[0]
        if first < soon:
            got = soon_ref[rows, :]
        else:
            got = late_ref[first - soon : first - soon + 256, :]
        two = grads_ref[below, :] + got.astype(f32) + err2_ref[rows, :]
        merged_ref[below, :] = two
        left_ref[8:16, rows] = thin(dot_nt, start2_ref[...], two)


def merge_ffn(grads, soon, mid, late, err1, err2, start1, start2):
    width = err1.shape[0]
    return pl.pallas_call(
        merge_ffn_kernel,
        out_shape=(
            jax.ShapeDtypeStruct(grads.shape, f32),
            jax.ShapeDtypeStruct((16, width), f32),
        ),
        in_specs=[VMEM] * 8,
        out_specs=(VMEM,) * 2,
        compiler_params=params(10),
        cost_estimate=cost(grads.size * 64, grads.size * 14),
        name="merge_ffn",
    )(grads, soon, mid, late, err1, err2, start1, start2)


def left_attn_kernel(mine_ref, send_ref, send_out_ref, err_ref, err_out_ref, start_ref, start_b_ref, start_out_ref, merged_ref, left_ref, left_b_ref):
    local = err_out_ref.shape[0]
    width = mine_ref.shape[1]
    left, left_b = None, None
    for t in range(3):
        rows = slice(t * local, (t + 1) * local)
        start, start_b = start_ref[8 * t : 8 * t + 8, :], start_b_ref[8 * t : 8 * t + 8, :]
        total = mine_ref[rows, :] + err_ref[rows, :]
        merged_ref[rows, :] = total
        term = thin(dot_nn, start, total)
        term_b = thin(dot_nn, start_b, send_ref[rows, :])
        left = term if left is None else left + term
        left_b = term_b if left_b is None else left_b + term_b
    rows = slice(3 * local, 4 * local)
    total = mine_ref[rows, :] + err_out_ref[...]
    merged_ref[rows, :] = total
    left_ref[0:8, :] = left
    left_b_ref[0:8, :] = left_b
    left_ref[8:16, :] = jnp.zeros((8, width), f32)
    left_b_ref[8:16, :] = jnp.zeros((8, width), f32)
    left_ref[8:16, 0:local] = thin(dot_nt, start_out_ref[...], total)
    left_b_ref[8:16, 0:local] = thin(dot_nt, start_out_ref[...], send_out_ref[...])


def left_attn(mine, send, send_out, err_qkv, err_out, start, start_b, start_out):
    width = mine.shape[1]
    piece = jax.ShapeDtypeStruct((16, width), f32)
    return pl.pallas_call(
        left_attn_kernel,
        out_shape=(jax.ShapeDtypeStruct(mine.shape, f32), piece, piece),
        in_specs=[VMEM] * 8,
        out_specs=(VMEM,) * 3,
        compiler_params=params(12),
        cost_estimate=cost(mine.size * 64, mine.size * 12),
        name="left_attn",
    )(mine, send, send_out, err_qkv, err_out, start, start_b, start_out)


def orthonormal(factor):
    place = lax.broadcasted_iota(jnp.int32, (8, 1), 0)
    for k in range(8):
        products = jnp.sum(factor * factor[k : k + 1, :], -1, keepdims=True)
        scale = lax.rsqrt(products[k : k + 1, :] + ORTHO_EPS)
        column = factor[k : k + 1, :] * scale
        weight = jnp.where(place > k, products * scale, 0.0)
        factor = jnp.where(place == k, column, factor - weight * column)
    return factor


def right_kernel(inverse, left_ref, part_ref, got_q, got_k, got_v, got_out_ref, ffn_ref, basis_ref, columns_ref, right_ref, merged_ref):
    local = part_ref.shape[0] // 4
    width = part_ref.shape[1]
    basis = [orthonormal(left_ref[8 * m : 8 * m + 8, :] * inverse) for m in range(4)]
    stack = []
    for m in range(4):
        high = basis[m].astype(bf16).astype(f32)
        stack += [high, high, basis[m] - high]
    stack.append(jnp.zeros((32, width), f32))
    columns_ref[...] = jnp.concatenate(stack, 0).T.astype(bf16)
    basis_ref[...] = basis[0]
    for t, got_ref in enumerate((got_q, got_k, got_v)):
        rows = slice(t * local, (t + 1) * local)
        merged_ref[rows, :] = part_ref[rows, :] + got_ref[...].astype(f32)
    total = merged_ref[0 : 3 * local, :]
    total_out = part_ref[3 * local : 4 * local, :] + got_out_ref[...].astype(f32)
    merged_ref[3 * local : 4 * local, :] = total_out
    right_ref[0:8, :] = jnp.zeros((8, width), f32)
    right_ref[0:8, 0 : 3 * local] = thin(dot_nt, basis[0], total)
    right_ref[8:16, :] = thin(dot_nn, basis[1][:, 0:local], total_out)
    right_ref[16:24, :] = thin(dot_nn, basis[2], ffn_ref[0:width, :])
    right_ref[24:32, :] = thin(dot_nn, basis[3], ffn_ref[width : 2 * width, :])


def right_factors(left, part, got, got_out, ffn_merged, count):
    width = part.shape[1]
    return pl.pallas_call(
        functools.partial(right_kernel, 1.0 / count),
        out_shape=(
            jax.ShapeDtypeStruct((8, width), f32),
            jax.ShapeDtypeStruct((width, 128), bf16),
            jax.ShapeDtypeStruct((32, width), f32),
            jax.ShapeDtypeStruct(part.shape, f32),
        ),
        in_specs=[VMEM] * 7,
        out_specs=(VMEM,) * 4,
        compiler_params=params(20),
        cost_estimate=cost(part.size * 200, part.size * 30),
        name="right_factors",
    )(left, part, *got, got_out, ffn_merged)


def final_kernel(
    inverse, right_ref, basis_ref, columns_ref, conv_g, conv_w, conv_m,
    q_g, q_w, q_m, o_g, o_w, o_m, f1_g, f1_w, f1_m, f2_g, f2_w, f2_m,
    q_w_new, q_m_new, q_e_new, o_w_new, o_m_new, o_e_new,
    f1_w_new, f1_m_new, f1_e_new, f2_w_new, f2_m_new, f2_e_new, conv_w_new, conv_m_new,
    factors, q_columns,
):
    step = pl.program_id(0)
    width = o_g.shape[1]

    @pl.when(step == 0)
    def _():
        factors[...] = jnp.zeros_like(factors)
        for m in range(4):
            right = right_ref[8 * m : 8 * m + 8, :] * inverse
            high = right.astype(bf16).astype(f32)
            if m == 0:
                stack = [high, right - high, high, jnp.zeros((104, width), f32)]
                q_columns[...] = jnp.concatenate(stack, 0).T.astype(bf16)
                near = basis_ref[...].astype(bf16).astype(f32)
                part = jnp.concatenate([near, near, basis_ref[...] - near], 0)
            else:
                part = jnp.concatenate([high, right - high, high], 0)
            at = 0 if m == 0 else 24 * m
            factors[m, at : at + 24, :] = part
        moment = MOMENTUM * conv_m[...] + conv_g[0:9, :] * inverse
        conv_m_new[...] = moment
        conv_w_new[...] = conv_w[...] - FAST_RATE * moment

    def update(gradient, weight, moment, columns, matrix, rate, outs):
        size = gradient.shape[0]
        rows = pl.ds(pl.multiple_of(step * size, 16), size)
        approx = dot_nn(columns[rows, :], factors[matrix].astype(bf16))
        fresh = MOMENTUM * moment[...] + approx
        outs[0][...] = weight[...] - rate * fresh
        outs[1][...] = fresh
        outs[2][...] = gradient[...] - approx

    update(q_g, q_w, q_m, q_columns, 0, LEARN_RATE, (q_w_new, q_m_new, q_e_new))
    update(o_g, o_w, o_m, columns_ref, 1, FAST_RATE, (o_w_new, o_m_new, o_e_new))
    update(f1_g, f1_w, f1_m, columns_ref, 2, LEARN_RATE, (f1_w_new, f1_m_new, f1_e_new))
    update(f2_g, f2_w, f2_m, columns_ref, 3, LEARN_RATE, (f2_w_new, f2_m_new, f2_e_new))


def final_update(right, basis, columns, conv, attn_merged, qkv, out, ffn_merged, fc1, fc2, count):
    steps = 6
    width = right.shape[1]
    fixed = lambda i: (0, 0)

    def rows_of(count_of_rows, shift=0):
        return pl.BlockSpec((count_of_rows // steps, width), lambda i: (i + shift, 0))

    q_spec, o_spec, f_spec = (rows_of(a[0].shape[0]) for a in (qkv, out, fc1))
    o_merged = rows_of(out[0].shape[0], qkv[0].shape[0] * steps // out[0].shape[0])
    below = rows_of(fc2[0].shape[0], steps)
    c_spec = pl.BlockSpec(conv[1].shape, fixed)
    shape = lambda like: jax.ShapeDtypeStruct(like.shape, f32)
    whole = lambda a: pl.BlockSpec(a.shape, fixed)
    return pl.pallas_call(
        functools.partial(final_kernel, 1.0 / count),
        grid=(steps,),
        out_shape=(shape(qkv[0]),) * 3
        + (shape(out[0]),) * 3
        + (shape(fc1[0]),) * 3
        + (shape(fc2[0]),) * 3
        + (shape(conv[1]),) * 2,
        in_specs=[whole(right), whole(basis), whole(columns), whole(conv[0]), c_spec, c_spec]
        + [q_spec] * 3
        + [o_merged, o_spec, o_spec]
        + [f_spec] * 3
        + [below, f_spec, f_spec],
        out_specs=(q_spec,) * 3 + (o_spec,) * 3 + (f_spec,) * 6 + (c_spec,) * 2,
        scratch_shapes=[pltpu.VMEM((4, 128, width), f32), pltpu.VMEM((width, 128), bf16)],
        compiler_params=params(FINAL_MIB),
        cost_estimate=cost(6 * width * width * 256, 50 << 20),
        name="final_update",
    )(right, basis, columns, *conv, attn_merged, *qkv, attn_merged, *out, ffn_merged, *fc1, ffn_merged, *fc2)


def mod_kernel(inverse, slot_ref, silu_ref, own_ref, got_ref, w_ref, m_ref, conv_w, conv_m, w_new, m_new, conv_w_new, conv_m_new, rows):
    step = pl.program_id(0)
    count = own_ref.shape[0] - 16

    @pl.when(step == 0)
    def _():
        mine = pl.multiple_of(slot_ref[0] * count, 16)
        rows[pl.ds(mine, count), :] = own_ref[16 : 16 + count, :]
        rows[pl.ds(count - mine, count), :] = got_ref[16 : 16 + count, :]
        gradient = own_ref[0:16, :].astype(f32) + got_ref[0:16, :].astype(f32)
        moment = MOMENTUM * conv_m[...] + gradient[0:9, :] * inverse
        conv_m_new[...] = moment
        conv_w_new[...] = conv_w[...] - LEARN_RATE * moment

    shape = (silu_ref.shape[0], 2 * count)
    row = lax.broadcasted_iota(jnp.int32, shape, 0)
    col = lax.broadcasted_iota(jnp.int32, shape, 1)
    pick = jnp.where(col == 16 * row + step, 1.0, 0.0).astype(bf16)
    silu = dot_tn(silu_ref[...], pick).astype(bf16)
    mean = dot_nn(silu, rows[...]) * inverse
    moment = MOMENTUM * m_ref[...] + mean
    m_new[...] = moment
    w_new[...] = w_ref[...] - LEARN_RATE * moment


def mod_update(slot, silu, own, got, w_mod, mom_mod, conv, mom_conv, count):
    width = own.shape[1]
    depth = w_mod.shape[0]
    fixed = lambda i: (0, 0)
    spec = pl.BlockSpec((depth, width), lambda i: (0, i))
    c_spec = pl.BlockSpec(conv.shape, fixed)
    rows = pl.BlockSpec(own.shape, fixed)
    return pl.pallas_call(
        functools.partial(mod_kernel, 1.0 / count),
        grid=(6,),
        out_shape=(jax.ShapeDtypeStruct(w_mod.shape, f32),) * 2 + (jax.ShapeDtypeStruct(conv.shape, f32),) * 2,
        in_specs=[SMEM, pl.BlockSpec(silu.shape, fixed), rows, rows, spec, spec, c_spec, c_spec],
        out_specs=(spec, spec, c_spec, c_spec),
        scratch_shapes=[pltpu.VMEM((2 * own.shape[0] - 32, width), bf16)],
        compiler_params=params(16),
        cost_estimate=cost(100 * w_mod.size, 16 * w_mod.size),
        name="mod_update",
    )(slot, silu, own, got, w_mod, mom_mod, conv, mom_conv)


def leave_kernel(slot_ref, own_ref, got_ref, out_ref, grad_ref):
    mine = slot_ref[0]
    for i, target in enumerate((out_ref, grad_ref)):
        target[mine] = own_ref[i]
        target[1 - mine] = got_ref[i]


def leave(slot, own, got):
    return pl.pallas_call(
        leave_kernel,
        out_shape=(jax.ShapeDtypeStruct(own.shape, bf16),) * 2,
        in_specs=[SMEM, VMEM, VMEM],
        out_specs=(VMEM, VMEM),
        compiler_params=params(4),
        cost_estimate=cost(0, 8 * own.size),
        name="leave",
    )(slot, own, got)


def per_device(
    latents, conditions, cotangent, counts, w_mod, mom_mod, conv_attn, mom_conv_attn,
    w_qkv, mom_qkv, err_qkv, start_qkv, w_out, mom_out, err_out, start_out,
    w_fc1, mom_fc1, err_fc1, start_fc1, conv_ffn, mom_conv_ffn, w_fc2, mom_fc2, err_fc2, start_fc2,
):
    slots, share, width = latents.shape
    local = w_out.shape[0]
    rank = start_out.shape[1]
    mp_count = lax.axis_size("mp")
    dp_count = lax.axis_size("dp")
    mp = lax.axis_index("mp")
    dp = lax.axis_index("dp")
    chip, core = mp // 2, mp % 2

    def swap_chip(values):
        return lax.ppermute(values, "mp", [(i, i ^ 2) for i in range(mp_count)])

    def swap_core(values):
        return lax.ppermute(values, "mp", [(i, i ^ 1) for i in range(mp_count)])

    def swap_dp(values, bit):
        return lax.ppermute(values, "dp", [(i, i ^ bit) for i in range(dp_count)])

    bits = [1 << b for b in range(dp_count.bit_length() - 1)]

    def sum_dp(values):
        for bit in bits:
            low = lax.optimization_barrier(values.astype(bf16))
            values = low.astype(f32) + swap_dp(low, bit).astype(f32)
        return values

    def after(values, earlier):
        return lax.optimization_barrier((values, earlier))[0]

    place = (dp ^ (dp >> 1)) & 1
    slot = jnp.reshape(chip, (1,)).astype(jnp.int32)
    idx = jnp.stack(
        [
            2 * chip + core, 2 * (1 - chip) + core, 2 * chip + 1 - core, 2 * (1 - chip) + 1 - core,
            core, place, dp & 3, chip,
        ]
    ).astype(jnp.int32)

    w_qkv_t, mom_qkv_t, err_qkv_t = (
        jnp.swapaxes(a, -1, -2).reshape(3 * local, width) for a in (w_qkv, mom_qkv, err_qkv[0])
    )
    qkv_a = w_qkv_t.astype(bf16)
    size = qkv_a.shape[0] // 4
    qkv_half = [lax.dynamic_slice_in_dim(qkv_a, (2 * place + i) * size, size, 0) for i in range(2)]
    qkv_near = [swap_chip(h) for h in qkv_half]

    own_l, own_c, snd_l, snd_c = enter(slot, after(latents, qkv_half), cotangent)
    got_l = swap_chip(snd_l)
    sib_own_l = swap_core(own_l)

    size = w_fc1.shape[0] // 4
    w_fc1_late, w_fc2_late = after((w_fc1, w_fc2), own_l)
    ffn_q = jnp.concatenate(
        [lax.dynamic_slice_in_dim(w, (dp & 3) * size, size, 0).astype(bf16) for w in (w_fc1_late, w_fc2_late)], 0
    )
    ffn_near = swap_chip(ffn_q)

    silu_own = after(jax.nn.silu(conditions.astype(f32)).astype(bf16), ffn_q)
    silu_all = lax.all_to_all(silu_own, "dp", split_axis=1, concat_axis=0, tiled=True)
    silu_all = silu_all.reshape(dp_count, slots, -1)
    silu_slot = after(lax.dynamic_index_in_dim(silu_all, chip, 1, keepdims=False), qkv_near)
    partial = jnp.dot(silu_slot, w_mod.astype(bf16), preferred_element_type=f32)
    gathered = lax.all_to_all(partial, "dp", split_axis=0, concat_axis=0, tiled=True)
    out_a = after(w_out, partial).astype(bf16)
    out_b = swap_chip(out_a)
    got_c = swap_chip(after(snd_c, out_a))
    sib_own_c = swap_core(after(own_c, out_a))

    near = after(qkv_near, partial)
    qkv_b = near + [swap_dp(near[0], 1), swap_dp(near[1], 2)]
    got_l = after(got_l, partial)
    sib_got_l = swap_core(got_l)
    lat, conv_one = first_conv(idx, (own_l, got_l, sib_own_l, sib_got_l), conv_attn)
    modulation = jnp.sum(after(gathered, conv_one), 0).reshape(6, width)
    live = (counts[0] > chip).astype(f32)
    mod = jnp.concatenate([modulation, jnp.full((2, width), live, f32)], 0)
    ffn_near = after(ffn_near, conv_one)
    ffn_y, ffn_z = swap_dp(ffn_near, 1), swap_dp(ffn_near, 2)
    wcat, conv_low, proj, att_t, lse = attn_forward(
        idx, after(conv_one, ffn_near), mod, conv_attn, qkv_a, qkv_b
    )
    att_sib = swap_core(att_t)
    ffn_y, ffn_z = after((ffn_y, ffn_z), att_t)
    ffn_pieces = (ffn_near, ffn_y, ffn_z, swap_dp(ffn_z[:size], 1), swap_dp(ffn_y[size:], 2))
    out_b, got_c = after((out_b, got_c), att_t)
    outs_sib = [swap_core(out_a), swap_core(out_b)]
    sib_got_c = swap_core(got_c)
    starts_qkv = start_qkv.transpose(0, 2, 1).reshape(3 * rank, local)
    small = swap_chip(
        jnp.concatenate(
            [
                after(conv_ffn, out_a),
                jnp.zeros((7, conv_ffn.shape[1]), f32),
                jnp.pad(starts_qkv, ((0, 0), (0, conv_ffn.shape[1] - local))),
            ],
            0,
        )
    )
    conv_ffn_b, starts_qkv_b = small[:9], small[16:, :local]

    attn, mixed, mixed_t, fgl, cot = second_norm(
        idx, lat, att_t, att_sib, [out_a, out_b, *outs_sib], [own_c, got_c, sib_own_c, sib_got_c], mod
    )
    ffn_b, mix_b, snd_soon, snd_mid, snd_late, kgrad_b = ffn(mixed, mixed_t, fgl, conv_ffn_b, idx=idx, pieces=ffn_pieces)
    got_soon = swap_chip(snd_soon)
    ffn_part, mix_part, grad_ffn, kgrad_a = ffn(
        mixed, mixed_t, fgl, conv_ffn, weights=(w_fc1, w_fc2), before=(ffn_b, mix_b)
    )
    mix_part, got_soon = lax.optimization_barrier((mix_part, got_soon))
    mix_got = swap_core(mix_part)
    got_mid = swap_chip(after(snd_mid, got_soon))
    conv_part, resid_grad, grad_attn, snd_attn, snd_attn_out, sums_two = attn_backward(
        lat, attn, cot, mix_part, mix_got, mod, conv_low, proj, att_t, lse, wcat, out_a, out_b
    )
    conv_got = swap_core(conv_part)
    ffn_got = swap_core(after(ffn_part, conv_part))

    grad_attn, got_mid = after((grad_attn, got_mid), conv_part)
    got_late = swap_chip(after(snd_late, got_mid))
    part_attn, left_a, left_b = left_attn(
        grad_attn, snd_attn, snd_attn_out, err_qkv_t, err_out[0], starts_qkv, starts_qkv_b, start_out.T
    )
    left_swap = swap_chip(jnp.concatenate([left_b, kgrad_b], 0))
    got_attn_out = swap_chip(after(snd_attn_out, left_b))
    own_out, snd_out, kgrad_attn, mod_rows = tail(
        idx, lat, attn, ffn_part, ffn_got, conv_part, conv_got, cot, resid_grad, sums_two, mod, conv_attn
    )
    got_late, left_swap, got_attn_out = after((got_late, left_swap, got_attn_out), kgrad_attn)
    snd_parts = [snd_attn[t * local : (t + 1) * local] for t in range(3)]
    got_parts = [swap_chip(after(snd_parts[0], got_attn_out))]
    merged_ffn, left_ffn = merge_ffn(
        grad_ffn, got_soon, got_mid, got_late, err_fc1[0], err_fc2[0], start_fc1.T, start_fc2.T
    )

    sums = jnp.concatenate(
        [left_a + left_swap[:16], left_ffn, kgrad_a + left_swap[16:], kgrad_attn], 0
    ).astype(bf16)
    mod_rows = jnp.concatenate([mod_rows, jnp.zeros_like(mod_rows)], 0).astype(bf16)
    count = sums.shape[0]
    for bit in bits:
        sent = lax.optimization_barrier(jnp.concatenate([sums, mod_rows], 0))
        if bit > 1 and len(got_parts) < 3:
            sent, *got_parts = lax.optimization_barrier((sent, *got_parts))
            got_parts.append(swap_chip(after(snd_parts[len(got_parts)], got_parts[-1])))
        got = swap_dp(sent, bit)
        total = sent[:count].astype(f32) + got[:count].astype(f32)
        sums = total.astype(bf16)
        mod_rows = jnp.concatenate([mod_rows, got[count:]], 0)

    while len(got_parts) < 3:
        got_parts.append(swap_chip(snd_parts[len(got_parts)]))

    basis, columns, rights, merged_attn = right_factors(
        total[:32], part_attn, got_parts, got_attn_out, merged_ffn, dp_count
    )
    right_sum = sum_dp(rights)
    (
        w_qkv_new, mom_qkv_new, err_qkv_new, w_out_new, mom_out_new, err_out_new,
        w_fc1_new, mom_fc1_new, err_fc1_new, w_fc2_new, mom_fc2_new, err_fc2_new,
        conv_ffn_new, mom_conv_ffn_new,
    ) = final_update(
        right_sum, basis, columns, (total[32:48], conv_ffn, mom_conv_ffn), merged_attn, (w_qkv_t, mom_qkv_t),
        (w_out, mom_out), merged_ffn, (w_fc1, mom_fc1), (w_fc2, mom_fc2), dp_count,
    )
    w_qkv_new, mom_qkv_new, err_qkv_new = (
        jnp.swapaxes(a.reshape(3, local, width), -1, -2) for a in (w_qkv_new, mom_qkv_new, err_qkv_new)
    )

    both = jnp.concatenate([sums[48:64], mod_rows], 0)
    other = swap_chip(both)
    got_out = swap_chip(after(snd_out, both))
    latents_out, latents_grad = leave(slot, own_out, got_out)
    count = jnp.arange(dp_count)
    pick = ((dp ^ count)[:, None] == count[None, :]).astype(bf16)
    silu_order = jnp.dot(pick, silu_all.reshape(dp_count, -1)).reshape(silu_all.shape)
    silu_order = silu_order.transpose(1, 0, 2).reshape(dp_count * slots, -1)
    w_mod_new, mom_mod_new, conv_attn_new, mom_conv_attn_new = mod_update(
        slot, silu_order, both, other, w_mod, mom_mod, conv_attn, mom_conv_attn, dp_count
    )
    return (
        latents_out, latents_grad, w_mod_new, mom_mod_new, conv_attn_new, mom_conv_attn_new,
        w_qkv_new, mom_qkv_new, err_qkv_new[None], w_out_new, mom_out_new, err_out_new[None],
        w_fc1_new, mom_fc1_new, err_fc1_new[None], conv_ffn_new, mom_conv_ffn_new,
        w_fc2_new, mom_fc2_new, err_fc2_new[None],
    )


def solution(mesh):
    token = P("dp", "mp", None)
    rows = P("mp", None)
    columns = P(None, "mp")
    placed = (
        token, P("dp", None), token, P("dp"), P("dp", None), P("dp", None), P(), P(),
        P(None, None, "mp"), P(None, None, "mp"), P("dp", None, None, "mp"), P(None, "mp", None),
        rows, rows, P("dp", "mp", None), P(),
        columns, columns, P("dp", None, "mp"), rows,
        columns, columns,
        rows, rows, P("dp", "mp", None), P(),
    )
    results = (
        token, token, P("dp", None), P("dp", None), P(), P(),
        P(None, None, "mp"), P(None, None, "mp"), P("dp", None, None, "mp"),
        rows, rows, P("dp", "mp", None),
        columns, columns, P("dp", None, "mp"),
        columns, columns,
        rows, rows, P("dp", "mp", None),
    )
    return jax.shard_map(per_device, mesh=mesh, in_specs=placed, out_specs=results, check_vma=False)
```

```python
import functools

import jax
import jax.numpy as jnp
from jax import lax
from jax.experimental import pallas as pl
from jax.experimental.pallas import tpu as pltpu
from jax.sharding import PartitionSpec as P

HEAD_DIM = 64
SIDE = 32
HALF = SIDE // 2
PHASE = HALF * HALF
TOKENS = SIDE * SIDE
PADDED = PHASE + 2 * HALF
LANES = 256
ROWS = 64
CHEAP = 4
FINAL_MIB = 58
UNROLL = 4

NORM_EPS = 1e-06
ORTHO_EPS = 1e-06
LEARN_RATE = 0.005
FAST_RATE = 0.025
MOMENTUM = 0.9
GELU_C = 0.7978845608
GELU_A = 0.044715

f32 = jnp.float32
bf16 = jnp.bfloat16
VMEM = pl.BlockSpec(memory_space=pltpu.VMEM)
SMEM = pl.BlockSpec(memory_space=pltpu.SMEM)


def params(mib, **more):
    return pltpu.CompilerParams(vmem_limit_bytes=mib << 20, **more)


def cost(flops, nbytes, trans=0):
    return pl.CostEstimate(flops=flops // CHEAP, bytes_accessed=nbytes // CHEAP, transcendentals=trans)


def dot_nn(a, b):
    return lax.dot_general(a, b, (((1,), (0,)), ((), ())), preferred_element_type=f32)


def dot_nt(a, b):
    return lax.dot_general(a, b, (((1,), (1,)), ((), ())), preferred_element_type=f32)


def dot_tn(a, b):
    return lax.dot_general(a, b, (((0,), (0,)), ((), ())), preferred_element_type=f32)


def taps_of(a, b):
    rows = (((1, -1), (0, 0), (1, 0)) if a == 0 else ((0, 0), (1, 0), (0, 1)))
    cols = (((1, True), (0, False), (1, False)) if b == 0 else ((0, False), (1, False), (0, True)))
    return [
        (3 * i + j, 2 * rows[i][0] + cols[j][0], cols[j][1], rows[i][1])
        for i in range(3)
        for j in range(3)
    ]


TAPS = [taps_of(g // 2, g % 2) for g in range(4)]


def shift_columns(values, phase):
    place = lax.broadcasted_iota(jnp.int32, values.shape, 0)
    if phase % 2 == 1:
        return jnp.where(place == 0, 0.0, pltpu.roll(values, 1, 0))
    return jnp.where(place == HALF - 1, 0.0, pltpu.roll(values, HALF - 1, 0))


def zero_edges(*buffers):
    for buffer in buffers:
        lanes = buffer.shape[-1]
        for g in range(4):
            buffer[g, 0:HALF, :] = jnp.zeros((HALF, lanes), f32)
            buffer[g, HALF + PHASE : PADDED, :] = jnp.zeros((HALF, lanes), f32)


def tap_rows(plain, shifted, g, tap, row, lanes):
    _, phase, moved, step = TAPS[g][tap]
    buffer = shifted if moved else plain
    start = pl.multiple_of(HALF + (row + step) * HALF, HALF)
    return buffer[phase, pl.ds(start, HALF), lanes]


def spread_kernel(k_ref, lanes, flip):
    width = lanes.stop - lanes.start
    return [
        jnp.broadcast_to(k_ref[(8 - t if flip else t) : (8 - t if flip else t) + 1, lanes], (8, width))
        for t in range(9)
    ]


def conv_row(plain, shifted, spread, g, row, lanes):
    width = lanes.stop - lanes.start
    total = None
    for t in range(9):
        value = tap_rows(plain, shifted, g, t, row, lanes).reshape(2, 8, width)
        term = spread[t][None] * value
        total = term if total is None else total + term
    return total.reshape(HALF, width)


def kernel_sums(plain, shifted, grads, lanes):
    width = lanes.stop - lanes.start

    def body(row, sums):
        sums = list(sums)
        for g in range(4):
            start = pl.multiple_of(HALF + row * HALF, HALF)
            grad = grads[g, pl.ds(start, HALF), lanes].reshape(2, 8, width)
            for t in range(9):
                value = tap_rows(plain, shifted, g, t, row, lanes).reshape(2, 8, width)
                term = value * grad
                sums[t] = sums[t] + (term[0] + term[1])
        return tuple(sums)

    return lax.fori_loop(0, HALF, body, tuple(jnp.zeros((8, width), f32) for _ in range(9)), unroll=2)


def grid_permutation(inverse):
    size = 8 * SIDE
    token = lax.broadcasted_iota(jnp.int32, (size, size), 0 if inverse else 1)
    place = lax.broadcasted_iota(jnp.int32, (size, size), 1 if inverse else 0)
    r, c = token >> 5, token & 31
    target = ((r & 1) * 2 + (c & 1)) * 64 + (r >> 1) * HALF + (c >> 1)
    return jnp.where(target == place, 1.0, 0.0).astype(bf16)


ANYWHERE = pl.BlockSpec(memory_space=pl.ANY)
FREE = pl.CostEstimate(flops=1, bytes_accessed=1, transcendentals=0)


def start_copies(pairs, sems, first=0):
    copies = [pltpu.make_async_copy(src, dst, sems.at[first + i]) for i, (src, dst) in enumerate(pairs)]
    for copy in copies:
        copy.start()
    return copies


def wait_all(copies):
    for copy in copies:
        copy.wait()


def token_pieces(idx_ref, whole, got, sib_whole, sib_got, raw, sems, first=0):
    chip = idx_ref[7]
    return start_copies(
        [(whole.at[chip], raw.at[0]), (got, raw.at[1]), (sib_whole.at[chip], raw.at[2]), (sib_got, raw.at[3])],
        sems,
        first,
    )


def place_pieces(idx_ref, raw, target):
    perm = grid_permutation(False)
    for i in range(4):
        piece = dot_nn(perm, raw[i]).astype(bf16)
        for g in range(4):
            start = pl.multiple_of(g * PHASE + idx_ref[i] * 64, 64)
            target[pl.ds(start, 64), :] = piece[g * 64 : (g + 1) * 64, :]


def modulation_kernel(silu_ref, w_ref, out_ref):
    step = pl.program_id(0)
    part = dot_nn(silu_ref[...], w_ref[...].astype(bf16))
    for n in range(part.shape[0]):
        out_ref[n, pl.ds(step, 1), :] = part[n : n + 1, :]

    @pl.when(step == 0)
    def _():
        out_ref[:, 6:8, :] = jnp.zeros((part.shape[0], 2, part.shape[1]), f32)


def modulation_part(silu, w_mod, width):
    count = silu.shape[0]
    return pl.pallas_call(
        modulation_kernel,
        grid=(6,),
        out_shape=jax.ShapeDtypeStruct((count, 8, width), f32),
        in_specs=[
            pl.BlockSpec(silu.shape, lambda i: (0, 0)),
            pl.BlockSpec((w_mod.shape[0], width), lambda i: (0, i)),
        ],
        out_specs=pl.BlockSpec((count, 8, width), lambda i: (0, 0, 0)),
        compiler_params=params(8),
        cost_estimate=FREE,
        name="modulation_part",
    )(silu, w_mod)


def norm_rows(values):
    mean = jnp.mean(values, -1, keepdims=True)
    centred = values - mean
    variance = jnp.mean(centred * centred, -1, keepdims=True)
    scale = lax.rsqrt(variance + NORM_EPS)
    return centred * scale, scale


def fill_shifted(lat_ref, mod_ref, plain, shifted):
    if mod_ref is not None:
        gain = 1.0 + mod_ref[1:2, :]
        bias = mod_ref[0:1, :]
    for g in range(4):

        def body(j, carry):
            values = lat_ref[pl.ds(pl.multiple_of(g * PHASE + j * ROWS, ROWS), ROWS), :].astype(f32)
            result, _ = norm_rows(values)
            if mod_ref is not None:
                result = result * gain + bias
            start = pl.multiple_of(HALF + j * ROWS, HALF)
            plain[g, pl.ds(start, ROWS), :] = result
            for h in range(ROWS // HALF):
                part = result[h * HALF : (h + 1) * HALF]
                shifted[g, pl.ds(start + h * HALF, HALF), :] = shift_columns(part, g)
            return carry

        lax.fori_loop(0, PHASE // ROWS, body, 0, unroll=UNROLL)


def first_conv_kernel(idx_ref, own, got, sib, sib_got, k_ref, lat_ref, conv_ref, plain, shifted, raw, sems):
    copies = token_pieces(idx_ref, own, got, sib, sib_got, raw, sems)
    zero_edges(plain, shifted)
    wait_all(copies)
    place_pieces(idx_ref, raw, lat_ref)
    fill_shifted(lat_ref, None, plain, shifted)
    for first in range(0, conv_ref.shape[1], LANES):
        lanes = slice(first, first + LANES)
        spread = spread_kernel(k_ref, lanes, False)

        def body(row, carry):
            for g in range(4):
                start = pl.multiple_of(g * PHASE + row * HALF, HALF)
                conv_ref[pl.ds(start, HALF), lanes] = conv_row(plain, shifted, spread, g, row, lanes)
            return carry

        lax.fori_loop(0, HALF, body, 0, unroll=2)


def first_conv(idx, pieces, kernel):
    width = kernel.shape[1]
    return pl.pallas_call(
        first_conv_kernel,
        out_shape=(jax.ShapeDtypeStruct((TOKENS, width), bf16), jax.ShapeDtypeStruct((TOKENS, width), f32)),
        in_specs=[SMEM] + [ANYWHERE] * 4 + [VMEM],
        out_specs=(VMEM, VMEM),
        scratch_shapes=[pltpu.VMEM((4, PADDED, width), f32)] * 2
        + [pltpu.VMEM((4, TOKENS // 4, width), bf16), pltpu.SemaphoreType.DMA((4,))],
        compiler_params=params(14),
        cost_estimate=cost(30 * TOKENS * width, 8 * TOKENS * width),
        name="first_conv",
    )(idx, *pieces, kernel)


def modulate(conv_ref, mod_ref, k_ref, low_ref):
    gain = 1.0 + mod_ref[1:2, :]
    bias = mod_ref[0:1, :]
    taps = [k_ref[t : t + 1, :] for t in range(9)]
    width = conv_ref.shape[1]
    for g in range(4):
        a, b = g // 2, g % 2
        inner = [bias * (taps[j] + taps[3 + j] + taps[6 + j]) for j in range(3)]
        edge = [bias * (taps[3 + j] + (taps[6 + j] if a == 0 else taps[j])) for j in range(3)]
        side = 0 if b == 0 else 2
        place = lax.broadcasted_iota(jnp.int32, (HALF, width), 0)
        inside = place != (0 if b == 0 else HALF - 1)

        def body(row, carry):
            outer = row == (0 if a == 0 else HALF - 1)
            sums = [jnp.where(outer, e, i) for e, i in zip(edge, inner)]
            base = sums[1] + sums[2 - side]
            rows = pl.ds(pl.multiple_of(g * PHASE + row * HALF, HALF), HALF)
            value = conv_ref[rows, :] * gain + base + jnp.where(inside, sums[side], 0.0)
            low_ref[rows, :] = value.astype(bf16)
            return carry

        lax.fori_loop(0, HALF, body, 0, unroll=4)


def head_mask(shape, half):
    lane = lax.broadcasted_iota(jnp.int32, shape, 1)
    return (lane < HEAD_DIM) if half == 0 else (lane >= HEAD_DIM)


def attn_forward_kernel(
    idx_ref, conv_ref, mod_ref, k_ref, wa_ref, q0, q1, q2, q3,
    wcat, low_ref, proj_ref, att_t_ref, lse_ref, token_ref, wide, sems,
):
    token_ref[...] = jnp.zeros_like(token_ref)
    local = wa_ref.shape[0] // 3
    both = 2 * local
    step = local // 4
    place = idx_ref[5]
    pairs = []
    for index, quarter in ((2 * place, q0), (2 * place + 1, q1), (2 - 2 * place, q2), (3 - 2 * place, q3)):
        for j in range(3):
            chunk = 3 * index + j
            start = pl.multiple_of((chunk >> 2) * both + local + (chunk & 3) * step, 16)
            pairs.append((quarter.at[pl.ds(j * step, step), :], wcat.at[pl.ds(start, step), :]))
    copies = start_copies([(wa_ref, wide)] + pairs, sems)
    modulate(conv_ref, mod_ref, k_ref, low_ref)
    wait_all(copies)
    for t in range(3):
        wcat[t * both : t * both + local, :] = wide[t * local : (t + 1) * local, :].astype(bf16)

    def body(g, carry):
        rows = pl.ds(g * PHASE, PHASE)
        proj_ref[rows, :] = dot_nt(low_ref[rows, :], wcat[...]).astype(bf16)
        for pair in range(both // 128):
            q = proj_ref[rows, pair * 128 : (pair + 1) * 128] * jnp.asarray(HEAD_DIM**-0.5, bf16)
            k = proj_ref[rows, both + pair * 128 : both + (pair + 1) * 128]
            v = proj_ref[rows, 2 * both + pair * 128 : 2 * both + (pair + 1) * 128]
            v_t = v.T
            halves = range(2)
            scores = [dot_nt(k, jnp.where(head_mask(q.shape, h), q, jnp.zeros_like(q))) for h in halves]
            tops = [jnp.max(x, 0, keepdims=True) for x in scores]
            weights = [jnp.exp(x - top) for x, top in zip(scores, tops)]
            totals = [jnp.sum(x, 0, keepdims=True) for x in weights]
            for half in halves:
                head = 2 * pair + half
                lse_ref[g, head : head + 1, :] = tops[half] + jnp.log(totals[half])
                out_t = dot_nn(v_t[half * HEAD_DIM : (half + 1) * HEAD_DIM, :], weights[half].astype(bf16))
                out_t = out_t * (1.0 / totals[half])
                att_t_ref[g, head * HEAD_DIM : (head + 1) * HEAD_DIM, :] = out_t.astype(bf16)
        return carry

    for g in range(4):
        body(g, 0)


def attn_forward(idx, conv, mod, kernel, wa, quarters):
    rows, width = wa.shape
    both = 2 * rows // 3
    return pl.pallas_call(
        attn_forward_kernel,
        out_shape=(
            jax.ShapeDtypeStruct((2 * rows, width), bf16),
            jax.ShapeDtypeStruct((TOKENS, width), bf16),
            jax.ShapeDtypeStruct((TOKENS, 3 * both), bf16),
            jax.ShapeDtypeStruct((4, both, PHASE), bf16),
            jax.ShapeDtypeStruct((4, 8, PHASE), f32),
            jax.ShapeDtypeStruct((8, 128), f32),
        ),
        in_specs=[SMEM] + [VMEM] * 3 + [ANYWHERE] * 5,
        out_specs=(VMEM,) * 6,
        scratch_shapes=[pltpu.VMEM((rows, width), f32), pltpu.SemaphoreType.DMA((13,))],
        compiler_params=params(16),
        cost_estimate=cost(8 * TOKENS * both * width + 8 * TOKENS * PHASE * both, 12 << 20),
        name="attn_forward",
    )(idx, conv, mod, kernel, wa, *quarters)


def second_norm_kernel(
    idx_ref, lat_ref, own_ref, sib_ref, oa, ob, sa, sb, cot_own, cot_got, cot_sib, cot_sib_got, mod_ref,
    attn_ref, mixed, mixed_t, fgl, cot, wo, heads, raw, sems,
):
    local = oa.shape[0]
    core = idx_ref[4]
    mine = pl.multiple_of(core * 2 * local, local)
    theirs = pl.multiple_of((1 - core) * 2 * local, local)
    weights = start_copies(
        [
            (oa, wo.at[pl.ds(mine, local), :]),
            (ob, wo.at[pl.ds(mine + local, local), :]),
            (sa, wo.at[pl.ds(theirs, local), :]),
            (sb, wo.at[pl.ds(theirs + local, local), :]),
        ]
        + [(sib_ref.at[g], heads.at[g, pl.ds(theirs, 2 * local), :]) for g in range(4)],
        sems,
    )
    tokens = token_pieces(idx_ref, cot_own, cot_got, cot_sib, cot_sib_got, raw, sems, 8)
    for g in range(4):
        heads[g, pl.ds(mine, 2 * local), :] = own_ref[g]
    wait_all(weights)
    for g in range(4):
        attn_ref[g * PHASE : (g + 1) * PHASE, :] = dot_tn(heads[g], wo[...]).astype(bf16)
    wait_all(tokens)
    place_pieces(idx_ref, raw, cot)
    gate_one = mod_ref[2:3, :]
    bias = mod_ref[3:4, :]
    gain = 1.0 + mod_ref[4:5, :]
    gate_two = mod_ref[5:6, :]
    live = idx_ref[8].astype(f32)

    def body(j, carry):
        rows = pl.ds(pl.multiple_of(j * ROWS, ROWS), ROWS)
        resid = lat_ref[rows, :].astype(f32) + gate_one * attn_ref[rows, :].astype(f32)
        normed, _ = norm_rows(resid)
        mixed[rows, :] = (normed * gain + bias).astype(bf16)
        grad = live * cot[rows, :].astype(f32)
        cot[rows, :] = grad.astype(bf16)
        fgl[rows, :] = (gate_two * grad).astype(bf16)
        return carry

    lax.fori_loop(0, TOKENS // ROWS, body, 0, unroll=UNROLL)
    mixed_t[...] = mixed[...].T


def second_norm(idx, lat, own, sib, outs, cots, mod):
    width = lat.shape[1]
    whole = jax.ShapeDtypeStruct((TOKENS, width), bf16)
    return pl.pallas_call(
        second_norm_kernel,
        out_shape=(whole, whole, jax.ShapeDtypeStruct((width, TOKENS), bf16), whole, whole),
        in_specs=[SMEM] + [VMEM] * 2 + [ANYWHERE] * 9 + [VMEM],
        out_specs=(VMEM,) * 5,
        scratch_shapes=[
            pltpu.VMEM((width, width), bf16),
            pltpu.VMEM((4, width, PHASE), bf16),
            pltpu.VMEM((4, TOKENS // 4, width), bf16),
            pltpu.SemaphoreType.DMA((12,)),
        ],
        compiler_params=params(16),
        cost_estimate=cost(2 * TOKENS * width * width, 16 * TOKENS * width),
        name="second_norm",
    )(idx, lat, own, sib, *outs, *cots, mod)


def ffn_tile(at, lanes, mixed, mixed_t, fgl, w1, w2, k_ref, buffers, act, hidden_grad, kg_ref):
    plain, shifted, grad, grad_shifted = buffers
    here = slice(0, LANES)
    there = slice(at, at + LANES)
    for g in range(4):
        rows = slice(g * PHASE, (g + 1) * PHASE)
        plain[g, HALF : HALF + PHASE, :] = dot_nn(mixed[rows, :], w1[:, lanes])
        grad[g, HALF : HALF + PHASE, :] = dot_nt(fgl[rows, :], w2[lanes, :])

    def shift_body(row, carry):
        rows = pl.ds(pl.multiple_of(HALF + row * HALF, HALF), HALF)
        for g in range(4):
            shifted[g, rows, :] = shift_columns(plain[g, rows, :], g)
        return carry

    lax.fori_loop(0, HALF, shift_body, 0, unroll=4)
    spread = [
        jnp.broadcast_to(k_ref[t : t + 1, lanes], (8, LANES)) for t in range(9)
    ]

    def act_body(row, carry):
        padded = pl.ds(pl.multiple_of(HALF + row * HALF, HALF), HALF)
        for g in range(4):
            pre = conv_row(plain, shifted, spread, g, row, here)
            square = pre * pre
            tanh = jnp.tanh(pre * (GELU_C + (GELU_C * GELU_A) * square))
            half = 0.5 + 0.5 * tanh
            rows = pl.ds(pl.multiple_of(g * PHASE + row * HALF, HALF), HALF)
            act[rows, there] = (pre * half).astype(bf16)
            slope = half + (0.5 * pre) * (1.0 - tanh * tanh) * (
                GELU_C + (3.0 * GELU_C * GELU_A) * square
            )
            result = grad[g, padded, :] * slope
            grad[g, padded, :] = result
            grad_shifted[g, padded, :] = shift_columns(result, g)
        return carry

    lax.fori_loop(0, HALF, act_body, 0, unroll=2)
    flipped = spread[::-1]

    def back_body(row, carry):
        for g in range(4):
            rows = pl.ds(pl.multiple_of(g * PHASE + row * HALF, HALF), HALF)
            hidden_grad[rows, there] = conv_row(grad, grad_shifted, flipped, g, row, here).astype(bf16)
        return carry

    lax.fori_loop(0, HALF, back_body, 0, unroll=2)
    sums = kernel_sums(plain, shifted, grad, here)
    for t in range(9):
        kg_ref[t : t + 1, there] = jnp.sum(sums[t], 0, keepdims=True)
    second = dot_tn(act[:, there], fgl[...])
    one = dot_nn(mixed_t[...], hidden_grad[:, there])
    return one, second


def fold_rows(one):
    return jnp.concatenate([one[i : i + LANES, :] for i in range(0, one.shape[0], LANES)], 1)


def ffn_first_kernel(
    idx_ref, mixed, mixed_t, fgl, near, far_y, far_z, diag_one, diag_two, k_ref,
    w1, w2, act, hidden_grad, send_ref, kg_ref, *rest,
):
    buffers, sems = rest[:4], rest[4]
    size = diag_one.shape[0]
    quarter = idx_ref[6]
    pairs = []
    for index, one, two in (
        (quarter, near.at[pl.ds(0, size), :], near.at[pl.ds(size, size), :]),
        (quarter ^ 1, far_y.at[pl.ds(0, size), :], far_y.at[pl.ds(size, size), :]),
        (quarter ^ 2, far_z.at[pl.ds(0, size), :], far_z.at[pl.ds(size, size), :]),
        (quarter ^ 3, diag_one, diag_two),
    ):
        rows = pl.ds(pl.multiple_of(index * size, 64), size)
        pairs += [(one, w1.at[rows, :]), (two, w2.at[rows, :])]
    copies = start_copies(pairs, sems)
    zero_edges(*buffers)
    kg_ref[9:16, :] = jnp.zeros((7, kg_ref.shape[1]), f32)
    wait_all(copies)
    one, second = ffn_tile(
        0, slice(0, LANES), mixed, mixed_t, fgl, w1, w2, k_ref, buffers, act, hidden_grad, kg_ref
    )
    send_ref[0:LANES, :] = second.astype(bf16)
    send_ref[LANES : 2 * LANES, :] = fold_rows(one).astype(bf16)


def ffn_scratch():
    return [pltpu.VMEM((4, PADDED, LANES), f32)] * 4


def ffn_first(idx, mixed, mixed_t, fgl, pieces, kernel):
    width, units = mixed.shape[1], kernel.shape[1]
    tile = jax.ShapeDtypeStruct((TOKENS, LANES), bf16)
    return pl.pallas_call(
        ffn_first_kernel,
        out_shape=(
            jax.ShapeDtypeStruct((width, units), bf16),
            jax.ShapeDtypeStruct((units, width), bf16),
            tile,
            tile,
            jax.ShapeDtypeStruct((2 * LANES, width), bf16),
            jax.ShapeDtypeStruct((16, LANES), f32),
        ),
        in_specs=[SMEM] + [VMEM] * 3 + [ANYWHERE] * 5 + [VMEM],
        out_specs=(VMEM,) * 6,
        scratch_shapes=ffn_scratch() + [pltpu.SemaphoreType.DMA((8,))],
        compiler_params=params(12),
        cost_estimate=FREE,
        name="ffn_first",
    )(idx, mixed, mixed_t, fgl, *pieces, kernel)


def ffn_sums(act, hidden_grad, w1, w2, ffn_out, mix_out, before=None):
    for g in range(4):
        rows = slice(g * PHASE, (g + 1) * PHASE)
        ffn_part = dot_nn(act[rows, :], w2[...])
        mix_part = dot_nt(hidden_grad[rows, :], w1[...])
        if before is not None:
            ffn_part = ffn_part + before[0][rows, :].astype(f32)
            mix_part = mix_part + before[1][rows, :].astype(f32)
        ffn_out[rows, :] = ffn_part.astype(bf16)
        mix_out[rows, :] = mix_part.astype(bf16)


def ffn_second_kernel(
    mixed, mixed_t, fgl, w1, w2, act_in, hidden_in, k_ref,
    ffn_out, mix_out, send_ref, late_ref, kg_ref, *rest,
):
    buffers, act, hidden_grad = rest[:4], rest[4], rest[5]
    zero_edges(*buffers)
    kg_ref[9:16, :] = jnp.zeros((7, kg_ref.shape[1]), f32)
    act[:, 0:LANES] = act_in[...]
    hidden_grad[:, 0:LANES] = hidden_in[...]
    soon = send_ref.shape[0] - LANES
    at = 0
    for first in range(LANES, w1.shape[1], LANES):
        lanes = slice(first, first + LANES)
        one, second = ffn_tile(
            first, lanes, mixed, mixed_t, fgl, w1, w2, k_ref, buffers, act, hidden_grad, kg_ref
        )
        folded = fold_rows(one).astype(bf16)
        if first == LANES:
            send_ref[0:LANES, :] = second.astype(bf16)
            send_ref[LANES : LANES + soon, :] = folded[0:soon, :]
            at = LANES - soon
            late_ref[0:at, :] = folded[soon:LANES, :]
        else:
            late_ref[at : at + LANES, :] = second.astype(bf16)
            late_ref[at + LANES : at + 2 * LANES, :] = folded
            at += 2 * LANES
    ffn_sums(act, hidden_grad, w1, w2, ffn_out, mix_out)


def ffn_second(mixed, mixed_t, fgl, w1, w2, act, hidden_grad, kernel):
    width, units = mixed.shape[1], kernel.shape[1]
    rows = 2 * (units - LANES)
    soon = LANES + LANES // 2
    whole = jax.ShapeDtypeStruct((TOKENS, width), bf16)
    return pl.pallas_call(
        ffn_second_kernel,
        out_shape=(
            whole,
            whole,
            jax.ShapeDtypeStruct((soon, width), bf16),
            jax.ShapeDtypeStruct((rows - soon, width), bf16),
            jax.ShapeDtypeStruct((16, units), f32),
        ),
        in_specs=[VMEM] * 8,
        out_specs=(VMEM,) * 5,
        scratch_shapes=ffn_scratch() + [pltpu.VMEM((TOKENS, units), bf16)] * 2,
        compiler_params=params(16),
        cost_estimate=FREE,
        name="ffn_second",
    )(mixed, mixed_t, fgl, w1, w2, act, hidden_grad, kernel)


def ffn_own_kernel(
    mixed, mixed_t, fgl, w1_ref, w2_ref, k_ref, ffn_in, mix_in, ffn_out, mix_out, grads_ref, kg_ref, *rest,
):
    buffers, act, hidden_grad, w1, w2 = rest[:4], rest[4], rest[5], rest[6], rest[7]
    width = mixed.shape[1]
    w1[...] = w1_ref[...].astype(bf16)
    w2[...] = w2_ref[...].astype(bf16)
    zero_edges(*buffers)
    kg_ref[9:16, :] = jnp.zeros((7, kg_ref.shape[1]), f32)
    for first in range(0, w1.shape[1], LANES):
        lanes = slice(first, first + LANES)
        one, second = ffn_tile(
            first, lanes, mixed, mixed_t, fgl, w1, w2, k_ref, buffers, act, hidden_grad, kg_ref
        )
        grads_ref[0:width, lanes] = one
        grads_ref[width + first : width + first + LANES, :] = second
    ffn_sums(act, hidden_grad, w1, w2, ffn_out, mix_out, (ffn_in, mix_in))


def ffn_own(mixed, mixed_t, fgl, w1, w2, kernel, before):
    width, units = w1.shape
    whole = jax.ShapeDtypeStruct((TOKENS, width), bf16)
    return pl.pallas_call(
        ffn_own_kernel,
        out_shape=(
            whole,
            whole,
            jax.ShapeDtypeStruct((width + units, width), f32),
            jax.ShapeDtypeStruct((16, units), f32),
        ),
        in_specs=[VMEM] * 8,
        out_specs=(VMEM,) * 4,
        scratch_shapes=ffn_scratch()
        + [pltpu.VMEM((TOKENS, units), bf16)] * 2
        + [pltpu.VMEM((width, units), bf16), pltpu.VMEM((units, width), bf16)],
        compiler_params=params(20),
        cost_estimate=FREE,
        name="ffn_own",
    )(mixed, mixed_t, fgl, w1, w2, kernel, *before)


def attn_backward_kernel(
    lat_ref, attn_ref, cot_ref, mo_ref, mr_ref, mod_ref, conv_ref, proj_ref, att_t_ref, lse_ref, wcat, oa, ob,
    part_ref, resid_ref, mine_ref, send_ref, send_v_ref, sums_ref,
    low, proj_t, grads, sums, wo,
):
    both = wcat.shape[0] // 3
    local = both // 2
    width = wcat.shape[1]
    wo[0:local, :] = oa[...]
    wo[local:both, :] = ob[...]
    sums[...] = jnp.zeros_like(sums)
    gate_one = mod_ref[2:3, :]
    gain = 1.0 + mod_ref[4:5, :]

    def fold(values):
        return jnp.sum(values.reshape(ROWS // 8, 8, width), 0)

    def norm_body(j, carry):
        rows = pl.ds(pl.multiple_of(j * ROWS, ROWS), ROWS)
        attn = attn_ref[rows, :].astype(f32)
        resid = lat_ref[rows, :].astype(f32) + gate_one * attn
        normed, scale = norm_rows(resid)
        mixed = mo_ref[rows, :].astype(f32) + mr_ref[rows, :].astype(f32)
        u = mixed * gain
        mean_u = jnp.mean(u, -1, keepdims=True)
        mean_un = jnp.mean(u * normed, -1, keepdims=True)
        grad = cot_ref[rows, :].astype(f32) + scale * (u - mean_u - normed * mean_un)
        resid_ref[rows, :] = grad
        low[rows, :] = (gate_one * grad).astype(bf16)
        sums[0] += fold(attn * grad)
        sums[1] += fold(mixed)
        sums[2] += fold(mixed * normed)
        return carry

    lax.fori_loop(0, TOKENS // ROWS, norm_body, 0, unroll=UNROLL)
    for t in range(3):
        sums_ref[t : t + 1, :] = jnp.sum(sums[t], 0, keepdims=True)
    sums_ref[3:8, :] = jnp.zeros((5, width), f32)
    scale = HEAD_DIM**-0.5

    def body(g, carry):
        rows = pl.ds(g * PHASE, PHASE)
        d_att = dot_nt(low[rows, :], wo[...]).astype(bf16)
        d_att_t = dot_nt(wo[...], low[rows, :]).astype(bf16)
        for pair in range(both // 128):
            q = proj_ref[rows, pair * 128 : (pair + 1) * 128] * jnp.asarray(scale, bf16)
            k = proj_ref[rows, both + pair * 128 : both + (pair + 1) * 128]
            v = proj_ref[rows, 2 * both + pair * 128 : 2 * both + (pair + 1) * 128]
            d_out = d_att[:, pair * 128 : (pair + 1) * 128]
            q_t = q.T
            k_t = k.T
            halves = range(2)
            masks = [head_mask(q.shape, h) for h in halves]
            scores = [dot_nt(k, jnp.where(mask, q, jnp.zeros_like(q))) for mask in masks]
            prob_grads = [dot_nt(v, jnp.where(mask, d_out, jnp.zeros_like(d_out))) for mask in masks]
            probs = [jnp.exp(scores[h] - lse_ref[g, 2 * pair + h : 2 * pair + h + 1, :]) for h in halves]
            means = [jnp.sum(probs[h] * prob_grads[h], 0, keepdims=True) for h in halves]
            score_grads = [(probs[h] * (prob_grads[h] - means[h])).astype(bf16) for h in halves]
            for half in halves:
                own = slice(half * HEAD_DIM, (half + 1) * HEAD_DIM)
                at = (2 * pair + half) * HEAD_DIM
                d_head = d_att_t[at : at + HEAD_DIM, :]
                score_grad, low_probs = score_grads[half], probs[half].astype(bf16)
                proj_t[g, at : at + HEAD_DIM, :] = (dot_nn(k_t[own, :], score_grad) * scale).astype(bf16)
                proj_t[g, both + at : both + at + HEAD_DIM, :] = dot_nt(q_t[own, :], score_grad).astype(bf16)
                proj_t[g, 2 * both + at : 2 * both + at + HEAD_DIM, :] = dot_nt(d_head, low_probs).astype(bf16)
        part_ref[rows, :] = dot_tn(proj_t[g], wcat[...]).astype(bf16)
        return carry

    for g in range(4):
        body(g, 0)

    def total(rows_of, other):
        result = None
        for g in range(4):
            term = dot_nn(rows_of(g), other[g * PHASE : (g + 1) * PHASE, :])
            result = term if result is None else result + term
        return result

    for t in range(4):
        for side in range(2):
            if t < 3:
                first = t * both + side * local
                value = total(lambda g: proj_t[g, first : first + local, :], conv_ref)
            else:
                value = total(lambda g: att_t_ref[g, side * local : (side + 1) * local, :], low)
            if side == 0:
                mine_ref[t * local : (t + 1) * local, :] = value
            elif t == 2:
                send_v_ref[...] = value.astype(bf16)
            else:
                at = ((t + 1) % 4) * local
                send_ref[at : at + local, :] = value.astype(bf16)


def attn_backward(lat, attn, cot, mix_own, mix_got, mod, conv_low, proj, att_t, lse, wcat, out_a, out_b):
    both = wcat.shape[0] // 3
    width = lat.shape[1]
    return pl.pallas_call(
        attn_backward_kernel,
        out_shape=(
            jax.ShapeDtypeStruct((TOKENS, width), bf16),
            jax.ShapeDtypeStruct((TOKENS, width), f32),
            jax.ShapeDtypeStruct((2 * both, width), f32),
            jax.ShapeDtypeStruct((3 * both // 2, width), bf16),
            jax.ShapeDtypeStruct((both // 2, width), bf16),
            jax.ShapeDtypeStruct((8, width), f32),
        ),
        in_specs=[VMEM] * 13,
        out_specs=(VMEM,) * 6,
        scratch_shapes=[
            pltpu.VMEM((TOKENS, width), bf16),
            pltpu.VMEM((4, 3 * both, PHASE), bf16),
            pltpu.VMEM((8, 128), f32),
            pltpu.VMEM((3, 8, width), f32),
            pltpu.VMEM((both, width), bf16),
        ],
        compiler_params=params(20),
        cost_estimate=pl.CostEstimate(flops=1, bytes_accessed=1, transcendentals=0),
        name="attn_backward",
    )(lat, attn, cot, mix_own, mix_got, mod, conv_low, proj, att_t, lse, wcat, out_a, out_b)


def tail_kernel(
    idx_ref, lat_ref, attn_ref, fo_ref, fr_ref, co_ref, cr_ref, cot_ref, resid_ref, two_ref, mod_ref, k_ref,
    own_ref, send_ref, kg_ref, rows_ref,
    plain, shifted, grad, grad_shifted, out_low, sums,
):
    width = lat_ref.shape[1]
    zero_edges(plain, shifted, grad, grad_shifted)
    fill_shifted(lat_ref, mod_ref, plain, shifted)
    def grad_body(row, carry):
        padded = pl.ds(pl.multiple_of(HALF + row * HALF, HALF), HALF)
        for g in range(4):
            rows = pl.ds(pl.multiple_of(g * PHASE + row * HALF, HALF), HALF)
            values = co_ref[rows, :].astype(f32) + cr_ref[rows, :].astype(f32)
            grad[g, padded, :] = values
            grad_shifted[g, padded, :] = shift_columns(values, g)
        return carry

    lax.fori_loop(0, HALF, grad_body, 0, unroll=2)
    for first in range(0, width, LANES):
        lanes = slice(first, first + LANES)
        totals = kernel_sums(plain, shifted, grad, lanes)
        for t in range(9):
            kg_ref[t : t + 1, lanes] = jnp.sum(totals[t], 0, keepdims=True)
    for first in range(0, width, LANES):
        lanes = slice(first, first + LANES)
        flipped = spread_kernel(k_ref, lanes, True)

        def back_body(row, carry):
            padded = pl.ds(pl.multiple_of(HALF + row * HALF, HALF), HALF)
            for g in range(4):
                plain[g, padded, lanes] = conv_row(grad, grad_shifted, flipped, g, row, lanes)
            return carry

        lax.fori_loop(0, HALF, back_body, 0, unroll=2)
    sums[...] = jnp.zeros_like(sums)
    gate_one = mod_ref[2:3, :]
    gate_two = mod_ref[5:6, :]
    live = idx_ref[8].astype(f32)
    gain = 1.0 + mod_ref[1:2, :]

    def fold(values):
        return jnp.sum(values.reshape(ROWS // 8, 8, width), 0)

    for g in range(4):

        def body(j, carry):
            rows = pl.ds(pl.multiple_of(g * PHASE + j * ROWS, ROWS), ROWS)
            latent = lat_ref[rows, :].astype(f32)
            attn = attn_ref[rows, :].astype(f32)
            ffn_out = fo_ref[rows, :].astype(f32) + fr_ref[rows, :].astype(f32)
            out = live * (latent + gate_one * attn + gate_two * ffn_out)
            out_low[0, rows, :] = out.astype(bf16)
            sums[2] += fold(ffn_out * cot_ref[rows, :].astype(f32))
            normed, scale = norm_rows(latent)
            back = plain[g, pl.ds(pl.multiple_of(HALF + j * ROWS, HALF), ROWS), :]
            u = back * gain
            mean_u = jnp.mean(u, -1, keepdims=True)
            mean_un = jnp.mean(u * normed, -1, keepdims=True)
            result = resid_ref[rows, :] + scale * (u - mean_u - normed * mean_un)
            out_low[1, rows, :] = result.astype(bf16)
            sums[0] += fold(back)
            sums[1] += fold(back * normed)
            return carry

        lax.fori_loop(0, PHASE // ROWS, body, 0, unroll=UNROLL)
    for t, row in enumerate((0, 1, 5)):
        rows_ref[row : row + 1, :] = jnp.sum(sums[t], 0, keepdims=True)
    rows_ref[2:5, :] = two_ref[0:3, :]
    rows_ref[6:8, :] = jnp.zeros((2, width), f32)
    kg_ref[9:16, :] = jnp.zeros((7, width), f32)
    perm = grid_permutation(True)
    for i, target in ((0, own_ref), (1, send_ref)):
        block = idx_ref[i]
        for which in range(2):
            values = jnp.concatenate(
                [
                    out_low[which, pl.ds(pl.multiple_of(g * PHASE + block * 64, 64), 64), :]
                    for g in range(4)
                ],
                0,
            )
            target[which] = dot_nn(perm, values).astype(bf16)


def tail(midx, lat, attn, ffn_own, ffn_got, conv_own, conv_got, cot, resid, two, mod, kernel):
    width = lat.shape[1]
    share = jax.ShapeDtypeStruct((2, TOKENS // 4, width), bf16)
    padded = pltpu.VMEM((4, PADDED, width), f32)
    return pl.pallas_call(
        tail_kernel,
        out_shape=(
            share,
            share,
            jax.ShapeDtypeStruct((16, width), f32),
            jax.ShapeDtypeStruct((8, width), f32),
        ),
        in_specs=[SMEM] + [VMEM] * 11,
        out_specs=(VMEM,) * 4,
        scratch_shapes=[padded] * 4 + [pltpu.VMEM((2, TOKENS, width), bf16), pltpu.VMEM((3, 8, width), f32)],
        compiler_params=params(30),
        cost_estimate=pl.CostEstimate(flops=1, bytes_accessed=1, transcendentals=0),
        name="tail",
    )(midx, lat, attn, ffn_own, ffn_got, conv_own, conv_got, cot, resid, two, mod, kernel)


def split_rows(values):
    high = values.astype(bf16).astype(f32)
    return jnp.concatenate([high, values - high], 0).astype(bf16)


def thin(product, rows, matrix):
    both = split_rows(rows)
    if matrix.dtype == bf16:
        result = product(both, matrix)
        return result[0:8] + result[8:16]
    high = matrix.astype(bf16)
    low = (matrix - high.astype(f32)).astype(bf16)
    first, second = product(both, high), product(both, low)
    return (first[0:8] + first[8:16]) + (second[0:8] + second[8:16])


def merge_ffn_kernel(
    grads_ref, piece_ref, soon_ref, late_ref, err1_ref, err2_ref, start1_ref, start2_ref, merged_ref, left_ref
):
    width = err1_ref.shape[0]
    pieces = [piece_ref, soon_ref, late_ref]
    edges = [0, piece_ref.shape[0], piece_ref.shape[0] + soon_ref.shape[0], 2 * width]

    def got(first, count, lanes):
        parts = []
        for ref, low, high in zip(pieces, edges[:-1], edges[1:]):
            begin, end = max(first, low), min(first + count, high)
            if begin < end:
                parts.append(ref[begin - low : end - low, lanes])
        return (parts[0] if len(parts) == 1 else jnp.concatenate(parts, 0)).astype(f32)

    for block, first in enumerate(range(0, width, LANES)):
        rows = slice(first, first + LANES)
        folded = [got(2 * LANES * t + LANES, LANES, rows) for t in range(width // LANES)]
        one = grads_ref[rows, :] + jnp.concatenate(folded, 1) + err1_ref[rows, :]
        merged_ref[rows, :] = one
        left_ref[0:8, rows] = thin(dot_nt, start1_ref[...], one)
        below = slice(width + first, width + first + LANES)
        second = got(2 * LANES * block, LANES, slice(0, width))
        two = grads_ref[below, :] + second + err2_ref[rows, :]
        merged_ref[below, :] = two
        left_ref[8:16, rows] = thin(dot_nt, start2_ref[...], two)


def merge_ffn(grads, pieces, err1, err2, start1, start2):
    width = err1.shape[0]
    return pl.pallas_call(
        merge_ffn_kernel,
        out_shape=(
            jax.ShapeDtypeStruct(grads.shape, f32),
            jax.ShapeDtypeStruct((16, width), f32),
        ),
        in_specs=[VMEM] * 8,
        out_specs=(VMEM,) * 2,
        compiler_params=params(10),
        cost_estimate=FREE,
        name="merge_ffn",
    )(grads, *pieces, err1, err2, start1, start2)


def left_attn_kernel(
    mine_ref, send_ref, send_v_ref, _, kg_one, kg_two, err_ref, err_out_ref, start_ref, start_b_ref, start_out_ref,
    merged_ref, left_ref, bulk_ref,
):
    local = err_out_ref.shape[0]
    width = mine_ref.shape[1]
    left, left_b = None, None
    for t in range(3):
        rows = slice(t * local, (t + 1) * local)
        start, start_b = start_ref[8 * t : 8 * t + 8, :], start_b_ref[8 * t : 8 * t + 8, :]
        total = mine_ref[rows, :] + err_ref[rows, :]
        merged_ref[rows, :] = total
        term = thin(dot_nn, start, total)
        other = send_v_ref[...] if t == 2 else send_ref[(t + 1) * local : (t + 2) * local, :]
        term_b = thin(dot_nn, start_b, other)
        left = term if left is None else left + term
        left_b = term_b if left_b is None else left_b + term_b
    rows = slice(3 * local, 4 * local)
    total = mine_ref[rows, :] + err_out_ref[...]
    merged_ref[rows, :] = total
    left_ref[0:8, :] = left
    left_ref[8:16, :] = jnp.zeros((8, width), f32)
    left_ref[8:16, 0:local] = thin(dot_nt, start_out_ref[...], total)
    left_out = thin(dot_nt, start_out_ref[...], send_ref[0:local, :])
    left_out = jnp.concatenate([left_out, jnp.zeros((8, width - local), f32)], 1)
    size = 3 * local
    tile = kg_one.shape[1]
    bulk_ref[0:size, :] = send_ref[...]
    bulk_ref[size : size + 16, :] = jnp.concatenate([left_b, left_out], 0).astype(bf16)
    bulk_ref[size + 16 : size + 32, 0:tile] = kg_one[...].astype(bf16)
    bulk_ref[size + 16 : size + 32, tile:width] = kg_two[:, tile:width].astype(bf16)


def left_attn(mine, send, send_v, late, kg_one, kg_two, err_qkv, err_out, start, start_b, start_out):
    width = mine.shape[1]
    piece = jax.ShapeDtypeStruct((16, width), f32)
    return pl.pallas_call(
        left_attn_kernel,
        out_shape=(
            jax.ShapeDtypeStruct(mine.shape, f32),
            piece,
            jax.ShapeDtypeStruct((send.shape[0] + 32, width), bf16),
        ),
        in_specs=[VMEM] * 3 + [ANYWHERE] + [VMEM] * 7,
        out_specs=(VMEM,) * 3,
        compiler_params=params(12),
        cost_estimate=cost(mine.size * 64, mine.size * 12),
        name="left_attn",
    )(mine, send, send_v, late, kg_one, kg_two, err_qkv, err_out, start, start_b, start_out)


def orthonormal(factor):
    place = lax.broadcasted_iota(jnp.int32, (8, 1), 0)
    for k in range(8):
        products = jnp.sum(factor * factor[k : k + 1, :], -1, keepdims=True)
        scale = lax.rsqrt(products[k : k + 1, :] + ORTHO_EPS)
        column = factor[k : k + 1, :] * scale
        weight = jnp.where(place > k, products * scale, 0.0)
        factor = jnp.where(place == k, column, factor - weight * column)
    return factor


def right_kernel(inverse, left_ref, part_ref, got_ref, got_v, ffn_ref, basis_ref, columns_ref, right_ref, merged_ref):
    local = part_ref.shape[0] // 4
    width = part_ref.shape[1]
    basis = [orthonormal(left_ref[8 * m : 8 * m + 8, :] * inverse) for m in range(4)]
    stack = []
    for m in range(4):
        high = basis[m].astype(bf16).astype(f32)
        stack += [high, high, basis[m] - high]
    stack.append(jnp.zeros((32, width), f32))
    columns_ref[...] = jnp.concatenate(stack, 0).T.astype(bf16)
    basis_ref[...] = basis[0]
    for t, got in enumerate((got_ref[local : 2 * local, :], got_ref[2 * local : 3 * local, :], got_v[...])):
        rows = slice(t * local, (t + 1) * local)
        merged_ref[rows, :] = part_ref[rows, :] + got.astype(f32)
    total = merged_ref[0 : 3 * local, :]
    total_out = part_ref[3 * local : 4 * local, :] + got_ref[0:local, :].astype(f32)
    merged_ref[3 * local : 4 * local, :] = total_out
    right_ref[0:8, :] = jnp.zeros((8, width), f32)
    right_ref[0:8, 0 : 3 * local] = thin(dot_nt, basis[0], total)
    right_ref[8:16, :] = thin(dot_nn, basis[1][:, 0:local], total_out)
    right_ref[16:24, :] = thin(dot_nn, basis[2], ffn_ref[0:width, :])
    right_ref[24:32, :] = thin(dot_nn, basis[3], ffn_ref[width : 2 * width, :])


def right_factors(left, part, got, ffn_merged, count):
    width = part.shape[1]
    return pl.pallas_call(
        functools.partial(right_kernel, 1.0 / count),
        out_shape=(
            jax.ShapeDtypeStruct((8, width), f32),
            jax.ShapeDtypeStruct((width, 128), bf16),
            jax.ShapeDtypeStruct((32, width), f32),
            jax.ShapeDtypeStruct(part.shape, f32),
        ),
        in_specs=[VMEM] * 5,
        out_specs=(VMEM,) * 4,
        compiler_params=params(20),
        cost_estimate=cost(part.size * 200, part.size * 30),
        name="right_factors",
    )(left, part, *got, ffn_merged)


def final_kernel(
    inverse, _, right_ref, basis_ref, columns_ref, conv_g, conv_w, conv_m, attn_ref, ffn_ref,
    wq, mq, wo, mo, w1, m1, w2, m2,
    q_w, q_m, q_e, o_w, o_m, o_e, f1_w, f1_m, f1_e, f2_w, f2_m, f2_e, conv_w_new, conv_m_new,
    factors, q_columns, staged, loaded, sems, load_sems,
):
    width = attn_ref.shape[1]
    size = staged.shape[2]
    blocks, at = [], 0
    for m, (sources, outs, columns, rate) in enumerate(
        (
            ((wq, mq), (q_w, q_m, q_e), q_columns, LEARN_RATE),
            ((wo, mo), (o_w, o_m, o_e), columns_ref, FAST_RATE),
            ((w1, m1), (f1_w, f1_m, f1_e), columns_ref, LEARN_RATE),
            ((w2, m2), (f2_w, f2_m, f2_e), columns_ref, LEARN_RATE),
        )
    ):
        for first in range(0, outs[0].shape[0], size):
            blocks.append((m, sources, outs, columns, rate, first, at + first))
        at += outs[0].shape[0]

    arriving = []
    for i, (_, sources, _, _, _, first, _) in enumerate(blocks):
        pairs = [(source.at[pl.ds(first, size), :], loaded.at[i, j]) for j, source in enumerate(sources)]
        arriving.append(start_copies(pairs, load_sems, 2 * i))
    factors[...] = jnp.zeros_like(factors)
    for m in range(4):
        right = right_ref[8 * m : 8 * m + 8, :] * inverse
        high = right.astype(bf16).astype(f32)
        if m == 0:
            stack = [high, right - high, high, jnp.zeros((104, width), f32)]
            q_columns[...] = jnp.concatenate(stack, 0).T.astype(bf16)
            near = basis_ref[...].astype(bf16).astype(f32)
            part = jnp.concatenate([near, near, basis_ref[...] - near], 0)
        else:
            part = jnp.concatenate([high, right - high, high], 0)
        at = 24 * m
        factors[m, at : at + 24, :] = part
    moment = MOMENTUM * conv_m[...] + conv_g[0:9, :] * inverse
    conv_m_new[...] = moment
    conv_w_new[...] = conv_w[...] - FAST_RATE * moment

    slots = staged.shape[0]
    flying = [[] for _ in range(slots)]
    for i, (m, sources, outs, columns, rate, first, at) in enumerate(blocks):
        slot = i % slots
        wait_all(arriving[i])
        wait_all(flying[slot])
        rows = slice(at, at + size)
        merged = attn_ref[rows, :] if m < 2 else ffn_ref[at - attn_ref.shape[0] : at - attn_ref.shape[0] + size, :]
        approx = dot_nn(columns[first : first + size, :], factors[m].astype(bf16))
        fresh = MOMENTUM * loaded[i, 1] + approx
        staged[slot, 0] = loaded[i, 0] - rate * fresh
        staged[slot, 1] = fresh
        staged[slot, 2] = merged - approx
        pairs = [(staged.at[slot, j], outs[j].at[pl.ds(first, size), :]) for j in range(3)]
        flying[slot] = start_copies(pairs, sems, 3 * slot)
    for copies in flying:
        wait_all(copies)


def final_update(token, right, basis, columns, conv, attn_merged, ffn_merged, weights, count):
    width = right.shape[1]
    sizes = [w.shape[0] for w in weights[::2]]
    outs = [jax.ShapeDtypeStruct((size, width), f32) for size in sizes for _ in range(3)]
    conv_out = jax.ShapeDtypeStruct(conv[1].shape, f32)
    return pl.pallas_call(
        functools.partial(final_kernel, 1.0 / count),
        out_shape=(*outs, conv_out, conv_out),
        in_specs=[ANYWHERE] + [VMEM] * 8 + [pl.BlockSpec(memory_space=pltpu.HBM)] * 8,
        out_specs=(ANYWHERE,) * len(outs) + (VMEM,) * 2,
        scratch_shapes=[
            pltpu.VMEM((4, 128, width), f32),
            pltpu.VMEM((width, 128), bf16),
            pltpu.VMEM((4, 3, 192, width), f32),
            pltpu.VMEM((sum(sizes) // 192, 2, 192, width), f32),
            pltpu.SemaphoreType.DMA((12,)),
            pltpu.SemaphoreType.DMA((2 * sum(sizes) // 192,)),
        ],
        compiler_params=params(54),
        cost_estimate=cost(6 * width * width * 256, 50 << 20),
        name="final_update",
    )(token, right, basis, columns, *conv, attn_merged, ffn_merged, *weights)


def mod_kernel(
    inverse, slot_ref, silu_ref, own_ref, got_ref, conv_w, conv_m, w_ref, m_ref,
    conv_w_new, conv_m_new, w_new, m_new, rows, weights, moments, load_sems, sems,
):
    width = own_ref.shape[1]
    arriving = []
    for j in range(6):
        lanes = pl.ds(j * width, width)
        pairs = [(w_ref.at[:, lanes], weights.at[:, lanes]), (m_ref.at[:, lanes], moments.at[:, lanes])]
        arriving.append(start_copies(pairs, load_sems, 2 * j))
    count = own_ref.shape[0] - 16
    mine = pl.multiple_of(slot_ref[0] * count, 16)
    rows[pl.ds(mine, count), :] = own_ref[16 : 16 + count, :]
    rows[pl.ds(count - mine, count), :] = got_ref[16 : 16 + count, :]
    gradient = own_ref[0:16, :].astype(f32) + got_ref[0:16, :].astype(f32)
    moment = MOMENTUM * conv_m[...] + gradient[0:9, :] * inverse
    conv_m_new[...] = moment
    conv_w_new[...] = conv_w[...] - LEARN_RATE * moment
    shape = (silu_ref.shape[0], 2 * count)
    row = lax.broadcasted_iota(jnp.int32, shape, 0)
    col = lax.broadcasted_iota(jnp.int32, shape, 1)
    leaving = []
    for j in range(6):
        pick = jnp.where(col == 8 * row + j, 1.0, 0.0).astype(bf16)
        silu = dot_tn(silu_ref[...], pick).astype(bf16)
        mean = dot_nn(silu, rows[...]) * inverse
        wait_all(arriving[j])
        here = slice(j * width, (j + 1) * width)
        moment = MOMENTUM * moments[:, here] + mean
        moments[:, here] = moment
        weights[:, here] = weights[:, here] - LEARN_RATE * moment
        lanes = pl.ds(j * width, width)
        pairs = [(weights.at[:, lanes], w_new.at[:, lanes]), (moments.at[:, lanes], m_new.at[:, lanes])]
        leaving += start_copies(pairs, sems, 2 * j)
    wait_all(leaving)


def mod_update(slot, silu, own, got, w_mod, mom_mod, conv, mom_conv, count):
    width = own.shape[1]
    hbm = pl.BlockSpec(memory_space=pltpu.HBM)
    conv_new, mom_conv_new, w_new, mom_new = pl.pallas_call(
        functools.partial(mod_kernel, 1.0 / count),
        out_shape=(jax.ShapeDtypeStruct(conv.shape, f32),) * 2 + (jax.ShapeDtypeStruct(w_mod.shape, f32),) * 2,
        in_specs=[SMEM] + [VMEM] * 5 + [hbm] * 2,
        out_specs=(VMEM, VMEM, ANYWHERE, ANYWHERE),
        scratch_shapes=[
            pltpu.VMEM((2 * own.shape[0] - 32, width), bf16),
            pltpu.VMEM(w_mod.shape, f32),
            pltpu.VMEM(w_mod.shape, f32),
            pltpu.SemaphoreType.DMA((12,)),
            pltpu.SemaphoreType.DMA((12,)),
        ],
        compiler_params=params(54),
        cost_estimate=cost(100 * w_mod.size, 16 * w_mod.size),
        name="mod_update",
    )(slot, silu, own, got, conv, mom_conv, w_mod, mom_mod)
    return w_new, mom_new, conv_new, mom_conv_new


def leave_kernel(slot_ref, own_ref, got_ref, out_ref, grad_ref):
    mine = slot_ref[0]
    for i, target in enumerate((out_ref, grad_ref)):
        target[mine] = own_ref[i]
        target[1 - mine] = got_ref[i]


def leave(slot, own, got):
    return pl.pallas_call(
        leave_kernel,
        out_shape=(jax.ShapeDtypeStruct(own.shape, bf16),) * 2,
        in_specs=[SMEM, VMEM, VMEM],
        out_specs=(VMEM, VMEM),
        compiler_params=params(4),
        cost_estimate=cost(0, 8 * own.size),
        name="leave",
    )(slot, own, got)


def per_device(
    latents, conditions, cotangent, counts, w_mod, mom_mod, conv_attn, mom_conv_attn,
    w_qkv, mom_qkv, err_qkv, start_qkv, w_out, mom_out, err_out, start_out,
    w_fc1, mom_fc1, err_fc1, start_fc1, conv_ffn, mom_conv_ffn, w_fc2, mom_fc2, err_fc2, start_fc2,
):
    slots, share, width = latents.shape
    local = w_out.shape[0]
    rank = start_out.shape[1]
    mp_count = lax.axis_size("mp")
    dp_count = lax.axis_size("dp")
    mp = lax.axis_index("mp")
    dp = lax.axis_index("dp")
    chip, core = mp // 2, mp % 2

    def swap_chip(values):
        return lax.ppermute(values, "mp", [(i, i ^ 2) for i in range(mp_count)])

    def swap_core(values):
        return lax.ppermute(values, "mp", [(i, i ^ 1) for i in range(mp_count)])

    def swap_dp(values, bit):
        return lax.ppermute(values, "dp", [(i, i ^ bit) for i in range(dp_count)])

    bits = [1 << b for b in range(dp_count.bit_length() - 1)]

    def sum_dp(values, earlier):
        for bit in bits:
            low = lax.optimization_barrier(values.astype(bf16))
            if bit == bits[-1]:
                low = after(low, earlier)
            values = low.astype(f32) + swap_dp(low, bit).astype(f32)
        return values

    def after(values, earlier):
        return lax.optimization_barrier((values, earlier))[0]

    place = (dp ^ (dp >> 1)) & 1
    slot = jnp.reshape(chip, (1,)).astype(jnp.int32)
    idx = jnp.stack(
        [
            2 * chip + core, 2 * (1 - chip) + core, 2 * chip + 1 - core, 2 * (1 - chip) + 1 - core,
            core, place, dp & 3, chip, counts[0] > chip,
        ]
    ).astype(jnp.int32)

    w_qkv_t, mom_qkv_t, err_qkv_t = (
        jnp.swapaxes(a, -1, -2).reshape(3 * local, width) for a in (w_qkv, mom_qkv, err_qkv[0])
    )
    size = w_qkv_t.shape[0] // 4
    near_half = [
        lax.dynamic_slice_in_dim(w_qkv_t, (2 * place + i) * size, size, 0).astype(bf16) for i in range(2)
    ]
    qkv_near = [swap_chip(h) for h in near_half]

    size = w_fc1.shape[0] // 4
    ffn_q = jnp.concatenate(
        [lax.dynamic_slice_in_dim(w, (dp & 3) * size, size, 0).astype(bf16) for w in (w_fc1, w_fc2)], 0
    )
    ffn_near = swap_chip(ffn_q)

    silu_own = after(jax.nn.silu(conditions.astype(f32)).astype(bf16), ffn_q)
    silu_own = silu_own.reshape(slots, dp_count, -1).transpose(1, 0, 2)
    silu_all = lax.all_to_all(silu_own, "dp", split_axis=0, concat_axis=0, tiled=True)
    silu_slot = lax.dynamic_index_in_dim(silu_all, chip, 1, keepdims=False)

    sib_l = swap_core(latents)
    snd_l = lax.dynamic_index_in_dim(after(latents, silu_own), 1 - chip, 0, keepdims=False)
    got_l = swap_chip(snd_l)

    silu_slot = after(silu_slot, (qkv_near, snd_l))
    partial = modulation_part(silu_slot, w_mod, width)
    gathered = lax.all_to_all(partial, "dp", split_axis=0, concat_axis=0, tiled=True)
    out_a = after(w_out, partial).astype(bf16)
    out_b = swap_chip(out_a)
    snd_c = lax.dynamic_index_in_dim(after(cotangent, out_a), 1 - chip, 0, keepdims=False)
    got_c = swap_chip(snd_c)
    sib_c = swap_core(after(cotangent, out_a))

    near = after(qkv_near, partial)
    qkv_b = near + [swap_dp(near[0], 1), swap_dp(near[1], 2)]
    ffn_near = after(ffn_near, partial)
    ffn_y, ffn_z = swap_dp(ffn_near, 1), swap_dp(ffn_near, 2)
    got_l = after(got_l, gathered)
    sib_got_l = swap_core(got_l)
    lat, conv_one = first_conv(idx, (latents, got_l, sib_l, sib_got_l), conv_attn)
    mod = jnp.sum(gathered, 0)
    wcat, conv_low, proj, att_t, lse, token = attn_forward(idx, conv_one, mod, conv_attn, w_qkv_t, qkv_b)
    att_sib = swap_core(att_t)
    ffn_y, ffn_z, out_b, got_c = after((ffn_y, ffn_z, out_b, got_c), token)
    ffn_pieces = (ffn_near, ffn_y, ffn_z, swap_dp(ffn_z[:size], 1), swap_dp(ffn_y[size:], 2))
    outs_sib = [swap_core(out_a), swap_core(out_b)]
    sib_got_c = swap_core(got_c)
    starts_qkv = start_qkv.transpose(0, 2, 1).reshape(3 * rank, local)
    small = swap_chip(
        jnp.concatenate(
            [
                after(conv_ffn, snd_c),
                jnp.zeros((7, conv_ffn.shape[1]), f32),
                jnp.pad(starts_qkv, ((0, 0), (0, conv_ffn.shape[1] - local))),
            ],
            0,
        )
    )
    conv_ffn_b, starts_qkv_b = small[:9], small[16:, :local]

    attn, mixed, mixed_t, fgl, cot = second_norm(
        idx, lat, att_t, att_sib, [out_a, out_b, *outs_sib], [cotangent, got_c, sib_c, sib_got_c], mod
    )
    w1_b, w2_b, act_b, hidden_b, snd_ffn, kgrad_b = ffn_first(idx, mixed, mixed_t, fgl, ffn_pieces, conv_ffn_b)
    got_ffn = swap_chip(snd_ffn)
    ffn_b, mix_b, snd_soon, snd_late, kgrad_c = ffn_second(
        mixed, mixed_t, fgl, w1_b, w2_b, act_b, hidden_b, conv_ffn_b
    )
    got_soon = swap_chip(snd_soon)
    ffn_part, mix_part, grad_ffn, kgrad_a = ffn_own(mixed, mixed_t, fgl, w_fc1, w_fc2, conv_ffn, (ffn_b, mix_b))
    mix_part, got_ffn, got_soon = lax.optimization_barrier((mix_part, got_ffn, got_soon))
    mix_got = swap_core(mix_part)
    got_late = swap_chip(after(snd_late, got_soon))
    conv_part, resid_grad, grad_attn, snd_attn, snd_v, sums_two = attn_backward(
        lat, attn, cot, mix_part, mix_got, mod, conv_low, proj, att_t, lse, wcat, out_a, out_b
    )
    conv_got = swap_core(conv_part)
    ffn_got = swap_core(after(ffn_part, sums_two))

    part_attn, left_a, bulk = left_attn(
        grad_attn, snd_attn, snd_v, got_late, kgrad_b, kgrad_c, err_qkv_t, err_out[0], starts_qkv, starts_qkv_b,
        start_out.T,
    )
    got_bulk = swap_chip(bulk)
    own_out, snd_out, kgrad_attn, mod_rows = tail(
        idx, lat, attn, ffn_part, ffn_got, conv_part, conv_got, cot, resid_grad, sums_two, mod, conv_attn
    )
    got_bulk = after(got_bulk, kgrad_attn)
    got_v = swap_chip(after(snd_v, got_bulk))
    left_swap = got_bulk[3 * local :].astype(f32)
    merged_ffn, left_ffn = merge_ffn(
        grad_ffn, (got_ffn, got_soon, got_late), err_fc1[0], err_fc2[0], start_fc1.T, start_fc2.T
    )

    sums = jnp.concatenate(
        [left_a + left_swap[:16], left_ffn, kgrad_a + left_swap[16:], kgrad_attn], 0
    ).astype(bf16)
    mod_rows = mod_rows.astype(bf16)
    count = sums.shape[0]
    for bit in bits:
        sent = lax.optimization_barrier(jnp.concatenate([sums, mod_rows], 0))
        if bit == 2:
            sent, got_v = lax.optimization_barrier((sent, got_v))
        got = swap_dp(sent, bit)
        total = sent[:count].astype(f32) + got[:count].astype(f32)
        sums = total.astype(bf16)
        mod_rows = jnp.concatenate([mod_rows, got[count:]], 0)

    basis, columns, rights, merged_attn = right_factors(
        total[:32], part_attn, (got_bulk, got_v), merged_ffn, dp_count
    )
    both = jnp.concatenate(after([sums[48:64], mod_rows], rights), 0)
    other = swap_chip(both)
    got_out = swap_chip(after(snd_out, other))
    count = jnp.arange(dp_count)
    pick = ((dp ^ count)[:, None] == count[None, :]).astype(bf16)
    silu_order = jnp.dot(pick, silu_all.reshape(dp_count, -1)).reshape(silu_all.shape)
    silu_order = silu_order.transpose(1, 0, 2).reshape(dp_count * slots, -1)
    w_mod_new, mom_mod_new, conv_attn_new, mom_conv_attn_new = mod_update(
        slot, silu_order, both, other, w_mod, mom_mod, conv_attn, mom_conv_attn, dp_count
    )
    right_sum = sum_dp(rights, conv_attn_new)
    (
        w_qkv_new, mom_qkv_new, err_qkv_new, w_out_new, mom_out_new, err_out_new,
        w_fc1_new, mom_fc1_new, err_fc1_new, w_fc2_new, mom_fc2_new, err_fc2_new,
        conv_ffn_new, mom_conv_ffn_new,
    ) = final_update(
        conv_attn_new, right_sum, basis, columns, (total[32:48], conv_ffn, mom_conv_ffn), merged_attn,
        merged_ffn, (w_qkv_t, mom_qkv_t, w_out, mom_out, w_fc1, mom_fc1, w_fc2, mom_fc2), dp_count,
    )
    w_qkv_new, mom_qkv_new, err_qkv_new = (
        jnp.swapaxes(a.reshape(3, local, width), -1, -2) for a in (w_qkv_new, mom_qkv_new, err_qkv_new)
    )

    latents_out, latents_grad = leave(slot, own_out, got_out)
    return (
        latents_out, latents_grad, w_mod_new, mom_mod_new, conv_attn_new, mom_conv_attn_new,
        w_qkv_new, mom_qkv_new, err_qkv_new[None], w_out_new, mom_out_new, err_out_new[None],
        w_fc1_new, mom_fc1_new, err_fc1_new[None], conv_ffn_new, mom_conv_ffn_new,
        w_fc2_new, mom_fc2_new, err_fc2_new[None],
    )


def solution(mesh):
    token = P("dp", "mp", None)
    rows = P("mp", None)
    columns = P(None, "mp")
    placed = (
        token, P("dp", None), token, P("dp"), P("dp", None), P("dp", None), P(), P(),
        P(None, None, "mp"), P(None, None, "mp"), P("dp", None, None, "mp"), P(None, "mp", None),
        rows, rows, P("dp", "mp", None), P(),
        columns, columns, P("dp", None, "mp"), rows,
        columns, columns,
        rows, rows, P("dp", "mp", None), P(),
    )
    results = (
        token, token, P("dp", None), P("dp", None), P(), P(),
        P(None, None, "mp"), P(None, None, "mp"), P("dp", None, None, "mp"),
        rows, rows, P("dp", "mp", None),
        columns, columns, P("dp", None, "mp"),
        columns, columns,
        rows, rows, P("dp", "mp", None),
    )
    return jax.shard_map(per_device, mesh=mesh, in_specs=placed, out_specs=results, check_vma=False)
```

```python
import functools

import jax
import jax.numpy as jnp
from jax import lax
from jax.experimental import pallas as pl
from jax.experimental.pallas import tpu as pltpu
from jax.sharding import PartitionSpec as P

HEAD_DIM = 64
SIDE = 32
HALF = SIDE // 2
PHASE = HALF * HALF
TOKENS = SIDE * SIDE
PADDED = PHASE + 2 * HALF
LANES = 256
ROWS = 64
CHEAP = 4
FINAL_MIB = 58
UNROLL = 4

NORM_EPS = 1e-06
ORTHO_EPS = 1e-06
LEARN_RATE = 0.005
FAST_RATE = 0.025
MOMENTUM = 0.9
GELU_C = 0.7978845608
GELU_A = 0.044715

f32 = jnp.float32
bf16 = jnp.bfloat16
VMEM = pl.BlockSpec(memory_space=pltpu.VMEM)
SMEM = pl.BlockSpec(memory_space=pltpu.SMEM)


def params(mib, **more):
    return pltpu.CompilerParams(vmem_limit_bytes=mib << 20, **more)


def cost(flops, nbytes, trans=0):
    return pl.CostEstimate(flops=flops // CHEAP, bytes_accessed=nbytes // CHEAP, transcendentals=trans)


def dot_nn(a, b):
    return lax.dot_general(a, b, (((1,), (0,)), ((), ())), preferred_element_type=f32)


def dot_nt(a, b):
    return lax.dot_general(a, b, (((1,), (1,)), ((), ())), preferred_element_type=f32)


def dot_tn(a, b):
    return lax.dot_general(a, b, (((0,), (0,)), ((), ())), preferred_element_type=f32)


def taps_of(a, b):
    rows = (((1, -1), (0, 0), (1, 0)) if a == 0 else ((0, 0), (1, 0), (0, 1)))
    cols = (((1, True), (0, False), (1, False)) if b == 0 else ((0, False), (1, False), (0, True)))
    return [
        (3 * i + j, 2 * rows[i][0] + cols[j][0], cols[j][1], rows[i][1])
        for i in range(3)
        for j in range(3)
    ]


TAPS = [taps_of(g // 2, g % 2) for g in range(4)]


def shift_columns(values, phase):
    place = lax.broadcasted_iota(jnp.int32, values.shape, 0)
    if phase % 2 == 1:
        return jnp.where(place == 0, 0.0, pltpu.roll(values, 1, 0))
    return jnp.where(place == HALF - 1, 0.0, pltpu.roll(values, HALF - 1, 0))


def zero_edges(*buffers):
    for buffer in buffers:
        lanes = buffer.shape[-1]
        for g in range(4):
            buffer[g, 0:HALF, :] = jnp.zeros((HALF, lanes), f32)
            buffer[g, HALF + PHASE : PADDED, :] = jnp.zeros((HALF, lanes), f32)


def tap_rows(plain, shifted, g, tap, row, lanes):
    _, phase, moved, step = TAPS[g][tap]
    buffer = shifted if moved else plain
    start = pl.multiple_of(HALF + (row + step) * HALF, HALF)
    return buffer[phase, pl.ds(start, HALF), lanes]


def spread_kernel(k_ref, lanes, flip):
    width = lanes.stop - lanes.start
    return [
        jnp.broadcast_to(k_ref[(8 - t if flip else t) : (8 - t if flip else t) + 1, lanes], (8, width))
        for t in range(9)
    ]


def conv_row(plain, shifted, spread, g, row, lanes):
    width = lanes.stop - lanes.start
    total = None
    for t in range(9):
        value = tap_rows(plain, shifted, g, t, row, lanes).reshape(2, 8, width)
        term = spread[t][None] * value
        total = term if total is None else total + term
    return total.reshape(HALF, width)


def kernel_sums(plain, shifted, grads, lanes):
    width = lanes.stop - lanes.start

    def body(row, sums):
        sums = list(sums)
        for g in range(4):
            start = pl.multiple_of(HALF + row * HALF, HALF)
            grad = grads[g, pl.ds(start, HALF), lanes].reshape(2, 8, width)
            for t in range(9):
                value = tap_rows(plain, shifted, g, t, row, lanes).reshape(2, 8, width)
                term = value * grad
                sums[t] = sums[t] + (term[0] + term[1])
        return tuple(sums)

    return lax.fori_loop(0, HALF, body, tuple(jnp.zeros((8, width), f32) for _ in range(9)), unroll=2)


def grid_permutation(inverse):
    size = 8 * SIDE
    token = lax.broadcasted_iota(jnp.int32, (size, size), 0 if inverse else 1)
    place = lax.broadcasted_iota(jnp.int32, (size, size), 1 if inverse else 0)
    r, c = token >> 5, token & 31
    target = ((r & 1) * 2 + (c & 1)) * 64 + (r >> 1) * HALF + (c >> 1)
    return jnp.where(target == place, 1.0, 0.0).astype(bf16)


ANYWHERE = pl.BlockSpec(memory_space=pl.ANY)
FREE = pl.CostEstimate(flops=1, bytes_accessed=1, transcendentals=0)


def start_copies(pairs, sems, first=0):
    copies = [pltpu.make_async_copy(src, dst, sems.at[first + i]) for i, (src, dst) in enumerate(pairs)]
    for copy in copies:
        copy.start()
    return copies


def wait_all(copies):
    for copy in copies:
        copy.wait()


def token_pieces(idx_ref, whole, got, sib_whole, sib_got, raw, sems, first=0):
    chip = idx_ref[7]
    return start_copies(
        [(whole.at[chip], raw.at[0]), (got, raw.at[1]), (sib_whole.at[chip], raw.at[2]), (sib_got, raw.at[3])],
        sems,
        first,
    )


def place_pieces(idx_ref, raw, target):
    perm = grid_permutation(False)
    for i in range(4):
        piece = dot_nn(perm, raw[i]).astype(bf16)
        for g in range(4):
            start = pl.multiple_of(g * PHASE + idx_ref[i] * 64, 64)
            target[pl.ds(start, 64), :] = piece[g * 64 : (g + 1) * 64, :]


def modulation_kernel(silu_ref, w_ref, out_ref):
    step = pl.program_id(0)
    part = dot_nn(silu_ref[...], w_ref[...].astype(bf16))
    for n in range(part.shape[0]):
        out_ref[n, pl.ds(step, 1), :] = part[n : n + 1, :]

    @pl.when(step == 0)
    def _():
        out_ref[:, 6:8, :] = jnp.zeros((part.shape[0], 2, part.shape[1]), f32)


def modulation_part(silu, w_mod, width):
    count = silu.shape[0]
    return pl.pallas_call(
        modulation_kernel,
        grid=(6,),
        out_shape=jax.ShapeDtypeStruct((count, 8, width), f32),
        in_specs=[
            pl.BlockSpec(silu.shape, lambda i: (0, 0)),
            pl.BlockSpec((w_mod.shape[0], width), lambda i: (0, i)),
        ],
        out_specs=pl.BlockSpec((count, 8, width), lambda i: (0, 0, 0)),
        compiler_params=params(8),
        cost_estimate=FREE,
        name="modulation_part",
    )(silu, w_mod)


def norm_rows(values):
    mean = jnp.mean(values, -1, keepdims=True)
    centred = values - mean
    variance = jnp.mean(centred * centred, -1, keepdims=True)
    scale = lax.rsqrt(variance + NORM_EPS)
    return centred * scale, scale


def fill_shifted(lat_ref, mod_ref, plain, shifted):
    if mod_ref is not None:
        gain = 1.0 + mod_ref[1:2, :]
        bias = mod_ref[0:1, :]
    for g in range(4):

        def body(j, carry):
            values = lat_ref[pl.ds(pl.multiple_of(g * PHASE + j * ROWS, ROWS), ROWS), :].astype(f32)
            result, _ = norm_rows(values)
            if mod_ref is not None:
                result = result * gain + bias
            start = pl.multiple_of(HALF + j * ROWS, HALF)
            plain[g, pl.ds(start, ROWS), :] = result
            for h in range(ROWS // HALF):
                part = result[h * HALF : (h + 1) * HALF]
                shifted[g, pl.ds(start + h * HALF, HALF), :] = shift_columns(part, g)
            return carry

        lax.fori_loop(0, PHASE // ROWS, body, 0, unroll=UNROLL)


def first_conv_kernel(idx_ref, own, got, sib, sib_got, k_ref, lat_ref, conv_ref, plain, shifted, raw, sems):
    copies = token_pieces(idx_ref, own, got, sib, sib_got, raw, sems)
    zero_edges(plain, shifted)
    wait_all(copies)
    place_pieces(idx_ref, raw, lat_ref)
    fill_shifted(lat_ref, None, plain, shifted)
    for first in range(0, conv_ref.shape[1], LANES):
        lanes = slice(first, first + LANES)
        spread = spread_kernel(k_ref, lanes, False)

        def body(row, carry):
            for g in range(4):
                start = pl.multiple_of(g * PHASE + row * HALF, HALF)
                conv_ref[pl.ds(start, HALF), lanes] = conv_row(plain, shifted, spread, g, row, lanes)
            return carry

        lax.fori_loop(0, HALF, body, 0, unroll=2)


def first_conv(idx, pieces, kernel):
    width = kernel.shape[1]
    return pl.pallas_call(
        first_conv_kernel,
        out_shape=(jax.ShapeDtypeStruct((TOKENS, width), bf16), jax.ShapeDtypeStruct((TOKENS, width), f32)),
        in_specs=[SMEM] + [ANYWHERE] * 4 + [VMEM],
        out_specs=(VMEM, VMEM),
        scratch_shapes=[pltpu.VMEM((4, PADDED, width), f32)] * 2
        + [pltpu.VMEM((4, TOKENS // 4, width), bf16), pltpu.SemaphoreType.DMA((4,))],
        compiler_params=params(14),
        cost_estimate=cost(30 * TOKENS * width, 8 * TOKENS * width),
        name="first_conv",
    )(idx, *pieces, kernel)


def modulate(conv_ref, mod_ref, k_ref, low_ref):
    gain = 1.0 + mod_ref[1:2, :]
    bias = mod_ref[0:1, :]
    taps = [k_ref[t : t + 1, :] for t in range(9)]
    width = conv_ref.shape[1]
    for g in range(4):
        a, b = g // 2, g % 2
        inner = [bias * (taps[j] + taps[3 + j] + taps[6 + j]) for j in range(3)]
        edge = [bias * (taps[3 + j] + (taps[6 + j] if a == 0 else taps[j])) for j in range(3)]
        side = 0 if b == 0 else 2
        place = lax.broadcasted_iota(jnp.int32, (HALF, width), 0)
        inside = place != (0 if b == 0 else HALF - 1)

        def body(row, carry):
            outer = row == (0 if a == 0 else HALF - 1)
            sums = [jnp.where(outer, e, i) for e, i in zip(edge, inner)]
            base = sums[1] + sums[2 - side]
            rows = pl.ds(pl.multiple_of(g * PHASE + row * HALF, HALF), HALF)
            value = conv_ref[rows, :] * gain + base + jnp.where(inside, sums[side], 0.0)
            low_ref[rows, :] = value.astype(bf16)
            return carry

        lax.fori_loop(0, HALF, body, 0, unroll=4)


def head_mask(shape, half):
    lane = lax.broadcasted_iota(jnp.int32, shape, 1)
    return (lane < HEAD_DIM) if half == 0 else (lane >= HEAD_DIM)


def attn_forward_kernel(
    idx_ref, conv_ref, mod_ref, k_ref, wa_ref, q0, q1, q2, q3,
    wcat, low_ref, proj_ref, att_t_ref, lse_ref, token_ref, wide, sems,
):
    token_ref[...] = jnp.zeros_like(token_ref)
    local = wa_ref.shape[0] // 3
    both = 2 * local
    step = local // 4
    place = idx_ref[5]
    pairs = []
    for index, quarter in ((2 * place, q0), (2 * place + 1, q1), (2 - 2 * place, q2), (3 - 2 * place, q3)):
        for j in range(3):
            chunk = 3 * index + j
            start = pl.multiple_of((chunk >> 2) * both + local + (chunk & 3) * step, 16)
            pairs.append((quarter.at[pl.ds(j * step, step), :], wcat.at[pl.ds(start, step), :]))
    copies = start_copies([(wa_ref, wide)] + pairs, sems)
    modulate(conv_ref, mod_ref, k_ref, low_ref)
    wait_all(copies)
    for t in range(3):
        wcat[t * both : t * both + local, :] = wide[t * local : (t + 1) * local, :].astype(bf16)

    def body(g, carry):
        rows = pl.ds(g * PHASE, PHASE)
        proj_ref[rows, :] = dot_nt(low_ref[rows, :], wcat[...]).astype(bf16)
        for pair in range(both // 128):
            q = proj_ref[rows, pair * 128 : (pair + 1) * 128] * jnp.asarray(HEAD_DIM**-0.5, bf16)
            k = proj_ref[rows, both + pair * 128 : both + (pair + 1) * 128]
            v = proj_ref[rows, 2 * both + pair * 128 : 2 * both + (pair + 1) * 128]
            v_t = v.T
            halves = range(2)
            scores = [dot_nt(k, jnp.where(head_mask(q.shape, h), q, jnp.zeros_like(q))) for h in halves]
            tops = [jnp.max(x, 0, keepdims=True) for x in scores]
            weights = [jnp.exp(x - top) for x, top in zip(scores, tops)]
            totals = [jnp.sum(x, 0, keepdims=True) for x in weights]
            for half in halves:
                head = 2 * pair + half
                lse_ref[g, head : head + 1, :] = tops[half] + jnp.log(totals[half])
                out_t = dot_nn(v_t[half * HEAD_DIM : (half + 1) * HEAD_DIM, :], weights[half].astype(bf16))
                out_t = out_t * (1.0 / totals[half])
                att_t_ref[g, head * HEAD_DIM : (head + 1) * HEAD_DIM, :] = out_t.astype(bf16)
        return carry

    for g in range(4):
        body(g, 0)


def attn_forward(idx, conv, mod, kernel, wa, quarters):
    rows, width = wa.shape
    both = 2 * rows // 3
    return pl.pallas_call(
        attn_forward_kernel,
        out_shape=(
            jax.ShapeDtypeStruct((2 * rows, width), bf16),
            jax.ShapeDtypeStruct((TOKENS, width), bf16),
            jax.ShapeDtypeStruct((TOKENS, 3 * both), bf16),
            jax.ShapeDtypeStruct((4, both, PHASE), bf16),
            jax.ShapeDtypeStruct((4, 8, PHASE), f32),
            jax.ShapeDtypeStruct((8, 128), f32),
        ),
        in_specs=[SMEM] + [VMEM] * 3 + [ANYWHERE] * 5,
        out_specs=(VMEM,) * 6,
        scratch_shapes=[pltpu.VMEM((rows, width), f32), pltpu.SemaphoreType.DMA((13,))],
        compiler_params=params(16),
        cost_estimate=cost(8 * TOKENS * both * width + 8 * TOKENS * PHASE * both, 12 << 20),
        name="attn_forward",
    )(idx, conv, mod, kernel, wa, *quarters)


def second_norm_kernel(
    idx_ref, lat_ref, own_ref, sib_ref, oa, ob, sa, sb, cot_own, cot_got, cot_sib, cot_sib_got, mod_ref,
    attn_ref, mixed, mixed_t, fgl, cot, wo, heads, raw, sems,
):
    local = oa.shape[0]
    core = idx_ref[4]
    mine = pl.multiple_of(core * 2 * local, local)
    theirs = pl.multiple_of((1 - core) * 2 * local, local)
    weights = start_copies(
        [
            (oa, wo.at[pl.ds(mine, local), :]),
            (ob.at[pl.ds(0, local), :], wo.at[pl.ds(mine + local, local), :]),
            (sa, wo.at[pl.ds(theirs, local), :]),
            (sb.at[pl.ds(0, local), :], wo.at[pl.ds(theirs + local, local), :]),
        ]
        + [(sib_ref.at[g], heads.at[g, pl.ds(theirs, 2 * local), :]) for g in range(4)],
        sems,
    )
    tokens = token_pieces(idx_ref, cot_own, cot_got, cot_sib, cot_sib_got, raw, sems, 8)
    for g in range(4):
        heads[g, pl.ds(mine, 2 * local), :] = own_ref[g]
    wait_all(weights)
    for g in range(4):
        attn_ref[g * PHASE : (g + 1) * PHASE, :] = dot_tn(heads[g], wo[...]).astype(bf16)
    wait_all(tokens)
    place_pieces(idx_ref, raw, cot)
    gate_one = mod_ref[2:3, :]
    bias = mod_ref[3:4, :]
    gain = 1.0 + mod_ref[4:5, :]
    gate_two = mod_ref[5:6, :]
    live = idx_ref[8].astype(f32)

    def body(j, carry):
        rows = pl.ds(pl.multiple_of(j * ROWS, ROWS), ROWS)
        resid = lat_ref[rows, :].astype(f32) + gate_one * attn_ref[rows, :].astype(f32)
        normed, _ = norm_rows(resid)
        mixed[rows, :] = (normed * gain + bias).astype(bf16)
        grad = live * cot[rows, :].astype(f32)
        cot[rows, :] = grad.astype(bf16)
        fgl[rows, :] = (gate_two * grad).astype(bf16)
        return carry

    lax.fori_loop(0, TOKENS // ROWS, body, 0, unroll=UNROLL)
    mixed_t[...] = mixed[...].T


def second_norm(idx, lat, own, sib, outs, cots, mod):
    width = lat.shape[1]
    whole = jax.ShapeDtypeStruct((TOKENS, width), bf16)
    return pl.pallas_call(
        second_norm_kernel,
        out_shape=(whole, whole, jax.ShapeDtypeStruct((width, TOKENS), bf16), whole, whole),
        in_specs=[SMEM] + [VMEM] * 2 + [ANYWHERE] * 9 + [VMEM],
        out_specs=(VMEM,) * 5,
        scratch_shapes=[
            pltpu.VMEM((width, width), bf16),
            pltpu.VMEM((4, width, PHASE), bf16),
            pltpu.VMEM((4, TOKENS // 4, width), bf16),
            pltpu.SemaphoreType.DMA((12,)),
        ],
        compiler_params=params(16),
        cost_estimate=cost(2 * TOKENS * width * width, 16 * TOKENS * width),
        name="second_norm",
    )(idx, lat, own, sib, *outs, *cots, mod)


def ffn_tile(at, lanes, mixed, mixed_t, fgl, w1, w2, k_ref, buffers, act, hidden_grad, kg_ref):
    plain, shifted, grad, grad_shifted = buffers
    here = slice(0, LANES)
    there = slice(at, at + LANES)
    for g in range(4):
        rows = slice(g * PHASE, (g + 1) * PHASE)
        plain[g, HALF : HALF + PHASE, :] = dot_nn(mixed[rows, :], w1[:, lanes])
        grad[g, HALF : HALF + PHASE, :] = dot_nt(fgl[rows, :], w2[lanes, :])

    def shift_body(row, carry):
        rows = pl.ds(pl.multiple_of(HALF + row * HALF, HALF), HALF)
        for g in range(4):
            shifted[g, rows, :] = shift_columns(plain[g, rows, :], g)
        return carry

    lax.fori_loop(0, HALF, shift_body, 0, unroll=4)
    spread = [
        jnp.broadcast_to(k_ref[t : t + 1, lanes], (8, LANES)) for t in range(9)
    ]

    def act_body(row, carry):
        padded = pl.ds(pl.multiple_of(HALF + row * HALF, HALF), HALF)
        for g in range(4):
            pre = conv_row(plain, shifted, spread, g, row, here)
            square = pre * pre
            tanh = jnp.tanh(pre * (GELU_C + (GELU_C * GELU_A) * square))
            half = 0.5 + 0.5 * tanh
            rows = pl.ds(pl.multiple_of(g * PHASE + row * HALF, HALF), HALF)
            act[rows, there] = (pre * half).astype(bf16)
            slope = half + (0.5 * pre) * (1.0 - tanh * tanh) * (
                GELU_C + (3.0 * GELU_C * GELU_A) * square
            )
            result = grad[g, padded, :] * slope
            grad[g, padded, :] = result
            grad_shifted[g, padded, :] = shift_columns(result, g)
        return carry

    lax.fori_loop(0, HALF, act_body, 0, unroll=2)
    flipped = spread[::-1]

    def back_body(row, carry):
        for g in range(4):
            rows = pl.ds(pl.multiple_of(g * PHASE + row * HALF, HALF), HALF)
            hidden_grad[rows, there] = conv_row(grad, grad_shifted, flipped, g, row, here).astype(bf16)
        return carry

    lax.fori_loop(0, HALF, back_body, 0, unroll=2)
    sums = kernel_sums(plain, shifted, grad, here)
    for t in range(9):
        kg_ref[t : t + 1, there] = jnp.sum(sums[t], 0, keepdims=True)
    second = dot_tn(act[:, there], fgl[...])
    one = dot_nn(mixed_t[...], hidden_grad[:, there])
    return one, second


def fold_rows(one):
    return jnp.concatenate([one[i : i + LANES, :] for i in range(0, one.shape[0], LANES)], 1)


def ffn_first_kernel(
    idx_ref, mixed, mixed_t, fgl, near, far_y, far_z, diag_one, diag_two, k_ref,
    w1, w2, act, hidden_grad, send_ref, kg_ref, *rest,
):
    buffers, sems = rest[:4], rest[4]
    size = diag_one.shape[0]
    quarter = idx_ref[6]
    pairs = []
    for index, one, two in (
        (quarter, near.at[pl.ds(0, size), :], near.at[pl.ds(size, size), :]),
        (quarter ^ 1, far_y.at[pl.ds(0, size), :], far_y.at[pl.ds(size, size), :]),
        (quarter ^ 2, far_z.at[pl.ds(0, size), :], far_z.at[pl.ds(size, size), :]),
        (quarter ^ 3, diag_one, diag_two),
    ):
        rows = pl.ds(pl.multiple_of(index * size, 64), size)
        pairs += [(one, w1.at[rows, :]), (two, w2.at[rows, :])]
    copies = start_copies(pairs, sems)
    zero_edges(*buffers)
    kg_ref[9:16, :] = jnp.zeros((7, kg_ref.shape[1]), f32)
    wait_all(copies)
    one, second = ffn_tile(
        0, slice(0, LANES), mixed, mixed_t, fgl, w1, w2, k_ref, buffers, act, hidden_grad, kg_ref
    )
    send_ref[0:LANES, :] = second.astype(bf16)
    send_ref[LANES : 2 * LANES, :] = fold_rows(one).astype(bf16)


def ffn_scratch():
    return [pltpu.VMEM((4, PADDED, LANES), f32)] * 4


def ffn_first(idx, mixed, mixed_t, fgl, pieces, kernel):
    width, units = mixed.shape[1], kernel.shape[1]
    tile = jax.ShapeDtypeStruct((TOKENS, LANES), bf16)
    return pl.pallas_call(
        ffn_first_kernel,
        out_shape=(
            jax.ShapeDtypeStruct((width, units), bf16),
            jax.ShapeDtypeStruct((units, width), bf16),
            tile,
            tile,
            jax.ShapeDtypeStruct((2 * LANES, width), bf16),
            jax.ShapeDtypeStruct((16, LANES), f32),
        ),
        in_specs=[SMEM] + [VMEM] * 3 + [ANYWHERE] * 5 + [VMEM],
        out_specs=(VMEM,) * 6,
        scratch_shapes=ffn_scratch() + [pltpu.SemaphoreType.DMA((8,))],
        compiler_params=params(12),
        cost_estimate=FREE,
        name="ffn_first",
    )(idx, mixed, mixed_t, fgl, *pieces, kernel)


def ffn_sums(act, hidden_grad, w1, w2, ffn_out, mix_out, before=None):
    for g in range(4):
        rows = slice(g * PHASE, (g + 1) * PHASE)
        ffn_part = dot_nn(act[rows, :], w2[...])
        mix_part = dot_nt(hidden_grad[rows, :], w1[...])
        if before is not None:
            ffn_part = ffn_part + before[0][rows, :].astype(f32)
            mix_part = mix_part + before[1][rows, :].astype(f32)
        ffn_out[rows, :] = ffn_part.astype(bf16)
        mix_out[rows, :] = mix_part.astype(bf16)


def ffn_second_kernel(
    mixed, mixed_t, fgl, w1, w2, act_in, hidden_in, k_ref,
    ffn_out, mix_out, send_ref, late_ref, kg_ref, *rest,
):
    buffers, act, hidden_grad = rest[:4], rest[4], rest[5]
    zero_edges(*buffers)
    kg_ref[9:16, :] = jnp.zeros((7, kg_ref.shape[1]), f32)
    act[:, 0:LANES] = act_in[...]
    hidden_grad[:, 0:LANES] = hidden_in[...]
    soon = send_ref.shape[0] - LANES
    at = 0
    for first in range(LANES, w1.shape[1], LANES):
        lanes = slice(first, first + LANES)
        one, second = ffn_tile(
            first, lanes, mixed, mixed_t, fgl, w1, w2, k_ref, buffers, act, hidden_grad, kg_ref
        )
        folded = fold_rows(one).astype(bf16)
        if first == LANES:
            send_ref[0:LANES, :] = second.astype(bf16)
            send_ref[LANES : LANES + soon, :] = folded[0:soon, :]
            at = LANES - soon
            late_ref[0:at, :] = folded[soon:LANES, :]
        else:
            late_ref[at : at + LANES, :] = second.astype(bf16)
            late_ref[at + LANES : at + 2 * LANES, :] = folded
            at += 2 * LANES
    ffn_sums(act, hidden_grad, w1, w2, ffn_out, mix_out)


def ffn_second(mixed, mixed_t, fgl, w1, w2, act, hidden_grad, kernel):
    width, units = mixed.shape[1], kernel.shape[1]
    rows = 2 * (units - LANES)
    soon = LANES + LANES // 2
    whole = jax.ShapeDtypeStruct((TOKENS, width), bf16)
    return pl.pallas_call(
        ffn_second_kernel,
        out_shape=(
            whole,
            whole,
            jax.ShapeDtypeStruct((soon, width), bf16),
            jax.ShapeDtypeStruct((rows - soon, width), bf16),
            jax.ShapeDtypeStruct((16, units), f32),
        ),
        in_specs=[VMEM] * 8,
        out_specs=(VMEM,) * 5,
        scratch_shapes=ffn_scratch() + [pltpu.VMEM((TOKENS, units), bf16)] * 2,
        compiler_params=params(16),
        cost_estimate=FREE,
        name="ffn_second",
    )(mixed, mixed_t, fgl, w1, w2, act, hidden_grad, kernel)


def ffn_own_kernel(
    mixed, mixed_t, fgl, w1_ref, w2_ref, k_ref, ffn_in, mix_in, ffn_out, mix_out, grads_ref, kg_ref, *rest,
):
    buffers, act, hidden_grad, w1, w2 = rest[:4], rest[4], rest[5], rest[6], rest[7]
    width = mixed.shape[1]
    w1[...] = w1_ref[...].astype(bf16)
    w2[...] = w2_ref[...].astype(bf16)
    zero_edges(*buffers)
    kg_ref[9:16, :] = jnp.zeros((7, kg_ref.shape[1]), f32)
    for first in range(0, w1.shape[1], LANES):
        lanes = slice(first, first + LANES)
        one, second = ffn_tile(
            first, lanes, mixed, mixed_t, fgl, w1, w2, k_ref, buffers, act, hidden_grad, kg_ref
        )
        grads_ref[0:width, lanes] = one
        grads_ref[width + first : width + first + LANES, :] = second
    ffn_sums(act, hidden_grad, w1, w2, ffn_out, mix_out, (ffn_in, mix_in))


def ffn_own(mixed, mixed_t, fgl, w1, w2, kernel, before):
    width, units = w1.shape
    whole = jax.ShapeDtypeStruct((TOKENS, width), bf16)
    return pl.pallas_call(
        ffn_own_kernel,
        out_shape=(
            whole,
            whole,
            jax.ShapeDtypeStruct((width + units, width), f32),
            jax.ShapeDtypeStruct((16, units), f32),
        ),
        in_specs=[VMEM] * 8,
        out_specs=(VMEM,) * 4,
        scratch_shapes=ffn_scratch()
        + [pltpu.VMEM((TOKENS, units), bf16)] * 2
        + [pltpu.VMEM((width, units), bf16), pltpu.VMEM((units, width), bf16)],
        compiler_params=params(20),
        cost_estimate=FREE,
        name="ffn_own",
    )(mixed, mixed_t, fgl, w1, w2, kernel, *before)


def attn_backward_kernel(
    lat_ref, attn_ref, cot_ref, mo_ref, mr_ref, mod_ref, conv_ref, proj_ref, att_t_ref, lse_ref, wcat, oa, ob,
    part_ref, resid_ref, mine_ref, send_ref, send_k_ref, send_v_ref, sums_ref,
    low, proj_t, grads, sums, wo,
):
    both = wcat.shape[0] // 3
    local = both // 2
    width = wcat.shape[1]
    wo[0:local, :] = oa[...]
    wo[local:both, :] = ob[0:local, :]
    sums[...] = jnp.zeros_like(sums)
    gate_one = mod_ref[2:3, :]
    gain = 1.0 + mod_ref[4:5, :]

    def fold(values):
        return jnp.sum(values.reshape(ROWS // 8, 8, width), 0)

    def norm_body(j, carry):
        rows = pl.ds(pl.multiple_of(j * ROWS, ROWS), ROWS)
        attn = attn_ref[rows, :].astype(f32)
        resid = lat_ref[rows, :].astype(f32) + gate_one * attn
        normed, scale = norm_rows(resid)
        mixed = mo_ref[rows, :].astype(f32) + mr_ref[rows, :].astype(f32)
        u = mixed * gain
        mean_u = jnp.mean(u, -1, keepdims=True)
        mean_un = jnp.mean(u * normed, -1, keepdims=True)
        grad = cot_ref[rows, :].astype(f32) + scale * (u - mean_u - normed * mean_un)
        resid_ref[rows, :] = grad
        low[rows, :] = (gate_one * grad).astype(bf16)
        sums[0] += fold(attn * grad)
        sums[1] += fold(mixed)
        sums[2] += fold(mixed * normed)
        return carry

    lax.fori_loop(0, TOKENS // ROWS, norm_body, 0, unroll=UNROLL)
    for t in range(3):
        sums_ref[t : t + 1, :] = jnp.sum(sums[t], 0, keepdims=True)
    sums_ref[3:8, :] = jnp.zeros((5, width), f32)
    scale = HEAD_DIM**-0.5

    def body(g, carry):
        rows = pl.ds(g * PHASE, PHASE)
        d_att = dot_nt(low[rows, :], wo[...]).astype(bf16)
        d_att_t = dot_nt(wo[...], low[rows, :]).astype(bf16)
        for pair in range(both // 128):
            q = proj_ref[rows, pair * 128 : (pair + 1) * 128] * jnp.asarray(scale, bf16)
            k = proj_ref[rows, both + pair * 128 : both + (pair + 1) * 128]
            v = proj_ref[rows, 2 * both + pair * 128 : 2 * both + (pair + 1) * 128]
            d_out = d_att[:, pair * 128 : (pair + 1) * 128]
            q_t = q.T
            k_t = k.T
            halves = range(2)
            masks = [head_mask(q.shape, h) for h in halves]
            scores = [dot_nt(k, jnp.where(mask, q, jnp.zeros_like(q))) for mask in masks]
            prob_grads = [dot_nt(v, jnp.where(mask, d_out, jnp.zeros_like(d_out))) for mask in masks]
            probs = [jnp.exp(scores[h] - lse_ref[g, 2 * pair + h : 2 * pair + h + 1, :]) for h in halves]
            means = [jnp.sum(probs[h] * prob_grads[h], 0, keepdims=True) for h in halves]
            score_grads = [(probs[h] * (prob_grads[h] - means[h])).astype(bf16) for h in halves]
            for half in halves:
                own = slice(half * HEAD_DIM, (half + 1) * HEAD_DIM)
                at = (2 * pair + half) * HEAD_DIM
                d_head = d_att_t[at : at + HEAD_DIM, :]
                score_grad, low_probs = score_grads[half], probs[half].astype(bf16)
                proj_t[g, at : at + HEAD_DIM, :] = (dot_nn(k_t[own, :], score_grad) * scale).astype(bf16)
                proj_t[g, both + at : both + at + HEAD_DIM, :] = dot_nt(q_t[own, :], score_grad).astype(bf16)
                proj_t[g, 2 * both + at : 2 * both + at + HEAD_DIM, :] = dot_nt(d_head, low_probs).astype(bf16)
        part_ref[rows, :] = dot_tn(proj_t[g], wcat[...]).astype(bf16)
        return carry

    for g in range(4):
        body(g, 0)

    def total(rows_of, other):
        result = None
        for g in range(4):
            term = dot_nn(rows_of(g), other[g * PHASE : (g + 1) * PHASE, :])
            result = term if result is None else result + term
        return result

    for t in range(4):
        for side in range(2):
            if t < 3:
                first = t * both + side * local
                value = total(lambda g: proj_t[g, first : first + local, :], conv_ref)
            else:
                value = total(lambda g: att_t_ref[g, side * local : (side + 1) * local, :], low)
            if side == 0:
                mine_ref[t * local : (t + 1) * local, :] = value
            else:
                target, at = ((send_ref, local), (send_k_ref, 0), (send_v_ref, 0), (send_ref, 0))[t]
                target[at : at + local, :] = value.astype(bf16)


def attn_backward(lat, attn, cot, mix_own, mix_got, mod, conv_low, proj, att_t, lse, wcat, out_a, out_b):
    both = wcat.shape[0] // 3
    width = lat.shape[1]
    return pl.pallas_call(
        attn_backward_kernel,
        out_shape=(
            jax.ShapeDtypeStruct((TOKENS, width), bf16),
            jax.ShapeDtypeStruct((TOKENS, width), f32),
            jax.ShapeDtypeStruct((2 * both, width), f32),
            jax.ShapeDtypeStruct((both, width), bf16),
            jax.ShapeDtypeStruct((both // 2, width), bf16),
            jax.ShapeDtypeStruct((both // 2, width), bf16),
            jax.ShapeDtypeStruct((8, width), f32),
        ),
        in_specs=[VMEM] * 13,
        out_specs=(VMEM,) * 7,
        scratch_shapes=[
            pltpu.VMEM((TOKENS, width), bf16),
            pltpu.VMEM((4, 3 * both, PHASE), bf16),
            pltpu.VMEM((8, 128), f32),
            pltpu.VMEM((3, 8, width), f32),
            pltpu.VMEM((both, width), bf16),
        ],
        compiler_params=params(20),
        cost_estimate=pl.CostEstimate(flops=1, bytes_accessed=1, transcendentals=0),
        name="attn_backward",
    )(lat, attn, cot, mix_own, mix_got, mod, conv_low, proj, att_t, lse, wcat, out_a, out_b)


def tail_kernel(
    idx_ref, lat_ref, attn_ref, fo_ref, fr_ref, co_ref, cr_ref, cot_ref, resid_ref, two_ref, mod_ref, k_ref,
    own_ref, send_ref, kg_ref, rows_ref,
    plain, shifted, grad, grad_shifted, out_low, sums,
):
    width = lat_ref.shape[1]
    zero_edges(plain, shifted, grad, grad_shifted)
    fill_shifted(lat_ref, mod_ref, plain, shifted)
    def grad_body(row, carry):
        padded = pl.ds(pl.multiple_of(HALF + row * HALF, HALF), HALF)
        for g in range(4):
            rows = pl.ds(pl.multiple_of(g * PHASE + row * HALF, HALF), HALF)
            values = co_ref[rows, :].astype(f32) + cr_ref[rows, :].astype(f32)
            grad[g, padded, :] = values
            grad_shifted[g, padded, :] = shift_columns(values, g)
        return carry

    lax.fori_loop(0, HALF, grad_body, 0, unroll=2)
    for first in range(0, width, LANES):
        lanes = slice(first, first + LANES)
        totals = kernel_sums(plain, shifted, grad, lanes)
        for t in range(9):
            kg_ref[t : t + 1, lanes] = jnp.sum(totals[t], 0, keepdims=True)
    for first in range(0, width, LANES):
        lanes = slice(first, first + LANES)
        flipped = spread_kernel(k_ref, lanes, True)

        def back_body(row, carry):
            padded = pl.ds(pl.multiple_of(HALF + row * HALF, HALF), HALF)
            for g in range(4):
                plain[g, padded, lanes] = conv_row(grad, grad_shifted, flipped, g, row, lanes)
            return carry

        lax.fori_loop(0, HALF, back_body, 0, unroll=2)
    sums[...] = jnp.zeros_like(sums)
    gate_one = mod_ref[2:3, :]
    gate_two = mod_ref[5:6, :]
    live = idx_ref[8].astype(f32)
    gain = 1.0 + mod_ref[1:2, :]

    def fold(values):
        return jnp.sum(values.reshape(ROWS // 8, 8, width), 0)

    for g in range(4):

        def body(j, carry):
            rows = pl.ds(pl.multiple_of(g * PHASE + j * ROWS, ROWS), ROWS)
            latent = lat_ref[rows, :].astype(f32)
            attn = attn_ref[rows, :].astype(f32)
            ffn_out = fo_ref[rows, :].astype(f32) + fr_ref[rows, :].astype(f32)
            out = live * (latent + gate_one * attn + gate_two * ffn_out)
            out_low[0, rows, :] = out.astype(bf16)
            sums[2] += fold(ffn_out * cot_ref[rows, :].astype(f32))
            normed, scale = norm_rows(latent)
            back = plain[g, pl.ds(pl.multiple_of(HALF + j * ROWS, HALF), ROWS), :]
            u = back * gain
            mean_u = jnp.mean(u, -1, keepdims=True)
            mean_un = jnp.mean(u * normed, -1, keepdims=True)
            result = resid_ref[rows, :] + scale * (u - mean_u - normed * mean_un)
            out_low[1, rows, :] = result.astype(bf16)
            sums[0] += fold(back)
            sums[1] += fold(back * normed)
            return carry

        lax.fori_loop(0, PHASE // ROWS, body, 0, unroll=UNROLL)
    for t, row in enumerate((0, 1, 5)):
        rows_ref[row : row + 1, :] = jnp.sum(sums[t], 0, keepdims=True)
    rows_ref[2:5, :] = two_ref[0:3, :]
    rows_ref[6:8, :] = jnp.zeros((2, width), f32)
    kg_ref[9:16, :] = jnp.zeros((7, width), f32)
    perm = grid_permutation(True)
    for i, target in ((0, own_ref), (1, send_ref)):
        block = idx_ref[i]
        for which in range(2):
            values = jnp.concatenate(
                [
                    out_low[which, pl.ds(pl.multiple_of(g * PHASE + block * 64, 64), 64), :]
                    for g in range(4)
                ],
                0,
            )
            target[which] = dot_nn(perm, values).astype(bf16)


def tail(midx, lat, attn, ffn_own, ffn_got, conv_own, conv_got, cot, resid, two, mod, kernel):
    width = lat.shape[1]
    share = jax.ShapeDtypeStruct((2, TOKENS // 4, width), bf16)
    padded = pltpu.VMEM((4, PADDED, width), f32)
    return pl.pallas_call(
        tail_kernel,
        out_shape=(
            share,
            share,
            jax.ShapeDtypeStruct((16, width), f32),
            jax.ShapeDtypeStruct((8, width), f32),
        ),
        in_specs=[SMEM] + [VMEM] * 11,
        out_specs=(VMEM,) * 4,
        scratch_shapes=[padded] * 4 + [pltpu.VMEM((2, TOKENS, width), bf16), pltpu.VMEM((3, 8, width), f32)],
        compiler_params=params(30),
        cost_estimate=pl.CostEstimate(flops=1, bytes_accessed=1, transcendentals=0),
        name="tail",
    )(midx, lat, attn, ffn_own, ffn_got, conv_own, conv_got, cot, resid, two, mod, kernel)


def split_rows(values):
    high = values.astype(bf16).astype(f32)
    return jnp.concatenate([high, values - high], 0).astype(bf16)


def thin(product, rows, matrix):
    both = split_rows(rows)
    if matrix.dtype == bf16:
        result = product(both, matrix)
        return result[0:8] + result[8:16]
    high = matrix.astype(bf16)
    low = (matrix - high.astype(f32)).astype(bf16)
    first, second = product(both, high), product(both, low)
    return (first[0:8] + first[8:16]) + (second[0:8] + second[8:16])


def merge_ffn_kernel(
    grads_ref, piece_ref, soon_ref, late_ref, err1_ref, err2_ref, start1_ref, start2_ref, merged_ref, left_ref
):
    width = err1_ref.shape[0]
    pieces = [piece_ref, soon_ref, late_ref]
    edges = [0, piece_ref.shape[0], piece_ref.shape[0] + soon_ref.shape[0], 2 * width]

    def got(first, count, lanes):
        parts = []
        for ref, low, high in zip(pieces, edges[:-1], edges[1:]):
            begin, end = max(first, low), min(first + count, high)
            if begin < end:
                parts.append(ref[begin - low : end - low, lanes])
        return (parts[0] if len(parts) == 1 else jnp.concatenate(parts, 0)).astype(f32)

    for block, first in enumerate(range(0, width, LANES)):
        rows = slice(first, first + LANES)
        folded = [got(2 * LANES * t + LANES, LANES, rows) for t in range(width // LANES)]
        one = grads_ref[rows, :] + jnp.concatenate(folded, 1) + err1_ref[rows, :]
        merged_ref[rows, :] = one
        left_ref[0:8, rows] = thin(dot_nt, start1_ref[...], one)
        below = slice(width + first, width + first + LANES)
        second = got(2 * LANES * block, LANES, slice(0, width))
        two = grads_ref[below, :] + second + err2_ref[rows, :]
        merged_ref[below, :] = two
        left_ref[8:16, rows] = thin(dot_nt, start2_ref[...], two)


def merge_ffn(grads, pieces, err1, err2, start1, start2):
    width = err1.shape[0]
    return pl.pallas_call(
        merge_ffn_kernel,
        out_shape=(
            jax.ShapeDtypeStruct(grads.shape, f32),
            jax.ShapeDtypeStruct((16, width), f32),
        ),
        in_specs=[VMEM] * 8,
        out_specs=(VMEM,) * 2,
        compiler_params=params(10),
        cost_estimate=FREE,
        name="merge_ffn",
    )(grads, *pieces, err1, err2, start1, start2)


def left_attn_kernel(
    mine_ref, send_ref, send_k_ref, send_v_ref, _, kg_one, kg_two, err_ref, err_out_ref, start_ref, start_b_ref, start_out_ref,
    merged_ref, left_ref, bulk_ref,
):
    local = err_out_ref.shape[0]
    width = mine_ref.shape[1]
    left, left_b = None, None
    for t in range(3):
        rows = slice(t * local, (t + 1) * local)
        start, start_b = start_ref[8 * t : 8 * t + 8, :], start_b_ref[8 * t : 8 * t + 8, :]
        total = mine_ref[rows, :] + err_ref[rows, :]
        merged_ref[rows, :] = total
        term = thin(dot_nn, start, total)
        other = (send_ref[local : 2 * local, :], send_k_ref[...], send_v_ref[...])[t]
        term_b = thin(dot_nn, start_b, other)
        left = term if left is None else left + term
        left_b = term_b if left_b is None else left_b + term_b
    rows = slice(3 * local, 4 * local)
    total = mine_ref[rows, :] + err_out_ref[...]
    merged_ref[rows, :] = total
    left_ref[0:8, :] = left
    left_ref[8:16, :] = jnp.zeros((8, width), f32)
    left_ref[8:16, 0:local] = thin(dot_nt, start_out_ref[...], total)
    left_out = thin(dot_nt, start_out_ref[...], send_ref[0:local, :])
    left_out = jnp.concatenate([left_out, jnp.zeros((8, width - local), f32)], 1)
    size = 2 * local
    tile = kg_one.shape[1]
    bulk_ref[0:size, :] = send_ref[...]
    bulk_ref[size : size + 16, :] = jnp.concatenate([left_b, left_out], 0).astype(bf16)
    bulk_ref[size + 16 : size + 32, 0:tile] = kg_one[...].astype(bf16)
    bulk_ref[size + 16 : size + 32, tile:width] = kg_two[:, tile:width].astype(bf16)


def left_attn(mine, send, send_k, send_v, late, kg_one, kg_two, err_qkv, err_out, start, start_b, start_out):
    width = mine.shape[1]
    piece = jax.ShapeDtypeStruct((16, width), f32)
    return pl.pallas_call(
        left_attn_kernel,
        out_shape=(
            jax.ShapeDtypeStruct(mine.shape, f32),
            piece,
            jax.ShapeDtypeStruct((send.shape[0] + 32, width), bf16),
        ),
        in_specs=[VMEM] * 4 + [ANYWHERE] + [VMEM] * 7,
        out_specs=(VMEM,) * 3,
        compiler_params=params(12),
        cost_estimate=cost(mine.size * 64, mine.size * 12),
        name="left_attn",
    )(mine, send, send_k, send_v, late, kg_one, kg_two, err_qkv, err_out, start, start_b, start_out)


def orthonormal(factor):
    place = lax.broadcasted_iota(jnp.int32, (8, 1), 0)
    for k in range(8):
        products = jnp.sum(factor * factor[k : k + 1, :], -1, keepdims=True)
        scale = lax.rsqrt(products[k : k + 1, :] + ORTHO_EPS)
        column = factor[k : k + 1, :] * scale
        weight = jnp.where(place > k, products * scale, 0.0)
        factor = jnp.where(place == k, column, factor - weight * column)
    return factor


def right_kernel(inverse, left_ref, part_ref, got_ref, got_k, got_v, ffn_ref, basis_ref, columns_ref, right_ref, merged_ref):
    local = part_ref.shape[0] // 4
    width = part_ref.shape[1]
    basis = [orthonormal(left_ref[8 * m : 8 * m + 8, :] * inverse) for m in range(4)]
    stack = []
    for m in range(4):
        high = basis[m].astype(bf16).astype(f32)
        stack += [high, high, basis[m] - high]
    stack.append(jnp.zeros((32, width), f32))
    columns_ref[...] = jnp.concatenate(stack, 0).T.astype(bf16)
    basis_ref[...] = basis[0]
    for t, got in enumerate((got_ref[local : 2 * local, :], got_k[...], got_v[...])):
        rows = slice(t * local, (t + 1) * local)
        merged_ref[rows, :] = part_ref[rows, :] + got.astype(f32)
    total = merged_ref[0 : 3 * local, :]
    total_out = part_ref[3 * local : 4 * local, :] + got_ref[0:local, :].astype(f32)
    merged_ref[3 * local : 4 * local, :] = total_out
    right_ref[0:8, :] = jnp.zeros((8, width), f32)
    right_ref[0:8, 0 : 3 * local] = thin(dot_nt, basis[0], total)
    right_ref[8:16, :] = thin(dot_nn, basis[1][:, 0:local], total_out)
    right_ref[16:24, :] = thin(dot_nn, basis[2], ffn_ref[0:width, :])
    right_ref[24:32, :] = thin(dot_nn, basis[3], ffn_ref[width : 2 * width, :])


def right_factors(left, part, got, ffn_merged, count):
    width = part.shape[1]
    return pl.pallas_call(
        functools.partial(right_kernel, 1.0 / count),
        out_shape=(
            jax.ShapeDtypeStruct((8, width), f32),
            jax.ShapeDtypeStruct((width, 128), bf16),
            jax.ShapeDtypeStruct((32, width), f32),
            jax.ShapeDtypeStruct(part.shape, f32),
        ),
        in_specs=[VMEM] * 6,
        out_specs=(VMEM,) * 4,
        compiler_params=params(20),
        cost_estimate=cost(part.size * 200, part.size * 30),
        name="right_factors",
    )(left, part, *got, ffn_merged)


def final_kernel(
    inverse, _, right_ref, basis_ref, columns_ref, conv_g, conv_w, conv_m, attn_ref, ffn_ref,
    wq, mq, wo, mo, w1, m1, w2, m2,
    q_w, q_m, q_e, o_w, o_m, o_e, f1_w, f1_m, f1_e, f2_w, f2_m, f2_e, conv_w_new, conv_m_new,
    factors, q_columns, staged, loaded, sems, load_sems,
):
    width = attn_ref.shape[1]
    size = staged.shape[2]
    blocks, at = [], 0
    for m, (sources, outs, columns, rate) in enumerate(
        (
            ((wq, mq), (q_w, q_m, q_e), q_columns, LEARN_RATE),
            ((wo, mo), (o_w, o_m, o_e), columns_ref, FAST_RATE),
            ((w1, m1), (f1_w, f1_m, f1_e), columns_ref, LEARN_RATE),
            ((w2, m2), (f2_w, f2_m, f2_e), columns_ref, LEARN_RATE),
        )
    ):
        for first in range(0, outs[0].shape[0], size):
            blocks.append((m, sources, outs, columns, rate, first, at + first))
        at += outs[0].shape[0]

    arriving = []
    for i, (_, sources, _, _, _, first, _) in enumerate(blocks):
        pairs = [(source.at[pl.ds(first, size), :], loaded.at[i, j]) for j, source in enumerate(sources)]
        arriving.append(start_copies(pairs, load_sems, 2 * i))
    factors[...] = jnp.zeros_like(factors)
    for m in range(4):
        right = right_ref[8 * m : 8 * m + 8, :] * inverse
        high = right.astype(bf16).astype(f32)
        if m == 0:
            stack = [high, right - high, high, jnp.zeros((104, width), f32)]
            q_columns[...] = jnp.concatenate(stack, 0).T.astype(bf16)
            near = basis_ref[...].astype(bf16).astype(f32)
            part = jnp.concatenate([near, near, basis_ref[...] - near], 0)
        else:
            part = jnp.concatenate([high, right - high, high], 0)
        at = 24 * m
        factors[m, at : at + 24, :] = part
    moment = MOMENTUM * conv_m[...] + conv_g[0:9, :] * inverse
    conv_m_new[...] = moment
    conv_w_new[...] = conv_w[...] - FAST_RATE * moment

    slots = staged.shape[0]
    flying = [[] for _ in range(slots)]
    for i, (m, sources, outs, columns, rate, first, at) in enumerate(blocks):
        slot = i % slots
        wait_all(arriving[i])
        wait_all(flying[slot])
        rows = slice(at, at + size)
        merged = attn_ref[rows, :] if m < 2 else ffn_ref[at - attn_ref.shape[0] : at - attn_ref.shape[0] + size, :]
        approx = dot_nn(columns[first : first + size, :], factors[m].astype(bf16))
        fresh = MOMENTUM * loaded[i, 1] + approx
        staged[slot, 0] = loaded[i, 0] - rate * fresh
        staged[slot, 1] = fresh
        staged[slot, 2] = merged - approx
        pairs = [(staged.at[slot, j], outs[j].at[pl.ds(first, size), :]) for j in range(3)]
        flying[slot] = start_copies(pairs, sems, 3 * slot)
    for copies in flying:
        wait_all(copies)


def final_update(token, right, basis, columns, conv, attn_merged, ffn_merged, weights, count):
    width = right.shape[1]
    sizes = [w.shape[0] for w in weights[::2]]
    outs = [jax.ShapeDtypeStruct((size, width), f32) for size in sizes for _ in range(3)]
    conv_out = jax.ShapeDtypeStruct(conv[1].shape, f32)
    return pl.pallas_call(
        functools.partial(final_kernel, 1.0 / count),
        out_shape=(*outs, conv_out, conv_out),
        in_specs=[ANYWHERE] + [VMEM] * 8 + [pl.BlockSpec(memory_space=pltpu.HBM)] * 8,
        out_specs=(ANYWHERE,) * len(outs) + (VMEM,) * 2,
        scratch_shapes=[
            pltpu.VMEM((4, 128, width), f32),
            pltpu.VMEM((width, 128), bf16),
            pltpu.VMEM((4, 3, 192, width), f32),
            pltpu.VMEM((sum(sizes) // 192, 2, 192, width), f32),
            pltpu.SemaphoreType.DMA((12,)),
            pltpu.SemaphoreType.DMA((2 * sum(sizes) // 192,)),
        ],
        compiler_params=params(54),
        cost_estimate=cost(6 * width * width * 256, 50 << 20),
        name="final_update",
    )(token, right, basis, columns, *conv, attn_merged, ffn_merged, *weights)


def mod_kernel(
    inverse, slot_ref, silu_ref, own_ref, got_ref, conv_w, conv_m, w_ref, m_ref,
    conv_w_new, conv_m_new, w_new, m_new, rows, weights, moments, load_sems, sems,
):
    width = own_ref.shape[1]
    arriving = []
    for j in range(6):
        lanes = pl.ds(j * width, width)
        pairs = [(w_ref.at[:, lanes], weights.at[:, lanes]), (m_ref.at[:, lanes], moments.at[:, lanes])]
        arriving.append(start_copies(pairs, load_sems, 2 * j))
    count = own_ref.shape[0] - 16
    mine = pl.multiple_of(slot_ref[0] * count, 16)
    rows[pl.ds(mine, count), :] = own_ref[16 : 16 + count, :]
    rows[pl.ds(count - mine, count), :] = got_ref[16 : 16 + count, :]
    gradient = own_ref[0:16, :].astype(f32) + got_ref[0:16, :].astype(f32)
    moment = MOMENTUM * conv_m[...] + gradient[0:9, :] * inverse
    conv_m_new[...] = moment
    conv_w_new[...] = conv_w[...] - LEARN_RATE * moment
    shape = (silu_ref.shape[0], 2 * count)
    row = lax.broadcasted_iota(jnp.int32, shape, 0)
    col = lax.broadcasted_iota(jnp.int32, shape, 1)
    leaving = []
    for j in range(6):
        pick = jnp.where(col == 8 * row + j, 1.0, 0.0).astype(bf16)
        silu = dot_tn(silu_ref[...], pick).astype(bf16)
        mean = dot_nn(silu, rows[...]) * inverse
        wait_all(arriving[j])
        here = slice(j * width, (j + 1) * width)
        moment = MOMENTUM * moments[:, here] + mean
        moments[:, here] = moment
        weights[:, here] = weights[:, here] - LEARN_RATE * moment
        lanes = pl.ds(j * width, width)
        pairs = [(weights.at[:, lanes], w_new.at[:, lanes]), (moments.at[:, lanes], m_new.at[:, lanes])]
        leaving += start_copies(pairs, sems, 2 * j)
    wait_all(leaving)


def mod_update(slot, silu, own, got, w_mod, mom_mod, conv, mom_conv, count):
    width = own.shape[1]
    hbm = pl.BlockSpec(memory_space=pltpu.HBM)
    conv_new, mom_conv_new, w_new, mom_new = pl.pallas_call(
        functools.partial(mod_kernel, 1.0 / count),
        out_shape=(jax.ShapeDtypeStruct(conv.shape, f32),) * 2 + (jax.ShapeDtypeStruct(w_mod.shape, f32),) * 2,
        in_specs=[SMEM] + [VMEM] * 5 + [hbm] * 2,
        out_specs=(VMEM, VMEM, ANYWHERE, ANYWHERE),
        scratch_shapes=[
            pltpu.VMEM((2 * own.shape[0] - 32, width), bf16),
            pltpu.VMEM(w_mod.shape, f32),
            pltpu.VMEM(w_mod.shape, f32),
            pltpu.SemaphoreType.DMA((12,)),
            pltpu.SemaphoreType.DMA((12,)),
        ],
        compiler_params=params(54),
        cost_estimate=cost(100 * w_mod.size, 16 * w_mod.size),
        name="mod_update",
    )(slot, silu, own, got, conv, mom_conv, w_mod, mom_mod)
    return w_new, mom_new, conv_new, mom_conv_new


def leave_kernel(slot_ref, own_ref, got_ref, out_ref, grad_ref):
    mine = slot_ref[0]
    for i, target in enumerate((out_ref, grad_ref)):
        target[mine] = own_ref[i]
        target[1 - mine] = got_ref[i]


def leave(slot, own, got):
    return pl.pallas_call(
        leave_kernel,
        out_shape=(jax.ShapeDtypeStruct(own.shape, bf16),) * 2,
        in_specs=[SMEM, VMEM, VMEM],
        out_specs=(VMEM, VMEM),
        compiler_params=params(4),
        cost_estimate=cost(0, 8 * own.size),
        name="leave",
    )(slot, own, got)


def per_device(
    latents, conditions, cotangent, counts, w_mod, mom_mod, conv_attn, mom_conv_attn,
    w_qkv, mom_qkv, err_qkv, start_qkv, w_out, mom_out, err_out, start_out,
    w_fc1, mom_fc1, err_fc1, start_fc1, conv_ffn, mom_conv_ffn, w_fc2, mom_fc2, err_fc2, start_fc2,
):
    slots, share, width = latents.shape
    local = w_out.shape[0]
    rank = start_out.shape[1]
    mp_count = lax.axis_size("mp")
    dp_count = lax.axis_size("dp")
    mp = lax.axis_index("mp")
    dp = lax.axis_index("dp")
    chip, core = mp // 2, mp % 2

    def swap_chip(values):
        return lax.ppermute(values, "mp", [(i, i ^ 2) for i in range(mp_count)])

    def swap_core(values):
        return lax.ppermute(values, "mp", [(i, i ^ 1) for i in range(mp_count)])

    def swap_dp(values, bit):
        return lax.ppermute(values, "dp", [(i, i ^ bit) for i in range(dp_count)])

    bits = [1 << b for b in range(dp_count.bit_length() - 1)]

    def sum_dp(values, earlier):
        for bit in bits:
            low = lax.optimization_barrier(values.astype(bf16))
            if bit == bits[-1]:
                low = after(low, earlier)
            values = low.astype(f32) + swap_dp(low, bit).astype(f32)
        return values

    def after(values, earlier):
        return lax.optimization_barrier((values, earlier))[0]

    place = (dp ^ (dp >> 1)) & 1
    slot = jnp.reshape(chip, (1,)).astype(jnp.int32)
    idx = jnp.stack(
        [
            2 * chip + core, 2 * (1 - chip) + core, 2 * chip + 1 - core, 2 * (1 - chip) + 1 - core,
            core, place, dp & 3, chip, counts[0] > chip,
        ]
    ).astype(jnp.int32)

    w_qkv_t, mom_qkv_t, err_qkv_t = (
        jnp.swapaxes(a, -1, -2).reshape(3 * local, width) for a in (w_qkv, mom_qkv, err_qkv[0])
    )
    size = w_qkv_t.shape[0] // 4
    near_half = [
        lax.dynamic_slice_in_dim(w_qkv_t, (2 * place + i) * size, size, 0).astype(bf16) for i in range(2)
    ]
    qkv_near = [swap_chip(h) for h in near_half]

    size = w_fc1.shape[0] // 4
    ffn_q = jnp.concatenate(
        [lax.dynamic_slice_in_dim(w, (dp & 3) * size, size, 0).astype(bf16) for w in (w_fc1, w_fc2)], 0
    )
    ffn_near = swap_chip(ffn_q)

    silu_own = after(jax.nn.silu(conditions.astype(f32)).astype(bf16), ffn_q)
    silu_own = silu_own.reshape(slots, dp_count, -1).transpose(1, 0, 2)
    silu_all = lax.all_to_all(silu_own, "dp", split_axis=0, concat_axis=0, tiled=True)
    silu_slot = lax.dynamic_index_in_dim(silu_all, chip, 1, keepdims=False)

    sib_l = swap_core(latents)
    snd_l = lax.dynamic_index_in_dim(after(latents, silu_own), 1 - chip, 0, keepdims=False)
    got_l = swap_chip(snd_l)

    silu_slot = after(silu_slot, (qkv_near, snd_l))
    partial = modulation_part(silu_slot, w_mod, width)
    gathered = lax.all_to_all(partial, "dp", split_axis=0, concat_axis=0, tiled=True)
    out_a = after(w_out, partial).astype(bf16)
    starts_qkv = start_qkv.transpose(0, 2, 1).reshape(3 * rank, local)
    rows = [
        jnp.pad(conv_ffn, ((0, 16 - conv_ffn.shape[0]), (0, 0))),
        jnp.pad(starts_qkv, ((0, 32 - 3 * rank), (0, width - local))),
    ]
    parts = [out_a]
    for values in rows:
        high = lax.reduce_precision(values, 8, 7)
        parts += [high.astype(bf16), (values - high).astype(bf16)]
    out_b = swap_chip(jnp.concatenate(parts, 0))
    snd_c = lax.dynamic_index_in_dim(after(cotangent, out_a), 1 - chip, 0, keepdims=False)
    got_c = swap_chip(snd_c)
    sib_c = swap_core(after(cotangent, out_a))

    near = after(qkv_near, partial)
    qkv_b = near + [swap_dp(near[0], 1), swap_dp(near[1], 2)]
    ffn_near = after(ffn_near, partial)
    ffn_y, ffn_z = swap_dp(ffn_near, 1), swap_dp(ffn_near, 2)
    got_l = after(got_l, gathered)
    sib_got_l = swap_core(got_l)
    lat, conv_one = first_conv(idx, (latents, got_l, sib_l, sib_got_l), conv_attn)
    mod = jnp.sum(gathered, 0)
    wcat, conv_low, proj, att_t, lse, token = attn_forward(idx, conv_one, mod, conv_attn, w_qkv_t, qkv_b)
    att_sib = swap_core(att_t)
    ffn_y, ffn_z, out_b, got_c = after((ffn_y, ffn_z, out_b, got_c), token)
    ffn_pieces = (ffn_near, ffn_y, ffn_z, swap_dp(ffn_z[:size], 1), swap_dp(ffn_y[size:], 2))
    outs_sib = [swap_core(out_a), swap_core(out_b)]
    sib_got_c = swap_core(got_c)
    conv_ffn_b = (out_b[local : local + 16].astype(f32) + out_b[local + 16 : local + 32].astype(f32))[:9]
    starts_qkv_b = out_b[local + 32 : local + 64].astype(f32) + out_b[local + 64 : local + 96].astype(f32)
    starts_qkv_b = starts_qkv_b[: 3 * rank, :local]

    attn, mixed, mixed_t, fgl, cot = second_norm(
        idx, lat, att_t, att_sib, [out_a, out_b, *outs_sib], [cotangent, got_c, sib_c, sib_got_c], mod
    )
    w1_b, w2_b, act_b, hidden_b, snd_ffn, kgrad_b = ffn_first(idx, mixed, mixed_t, fgl, ffn_pieces, conv_ffn_b)
    got_ffn = swap_chip(snd_ffn)
    ffn_b, mix_b, snd_soon, snd_late, kgrad_c = ffn_second(
        mixed, mixed_t, fgl, w1_b, w2_b, act_b, hidden_b, conv_ffn_b
    )
    got_soon = swap_chip(snd_soon)
    ffn_part, mix_part, grad_ffn, kgrad_a = ffn_own(mixed, mixed_t, fgl, w_fc1, w_fc2, conv_ffn, (ffn_b, mix_b))
    mix_part, got_ffn, got_soon = lax.optimization_barrier((mix_part, got_ffn, got_soon))
    mix_got = swap_core(mix_part)
    got_late = swap_chip(after(snd_late, got_soon))
    conv_part, resid_grad, grad_attn, snd_attn, snd_k, snd_v, sums_two = attn_backward(
        lat, attn, cot, mix_part, mix_got, mod, conv_low, proj, att_t, lse, wcat, out_a, out_b
    )
    conv_got = swap_core(conv_part)
    ffn_got = swap_core(after(ffn_part, sums_two))

    part_attn, left_a, bulk = left_attn(
        grad_attn, snd_attn, snd_k, snd_v, got_late, kgrad_b, kgrad_c, err_qkv_t, err_out[0], starts_qkv, starts_qkv_b,
        start_out.T,
    )
    got_bulk = swap_chip(bulk)
    own_out, snd_out, kgrad_attn, mod_rows = tail(
        idx, lat, attn, ffn_part, ffn_got, conv_part, conv_got, cot, resid_grad, sums_two, mod, conv_attn
    )
    got_bulk = after(got_bulk, kgrad_attn)
    got_k = swap_chip(after(snd_k, got_bulk))
    got_v = None
    left_swap = got_bulk[2 * local :].astype(f32)
    merged_ffn, left_ffn = merge_ffn(
        grad_ffn, (got_ffn, got_soon, got_late), err_fc1[0], err_fc2[0], start_fc1.T, start_fc2.T
    )

    sums = jnp.concatenate(
        [left_a + left_swap[:16], left_ffn, kgrad_a + left_swap[16:], kgrad_attn], 0
    ).astype(bf16)
    mod_rows = mod_rows.astype(bf16)
    count = sums.shape[0]
    for bit in bits:
        sent = lax.optimization_barrier(jnp.concatenate([sums, mod_rows], 0))
        if bit == 2:
            sent, got_k = lax.optimization_barrier((sent, got_k))
            got_v = swap_chip(after(snd_v, got_k))
        if bit == 4:
            sent, got_v = lax.optimization_barrier((sent, got_v))
        got = swap_dp(sent, bit)
        total = sent[:count].astype(f32) + got[:count].astype(f32)
        sums = total.astype(bf16)
        mod_rows = jnp.concatenate([mod_rows, got[count:]], 0)

    basis, columns, rights, merged_attn = right_factors(
        total[:32], part_attn, (got_bulk, got_k, got_v), merged_ffn, dp_count
    )
    both = jnp.concatenate(after([sums[48:64], mod_rows], rights), 0)
    other = swap_chip(both)
    count = jnp.arange(dp_count)
    pick = ((dp ^ count)[:, None] == count[None, :]).astype(bf16)
    silu_order = jnp.dot(pick, silu_all.reshape(dp_count, -1)).reshape(silu_all.shape)
    silu_order = silu_order.transpose(1, 0, 2).reshape(dp_count * slots, -1)
    w_mod_new, mom_mod_new, conv_attn_new, mom_conv_attn_new = mod_update(
        slot, silu_order, both, other, w_mod, mom_mod, conv_attn, mom_conv_attn, dp_count
    )
    got_out = swap_chip(after(snd_out, conv_attn_new))
    right_sum = sum_dp(rights, conv_attn_new)
    (
        w_qkv_new, mom_qkv_new, err_qkv_new, w_out_new, mom_out_new, err_out_new,
        w_fc1_new, mom_fc1_new, err_fc1_new, w_fc2_new, mom_fc2_new, err_fc2_new,
        conv_ffn_new, mom_conv_ffn_new,
    ) = final_update(
        conv_attn_new, right_sum, basis, columns, (total[32:48], conv_ffn, mom_conv_ffn), merged_attn,
        merged_ffn, (w_qkv_t, mom_qkv_t, w_out, mom_out, w_fc1, mom_fc1, w_fc2, mom_fc2), dp_count,
    )
    w_qkv_new, mom_qkv_new, err_qkv_new = (
        jnp.swapaxes(a.reshape(3, local, width), -1, -2) for a in (w_qkv_new, mom_qkv_new, err_qkv_new)
    )

    latents_out, latents_grad = leave(slot, own_out, got_out)
    return (
        latents_out, latents_grad, w_mod_new, mom_mod_new, conv_attn_new, mom_conv_attn_new,
        w_qkv_new, mom_qkv_new, err_qkv_new[None], w_out_new, mom_out_new, err_out_new[None],
        w_fc1_new, mom_fc1_new, err_fc1_new[None], conv_ffn_new, mom_conv_ffn_new,
        w_fc2_new, mom_fc2_new, err_fc2_new[None],
    )


def solution(mesh):
    token = P("dp", "mp", None)
    rows = P("mp", None)
    columns = P(None, "mp")
    placed = (
        token, P("dp", None), token, P("dp"), P("dp", None), P("dp", None), P(), P(),
        P(None, None, "mp"), P(None, None, "mp"), P("dp", None, None, "mp"), P(None, "mp", None),
        rows, rows, P("dp", "mp", None), P(),
        columns, columns, P("dp", None, "mp"), rows,
        columns, columns,
        rows, rows, P("dp", "mp", None), P(),
    )
    results = (
        token, token, P("dp", None), P("dp", None), P(), P(),
        P(None, None, "mp"), P(None, None, "mp"), P("dp", None, None, "mp"),
        rows, rows, P("dp", "mp", None),
        columns, columns, P("dp", None, "mp"),
        columns, columns,
        rows, rows, P("dp", "mp", None),
    )
    return jax.shard_map(per_device, mesh=mesh, in_specs=placed, out_specs=results, check_vma=False)
```

```python
import functools

import jax
import jax.numpy as jnp
from jax import lax
from jax.experimental import pallas as pl
from jax.experimental.pallas import tpu as pltpu
from jax.sharding import PartitionSpec as P

HEAD_DIM = 64
SIDE = 32
HALF = SIDE // 2
PHASE = HALF * HALF
TOKENS = SIDE * SIDE
PADDED = PHASE + 2 * HALF
LANES = 256
ROWS = 64
CHEAP = 4
FINAL_MIB = 58
UNROLL = 4

NORM_EPS = 1e-06
ORTHO_EPS = 1e-06
LEARN_RATE = 0.005
FAST_RATE = 0.025
MOMENTUM = 0.9
GELU_C = 0.7978845608
GELU_A = 0.044715

f32 = jnp.float32
bf16 = jnp.bfloat16
VMEM = pl.BlockSpec(memory_space=pltpu.VMEM)
SMEM = pl.BlockSpec(memory_space=pltpu.SMEM)


def params(mib, **more):
    return pltpu.CompilerParams(vmem_limit_bytes=mib << 20, **more)


def cost(flops, nbytes, trans=0):
    return pl.CostEstimate(flops=flops // CHEAP, bytes_accessed=nbytes // CHEAP, transcendentals=trans)


def dot_nn(a, b):
    return lax.dot_general(a, b, (((1,), (0,)), ((), ())), preferred_element_type=f32)


def dot_nt(a, b):
    return lax.dot_general(a, b, (((1,), (1,)), ((), ())), preferred_element_type=f32)


def dot_tn(a, b):
    return lax.dot_general(a, b, (((0,), (0,)), ((), ())), preferred_element_type=f32)


def taps_of(a, b):
    rows = (((1, -1), (0, 0), (1, 0)) if a == 0 else ((0, 0), (1, 0), (0, 1)))
    cols = (((1, True), (0, False), (1, False)) if b == 0 else ((0, False), (1, False), (0, True)))
    return [
        (3 * i + j, 2 * rows[i][0] + cols[j][0], cols[j][1], rows[i][1])
        for i in range(3)
        for j in range(3)
    ]


TAPS = [taps_of(g // 2, g % 2) for g in range(4)]


def shift_columns(values, phase):
    place = lax.broadcasted_iota(jnp.int32, values.shape, 0)
    if phase % 2 == 1:
        return jnp.where(place == 0, 0.0, pltpu.roll(values, 1, 0))
    return jnp.where(place == HALF - 1, 0.0, pltpu.roll(values, HALF - 1, 0))


def zero_edges(*buffers):
    for buffer in buffers:
        lanes = buffer.shape[-1]
        for g in range(4):
            buffer[g, 0:HALF, :] = jnp.zeros((HALF, lanes), f32)
            buffer[g, HALF + PHASE : PADDED, :] = jnp.zeros((HALF, lanes), f32)


def tap_rows(plain, shifted, g, tap, row, lanes):
    _, phase, moved, step = TAPS[g][tap]
    buffer = shifted if moved else plain
    start = pl.multiple_of(HALF + (row + step) * HALF, HALF)
    return buffer[phase, pl.ds(start, HALF), lanes]


def spread_kernel(k_ref, lanes, flip):
    width = lanes.stop - lanes.start
    return [
        jnp.broadcast_to(k_ref[(8 - t if flip else t) : (8 - t if flip else t) + 1, lanes], (8, width))
        for t in range(9)
    ]


def conv_row(plain, shifted, spread, g, row, lanes):
    width = lanes.stop - lanes.start
    total = None
    for t in range(9):
        value = tap_rows(plain, shifted, g, t, row, lanes).reshape(2, 8, width)
        term = spread[t][None] * value
        total = term if total is None else total + term
    return total.reshape(HALF, width)


def kernel_sums(plain, shifted, grads, lanes):
    width = lanes.stop - lanes.start

    def body(row, sums):
        sums = list(sums)
        for g in range(4):
            start = pl.multiple_of(HALF + row * HALF, HALF)
            grad = grads[g, pl.ds(start, HALF), lanes].reshape(2, 8, width)
            for t in range(9):
                value = tap_rows(plain, shifted, g, t, row, lanes).reshape(2, 8, width)
                term = value * grad
                sums[t] = sums[t] + (term[0] + term[1])
        return tuple(sums)

    return lax.fori_loop(0, HALF, body, tuple(jnp.zeros((8, width), f32) for _ in range(9)), unroll=2)


def grid_permutation(inverse):
    size = 8 * SIDE
    token = lax.broadcasted_iota(jnp.int32, (size, size), 0 if inverse else 1)
    place = lax.broadcasted_iota(jnp.int32, (size, size), 1 if inverse else 0)
    r, c = token >> 5, token & 31
    target = ((r & 1) * 2 + (c & 1)) * 64 + (r >> 1) * HALF + (c >> 1)
    return jnp.where(target == place, 1.0, 0.0).astype(bf16)


ANYWHERE = pl.BlockSpec(memory_space=pl.ANY)
FREE = pl.CostEstimate(flops=1, bytes_accessed=1, transcendentals=0)


def start_copies(pairs, sems, first=0):
    copies = [pltpu.make_async_copy(src, dst, sems.at[first + i]) for i, (src, dst) in enumerate(pairs)]
    for copy in copies:
        copy.start()
    return copies


def wait_all(copies):
    for copy in copies:
        copy.wait()


def token_pieces(idx_ref, whole, got, sib_whole, sib_got, raw, sems, first=0):
    chip = idx_ref[7]
    return start_copies(
        [(whole.at[chip], raw.at[0]), (got, raw.at[1]), (sib_whole.at[chip], raw.at[2]), (sib_got, raw.at[3])],
        sems,
        first,
    )


def place_pieces(idx_ref, raw, target):
    perm = grid_permutation(False)
    for i in range(4):
        piece = dot_nn(perm, raw[i]).astype(bf16)
        for g in range(4):
            start = pl.multiple_of(g * PHASE + idx_ref[i] * 64, 64)
            target[pl.ds(start, 64), :] = piece[g * 64 : (g + 1) * 64, :]


def modulation_kernel(silu_ref, w_ref, out_ref):
    step = pl.program_id(0)
    part = dot_nn(silu_ref[...], w_ref[...].astype(bf16))
    for n in range(part.shape[0]):
        out_ref[n, pl.ds(step, 1), :] = part[n : n + 1, :]

    @pl.when(step == 0)
    def _():
        out_ref[:, 6:8, :] = jnp.zeros((part.shape[0], 2, part.shape[1]), f32)


def modulation_part(silu, w_mod, width):
    count = silu.shape[0]
    return pl.pallas_call(
        modulation_kernel,
        grid=(6,),
        out_shape=jax.ShapeDtypeStruct((count, 8, width), f32),
        in_specs=[
            pl.BlockSpec(silu.shape, lambda i: (0, 0)),
            pl.BlockSpec((w_mod.shape[0], width), lambda i: (0, i)),
        ],
        out_specs=pl.BlockSpec((count, 8, width), lambda i: (0, 0, 0)),
        compiler_params=params(8),
        cost_estimate=FREE,
        name="modulation_part",
    )(silu, w_mod)


def norm_rows(values):
    mean = jnp.mean(values, -1, keepdims=True)
    centred = values - mean
    variance = jnp.mean(centred * centred, -1, keepdims=True)
    scale = lax.rsqrt(variance + NORM_EPS)
    return centred * scale, scale


def fill_shifted(lat_ref, mod_ref, plain, shifted):
    if mod_ref is not None:
        gain = 1.0 + mod_ref[1:2, :]
        bias = mod_ref[0:1, :]
    for g in range(4):

        def body(j, carry):
            values = lat_ref[pl.ds(pl.multiple_of(g * PHASE + j * ROWS, ROWS), ROWS), :].astype(f32)
            result, _ = norm_rows(values)
            if mod_ref is not None:
                result = result * gain + bias
            start = pl.multiple_of(HALF + j * ROWS, HALF)
            plain[g, pl.ds(start, ROWS), :] = result
            for h in range(ROWS // HALF):
                part = result[h * HALF : (h + 1) * HALF]
                shifted[g, pl.ds(start + h * HALF, HALF), :] = shift_columns(part, g)
            return carry

        lax.fori_loop(0, PHASE // ROWS, body, 0, unroll=UNROLL)


def first_conv_kernel(idx_ref, own, got, sib, sib_got, k_ref, lat_ref, conv_ref, plain, shifted, raw, sems):
    copies = token_pieces(idx_ref, own, got, sib, sib_got, raw, sems)
    zero_edges(plain, shifted)
    wait_all(copies)
    place_pieces(idx_ref, raw, lat_ref)
    fill_shifted(lat_ref, None, plain, shifted)
    for first in range(0, conv_ref.shape[1], LANES):
        lanes = slice(first, first + LANES)
        spread = spread_kernel(k_ref, lanes, False)

        def body(row, carry):
            for g in range(4):
                start = pl.multiple_of(g * PHASE + row * HALF, HALF)
                conv_ref[pl.ds(start, HALF), lanes] = conv_row(plain, shifted, spread, g, row, lanes)
            return carry

        lax.fori_loop(0, HALF, body, 0, unroll=2)


def first_conv(idx, pieces, kernel):
    width = kernel.shape[1]
    return pl.pallas_call(
        first_conv_kernel,
        out_shape=(jax.ShapeDtypeStruct((TOKENS, width), bf16), jax.ShapeDtypeStruct((TOKENS, width), f32)),
        in_specs=[SMEM] + [ANYWHERE] * 4 + [VMEM],
        out_specs=(VMEM, VMEM),
        scratch_shapes=[pltpu.VMEM((4, PADDED, width), f32)] * 2
        + [pltpu.VMEM((4, TOKENS // 4, width), bf16), pltpu.SemaphoreType.DMA((4,))],
        compiler_params=params(14),
        cost_estimate=cost(30 * TOKENS * width, 8 * TOKENS * width),
        name="first_conv",
    )(idx, *pieces, kernel)


def modulate(conv_ref, mod_ref, k_ref, low_ref):
    gain = 1.0 + mod_ref[1:2, :]
    bias = mod_ref[0:1, :]
    taps = [k_ref[t : t + 1, :] for t in range(9)]
    width = conv_ref.shape[1]
    for g in range(4):
        a, b = g // 2, g % 2
        inner = [bias * (taps[j] + taps[3 + j] + taps[6 + j]) for j in range(3)]
        edge = [bias * (taps[3 + j] + (taps[6 + j] if a == 0 else taps[j])) for j in range(3)]
        side = 0 if b == 0 else 2
        place = lax.broadcasted_iota(jnp.int32, (HALF, width), 0)
        inside = place != (0 if b == 0 else HALF - 1)

        def body(row, carry):
            outer = row == (0 if a == 0 else HALF - 1)
            sums = [jnp.where(outer, e, i) for e, i in zip(edge, inner)]
            base = sums[1] + sums[2 - side]
            rows = pl.ds(pl.multiple_of(g * PHASE + row * HALF, HALF), HALF)
            value = conv_ref[rows, :] * gain + base + jnp.where(inside, sums[side], 0.0)
            low_ref[rows, :] = value.astype(bf16)
            return carry

        lax.fori_loop(0, HALF, body, 0, unroll=4)


def head_mask(shape, half):
    lane = lax.broadcasted_iota(jnp.int32, shape, 1)
    return (lane < HEAD_DIM) if half == 0 else (lane >= HEAD_DIM)


def attn_forward_kernel(
    idx_ref, conv_ref, mod_ref, k_ref, wa_ref, q0, q1, q2, q3,
    wcat, low_ref, proj_ref, att_t_ref, lse_ref, token_ref, wide, sems,
):
    token_ref[...] = jnp.zeros_like(token_ref)
    local = wa_ref.shape[0] // 3
    both = 2 * local
    step = local // 4
    place = idx_ref[5]
    pairs = []
    for index, quarter in ((2 * place, q0), (2 * place + 1, q1), (2 - 2 * place, q2), (3 - 2 * place, q3)):
        for j in range(3):
            chunk = 3 * index + j
            start = pl.multiple_of((chunk >> 2) * both + local + (chunk & 3) * step, 16)
            pairs.append((quarter.at[pl.ds(j * step, step), :], wcat.at[pl.ds(start, step), :]))
    copies = start_copies([(wa_ref, wide)] + pairs, sems)
    modulate(conv_ref, mod_ref, k_ref, low_ref)
    wait_all(copies)
    for t in range(3):
        wcat[t * both : t * both + local, :] = wide[t * local : (t + 1) * local, :].astype(bf16)

    def body(g, carry):
        rows = pl.ds(g * PHASE, PHASE)
        proj_ref[rows, :] = dot_nt(low_ref[rows, :], wcat[...]).astype(bf16)
        for pair in range(both // 128):
            q = proj_ref[rows, pair * 128 : (pair + 1) * 128] * jnp.asarray(HEAD_DIM**-0.5, bf16)
            k = proj_ref[rows, both + pair * 128 : both + (pair + 1) * 128]
            v = proj_ref[rows, 2 * both + pair * 128 : 2 * both + (pair + 1) * 128]
            v_t = v.T
            halves = range(2)
            scores = [dot_nt(k, jnp.where(head_mask(q.shape, h), q, jnp.zeros_like(q))) for h in halves]
            tops = [jnp.max(x, 0, keepdims=True) for x in scores]
            weights = [jnp.exp(x - top) for x, top in zip(scores, tops)]
            totals = [jnp.sum(x, 0, keepdims=True) for x in weights]
            for half in halves:
                head = 2 * pair + half
                lse_ref[g, head : head + 1, :] = tops[half] + jnp.log(totals[half])
                out_t = dot_nn(v_t[half * HEAD_DIM : (half + 1) * HEAD_DIM, :], weights[half].astype(bf16))
                out_t = out_t * (1.0 / totals[half])
                att_t_ref[g, head * HEAD_DIM : (head + 1) * HEAD_DIM, :] = out_t.astype(bf16)
        return carry

    for g in range(4):
        body(g, 0)


def attn_forward(idx, conv, mod, kernel, wa, quarters):
    rows, width = wa.shape
    both = 2 * rows // 3
    return pl.pallas_call(
        attn_forward_kernel,
        out_shape=(
            jax.ShapeDtypeStruct((2 * rows, width), bf16),
            jax.ShapeDtypeStruct((TOKENS, width), bf16),
            jax.ShapeDtypeStruct((TOKENS, 3 * both), bf16),
            jax.ShapeDtypeStruct((4, both, PHASE), bf16),
            jax.ShapeDtypeStruct((4, 8, PHASE), f32),
            jax.ShapeDtypeStruct((8, 128), f32),
        ),
        in_specs=[SMEM] + [VMEM] * 3 + [ANYWHERE] * 5,
        out_specs=(VMEM,) * 6,
        scratch_shapes=[pltpu.VMEM((rows, width), f32), pltpu.SemaphoreType.DMA((13,))],
        compiler_params=params(16),
        cost_estimate=cost(8 * TOKENS * both * width + 8 * TOKENS * PHASE * both, 12 << 20),
        name="attn_forward",
    )(idx, conv, mod, kernel, wa, *quarters)


def second_norm_kernel(
    idx_ref, lat_ref, own_ref, sib_ref, oa, ob, sa, sb, cot_own, cot_got, cot_sib, cot_sib_got, mod_ref,
    attn_ref, mixed, mixed_t, fgl, cot, wo, heads, raw, sems,
):
    local = oa.shape[0]
    core = idx_ref[4]
    mine = pl.multiple_of(core * 2 * local, local)
    theirs = pl.multiple_of((1 - core) * 2 * local, local)
    weights = start_copies(
        [
            (oa, wo.at[pl.ds(mine, local), :]),
            (ob.at[pl.ds(0, local), :], wo.at[pl.ds(mine + local, local), :]),
            (sa, wo.at[pl.ds(theirs, local), :]),
            (sb.at[pl.ds(0, local), :], wo.at[pl.ds(theirs + local, local), :]),
        ]
        + [(sib_ref.at[g], heads.at[g, pl.ds(theirs, 2 * local), :]) for g in range(4)],
        sems,
    )
    tokens = token_pieces(idx_ref, cot_own, cot_got, cot_sib, cot_sib_got, raw, sems, 8)
    for g in range(4):
        heads[g, pl.ds(mine, 2 * local), :] = own_ref[g]
    wait_all(weights)
    for g in range(4):
        attn_ref[g * PHASE : (g + 1) * PHASE, :] = dot_tn(heads[g], wo[...]).astype(bf16)
    wait_all(tokens)
    place_pieces(idx_ref, raw, cot)
    gate_one = mod_ref[2:3, :]
    bias = mod_ref[3:4, :]
    gain = 1.0 + mod_ref[4:5, :]
    gate_two = mod_ref[5:6, :]
    live = idx_ref[8].astype(f32)

    def body(j, carry):
        rows = pl.ds(pl.multiple_of(j * ROWS, ROWS), ROWS)
        resid = lat_ref[rows, :].astype(f32) + gate_one * attn_ref[rows, :].astype(f32)
        normed, _ = norm_rows(resid)
        mixed[rows, :] = (normed * gain + bias).astype(bf16)
        grad = live * cot[rows, :].astype(f32)
        cot[rows, :] = grad.astype(bf16)
        fgl[rows, :] = (gate_two * grad).astype(bf16)
        return carry

    lax.fori_loop(0, TOKENS // ROWS, body, 0, unroll=UNROLL)
    mixed_t[...] = mixed[...].T


def second_norm(idx, lat, own, sib, outs, cots, mod):
    width = lat.shape[1]
    whole = jax.ShapeDtypeStruct((TOKENS, width), bf16)
    return pl.pallas_call(
        second_norm_kernel,
        out_shape=(whole, whole, jax.ShapeDtypeStruct((width, TOKENS), bf16), whole, whole),
        in_specs=[SMEM] + [VMEM] * 2 + [ANYWHERE] * 9 + [VMEM],
        out_specs=(VMEM,) * 5,
        scratch_shapes=[
            pltpu.VMEM((width, width), bf16),
            pltpu.VMEM((4, width, PHASE), bf16),
            pltpu.VMEM((4, TOKENS // 4, width), bf16),
            pltpu.SemaphoreType.DMA((12,)),
        ],
        compiler_params=params(16),
        cost_estimate=cost(2 * TOKENS * width * width, 16 * TOKENS * width),
        name="second_norm",
    )(idx, lat, own, sib, *outs, *cots, mod)


def ffn_tile(at, lanes, mixed, mixed_t, fgl, w1, w2, k_ref, buffers, act, hidden_grad, kg_ref):
    plain, shifted, grad, grad_shifted = buffers
    here = slice(0, LANES)
    there = slice(at, at + LANES)
    for g in range(4):
        rows = slice(g * PHASE, (g + 1) * PHASE)
        plain[g, HALF : HALF + PHASE, :] = dot_nn(mixed[rows, :], w1[:, lanes])
        grad[g, HALF : HALF + PHASE, :] = dot_nt(fgl[rows, :], w2[lanes, :])

    def shift_body(row, carry):
        rows = pl.ds(pl.multiple_of(HALF + row * HALF, HALF), HALF)
        for g in range(4):
            shifted[g, rows, :] = shift_columns(plain[g, rows, :], g)
        return carry

    lax.fori_loop(0, HALF, shift_body, 0, unroll=4)
    spread = [
        jnp.broadcast_to(k_ref[t : t + 1, lanes], (8, LANES)) for t in range(9)
    ]

    def act_body(row, carry):
        padded = pl.ds(pl.multiple_of(HALF + row * HALF, HALF), HALF)
        for g in range(4):
            pre = conv_row(plain, shifted, spread, g, row, here)
            square = pre * pre
            tanh = jnp.tanh(pre * (GELU_C + (GELU_C * GELU_A) * square))
            half = 0.5 + 0.5 * tanh
            rows = pl.ds(pl.multiple_of(g * PHASE + row * HALF, HALF), HALF)
            act[rows, there] = (pre * half).astype(bf16)
            slope = half + (0.5 * pre) * (1.0 - tanh * tanh) * (
                GELU_C + (3.0 * GELU_C * GELU_A) * square
            )
            result = grad[g, padded, :] * slope
            grad[g, padded, :] = result
            grad_shifted[g, padded, :] = shift_columns(result, g)
        return carry

    lax.fori_loop(0, HALF, act_body, 0, unroll=2)
    flipped = spread[::-1]

    def back_body(row, carry):
        for g in range(4):
            rows = pl.ds(pl.multiple_of(g * PHASE + row * HALF, HALF), HALF)
            hidden_grad[rows, there] = conv_row(grad, grad_shifted, flipped, g, row, here).astype(bf16)
        return carry

    lax.fori_loop(0, HALF, back_body, 0, unroll=2)
    sums = kernel_sums(plain, shifted, grad, here)
    for t in range(9):
        kg_ref[t : t + 1, there] = jnp.sum(sums[t], 0, keepdims=True)
    second = dot_tn(act[:, there], fgl[...])
    one = dot_nn(mixed_t[...], hidden_grad[:, there])
    return one, second


def fold_rows(one):
    return jnp.concatenate([one[i : i + LANES, :] for i in range(0, one.shape[0], LANES)], 1)


def ffn_first_kernel(
    idx_ref, mixed, mixed_t, fgl, near, far_y, far_z, diag_one, diag_two, k_ref,
    w1, w2, act, hidden_grad, send_ref, kg_ref, *rest,
):
    buffers, sems = rest[:4], rest[4]
    size = diag_one.shape[0]
    quarter = idx_ref[6]
    pairs = []
    for index, one, two in (
        (quarter, near.at[pl.ds(0, size), :], near.at[pl.ds(size, size), :]),
        (quarter ^ 1, far_y.at[pl.ds(0, size), :], far_y.at[pl.ds(size, size), :]),
        (quarter ^ 2, far_z.at[pl.ds(0, size), :], far_z.at[pl.ds(size, size), :]),
        (quarter ^ 3, diag_one, diag_two),
    ):
        rows = pl.ds(pl.multiple_of(index * size, 64), size)
        pairs += [(one, w1.at[rows, :]), (two, w2.at[rows, :])]
    copies = start_copies(pairs, sems)
    zero_edges(*buffers)
    kg_ref[9:16, :] = jnp.zeros((7, kg_ref.shape[1]), f32)
    wait_all(copies)
    one, second = ffn_tile(
        0, slice(0, LANES), mixed, mixed_t, fgl, w1, w2, k_ref, buffers, act, hidden_grad, kg_ref
    )
    send_ref[0:LANES, :] = second.astype(bf16)
    send_ref[LANES : 2 * LANES, :] = fold_rows(one).astype(bf16)


def ffn_scratch():
    return [pltpu.VMEM((4, PADDED, LANES), f32)] * 4


def ffn_first(idx, mixed, mixed_t, fgl, pieces, kernel):
    width, units = mixed.shape[1], kernel.shape[1]
    tile = jax.ShapeDtypeStruct((TOKENS, LANES), bf16)
    return pl.pallas_call(
        ffn_first_kernel,
        out_shape=(
            jax.ShapeDtypeStruct((width, units), bf16),
            jax.ShapeDtypeStruct((units, width), bf16),
            tile,
            tile,
            jax.ShapeDtypeStruct((2 * LANES, width), bf16),
            jax.ShapeDtypeStruct((16, LANES), f32),
        ),
        in_specs=[SMEM] + [VMEM] * 3 + [ANYWHERE] * 5 + [VMEM],
        out_specs=(VMEM,) * 6,
        scratch_shapes=ffn_scratch() + [pltpu.SemaphoreType.DMA((8,))],
        compiler_params=params(12),
        cost_estimate=FREE,
        name="ffn_first",
    )(idx, mixed, mixed_t, fgl, *pieces, kernel)


def ffn_sums(act, hidden_grad, w1, w2, ffn_out, mix_out, before=None):
    for g in range(4):
        rows = slice(g * PHASE, (g + 1) * PHASE)
        ffn_part = dot_nn(act[rows, :], w2[...])
        mix_part = dot_nt(hidden_grad[rows, :], w1[...])
        if before is not None:
            ffn_part = ffn_part + before[0][rows, :].astype(f32)
            mix_part = mix_part + before[1][rows, :].astype(f32)
        ffn_out[rows, :] = ffn_part.astype(bf16)
        mix_out[rows, :] = mix_part.astype(bf16)


def ffn_second_kernel(
    mixed, mixed_t, fgl, w1, w2, act_in, hidden_in, k_ref,
    ffn_out, mix_out, send_ref, late_ref, kg_ref, *rest,
):
    buffers, act, hidden_grad = rest[:4], rest[4], rest[5]
    zero_edges(*buffers)
    kg_ref[9:16, :] = jnp.zeros((7, kg_ref.shape[1]), f32)
    act[:, 0:LANES] = act_in[...]
    hidden_grad[:, 0:LANES] = hidden_in[...]
    soon = send_ref.shape[0] - LANES
    at = 0
    for first in range(LANES, w1.shape[1], LANES):
        lanes = slice(first, first + LANES)
        one, second = ffn_tile(
            first, lanes, mixed, mixed_t, fgl, w1, w2, k_ref, buffers, act, hidden_grad, kg_ref
        )
        folded = fold_rows(one).astype(bf16)
        if first == LANES:
            send_ref[0:LANES, :] = second.astype(bf16)
            send_ref[LANES : LANES + soon, :] = folded[0:soon, :]
            at = LANES - soon
            late_ref[0:at, :] = folded[soon:LANES, :]
        else:
            late_ref[at : at + LANES, :] = second.astype(bf16)
            late_ref[at + LANES : at + 2 * LANES, :] = folded
            at += 2 * LANES
    ffn_sums(act, hidden_grad, w1, w2, ffn_out, mix_out)


def ffn_second(mixed, mixed_t, fgl, w1, w2, act, hidden_grad, kernel):
    width, units = mixed.shape[1], kernel.shape[1]
    rows = 2 * (units - LANES)
    soon = LANES + LANES // 2
    whole = jax.ShapeDtypeStruct((TOKENS, width), bf16)
    return pl.pallas_call(
        ffn_second_kernel,
        out_shape=(
            whole,
            whole,
            jax.ShapeDtypeStruct((soon, width), bf16),
            jax.ShapeDtypeStruct((rows - soon, width), bf16),
            jax.ShapeDtypeStruct((16, units), f32),
        ),
        in_specs=[VMEM] * 8,
        out_specs=(VMEM,) * 5,
        scratch_shapes=ffn_scratch() + [pltpu.VMEM((TOKENS, units), bf16)] * 2,
        compiler_params=params(16),
        cost_estimate=FREE,
        name="ffn_second",
    )(mixed, mixed_t, fgl, w1, w2, act, hidden_grad, kernel)


def ffn_own_kernel(
    mixed, mixed_t, fgl, w1_ref, w2_ref, k_ref, ffn_in, mix_in, ffn_out, mix_out, grads_ref, kg_ref, *rest,
):
    buffers, act, hidden_grad, w1, w2 = rest[:4], rest[4], rest[5], rest[6], rest[7]
    width = mixed.shape[1]
    w1[...] = w1_ref[...].astype(bf16)
    w2[...] = w2_ref[...].astype(bf16)
    zero_edges(*buffers)
    kg_ref[9:16, :] = jnp.zeros((7, kg_ref.shape[1]), f32)
    for first in range(0, w1.shape[1], LANES):
        lanes = slice(first, first + LANES)
        one, second = ffn_tile(
            first, lanes, mixed, mixed_t, fgl, w1, w2, k_ref, buffers, act, hidden_grad, kg_ref
        )
        grads_ref[0:width, lanes] = one
        grads_ref[width + first : width + first + LANES, :] = second
    ffn_sums(act, hidden_grad, w1, w2, ffn_out, mix_out, (ffn_in, mix_in))


def ffn_own(mixed, mixed_t, fgl, w1, w2, kernel, before):
    width, units = w1.shape
    whole = jax.ShapeDtypeStruct((TOKENS, width), bf16)
    return pl.pallas_call(
        ffn_own_kernel,
        out_shape=(
            whole,
            whole,
            jax.ShapeDtypeStruct((width + units, width), f32),
            jax.ShapeDtypeStruct((16, units), f32),
        ),
        in_specs=[VMEM] * 8,
        out_specs=(VMEM,) * 4,
        scratch_shapes=ffn_scratch()
        + [pltpu.VMEM((TOKENS, units), bf16)] * 2
        + [pltpu.VMEM((width, units), bf16), pltpu.VMEM((units, width), bf16)],
        compiler_params=params(20),
        cost_estimate=FREE,
        name="ffn_own",
    )(mixed, mixed_t, fgl, w1, w2, kernel, *before)


def attn_backward_kernel(
    lat_ref, attn_ref, cot_ref, mo_ref, mr_ref, mod_ref, conv_ref, proj_ref, att_t_ref, lse_ref, wcat, oa, ob,
    part_ref, resid_ref, mine_ref, send_ref, send_k_ref, send_v_ref, sums_ref,
    low, proj_t, grads, sums, wo,
):
    both = wcat.shape[0] // 3
    local = both // 2
    width = wcat.shape[1]
    wo[0:local, :] = oa[...]
    wo[local:both, :] = ob[0:local, :]
    sums[...] = jnp.zeros_like(sums)
    gate_one = mod_ref[2:3, :]
    gain = 1.0 + mod_ref[4:5, :]

    def fold(values):
        return jnp.sum(values.reshape(ROWS // 8, 8, width), 0)

    def norm_body(j, carry):
        rows = pl.ds(pl.multiple_of(j * ROWS, ROWS), ROWS)
        attn = attn_ref[rows, :].astype(f32)
        resid = lat_ref[rows, :].astype(f32) + gate_one * attn
        normed, scale = norm_rows(resid)
        mixed = mo_ref[rows, :].astype(f32) + mr_ref[rows, :].astype(f32)
        u = mixed * gain
        mean_u = jnp.mean(u, -1, keepdims=True)
        mean_un = jnp.mean(u * normed, -1, keepdims=True)
        grad = cot_ref[rows, :].astype(f32) + scale * (u - mean_u - normed * mean_un)
        resid_ref[rows, :] = grad
        low[rows, :] = (gate_one * grad).astype(bf16)
        sums[0] += fold(attn * grad)
        sums[1] += fold(mixed)
        sums[2] += fold(mixed * normed)
        return carry

    lax.fori_loop(0, TOKENS // ROWS, norm_body, 0, unroll=UNROLL)
    for t in range(3):
        sums_ref[t : t + 1, :] = jnp.sum(sums[t], 0, keepdims=True)
    sums_ref[3:8, :] = jnp.zeros((5, width), f32)
    scale = HEAD_DIM**-0.5

    def body(g, carry):
        rows = pl.ds(g * PHASE, PHASE)
        d_att = dot_nt(low[rows, :], wo[...]).astype(bf16)
        d_att_t = dot_nt(wo[...], low[rows, :]).astype(bf16)
        for pair in range(both // 128):
            q = proj_ref[rows, pair * 128 : (pair + 1) * 128] * jnp.asarray(scale, bf16)
            k = proj_ref[rows, both + pair * 128 : both + (pair + 1) * 128]
            v = proj_ref[rows, 2 * both + pair * 128 : 2 * both + (pair + 1) * 128]
            d_out = d_att[:, pair * 128 : (pair + 1) * 128]
            q_t = q.T
            k_t = k.T
            halves = range(2)
            masks = [head_mask(q.shape, h) for h in halves]
            scores = [dot_nt(k, jnp.where(mask, q, jnp.zeros_like(q))) for mask in masks]
            prob_grads = [dot_nt(v, jnp.where(mask, d_out, jnp.zeros_like(d_out))) for mask in masks]
            probs = [jnp.exp(scores[h] - lse_ref[g, 2 * pair + h : 2 * pair + h + 1, :]) for h in halves]
            means = [jnp.sum(probs[h] * prob_grads[h], 0, keepdims=True) for h in halves]
            score_grads = [(probs[h] * (prob_grads[h] - means[h])).astype(bf16) for h in halves]
            for half in halves:
                own = slice(half * HEAD_DIM, (half + 1) * HEAD_DIM)
                at = (2 * pair + half) * HEAD_DIM
                d_head = d_att_t[at : at + HEAD_DIM, :]
                score_grad, low_probs = score_grads[half], probs[half].astype(bf16)
                proj_t[g, at : at + HEAD_DIM, :] = (dot_nn(k_t[own, :], score_grad) * scale).astype(bf16)
                proj_t[g, both + at : both + at + HEAD_DIM, :] = dot_nt(q_t[own, :], score_grad).astype(bf16)
                proj_t[g, 2 * both + at : 2 * both + at + HEAD_DIM, :] = dot_nt(d_head, low_probs).astype(bf16)
        part_ref[rows, :] = dot_tn(proj_t[g], wcat[...]).astype(bf16)
        return carry

    for g in range(4):
        body(g, 0)

    def total(rows_of, other):
        result = None
        for g in range(4):
            term = dot_nn(rows_of(g), other[g * PHASE : (g + 1) * PHASE, :])
            result = term if result is None else result + term
        return result

    for t in range(4):
        for side in range(2):
            if t < 3:
                first = t * both + side * local
                value = total(lambda g: proj_t[g, first : first + local, :], conv_ref)
            else:
                value = total(lambda g: att_t_ref[g, side * local : (side + 1) * local, :], low)
            if side == 0:
                mine_ref[t * local : (t + 1) * local, :] = value
            else:
                target, at = ((send_ref, local), (send_k_ref, 0), (send_v_ref, 0), (send_ref, 0))[t]
                target[at : at + local, :] = value.astype(bf16)


def attn_backward(lat, attn, cot, mix_own, mix_got, mod, conv_low, proj, att_t, lse, wcat, out_a, out_b):
    both = wcat.shape[0] // 3
    width = lat.shape[1]
    return pl.pallas_call(
        attn_backward_kernel,
        out_shape=(
            jax.ShapeDtypeStruct((TOKENS, width), bf16),
            jax.ShapeDtypeStruct((TOKENS, width), f32),
            jax.ShapeDtypeStruct((2 * both, width), f32),
            jax.ShapeDtypeStruct((both, width), bf16),
            jax.ShapeDtypeStruct((both // 2, width), bf16),
            jax.ShapeDtypeStruct((both // 2, width), bf16),
            jax.ShapeDtypeStruct((8, width), f32),
        ),
        in_specs=[VMEM] * 13,
        out_specs=(VMEM,) * 7,
        scratch_shapes=[
            pltpu.VMEM((TOKENS, width), bf16),
            pltpu.VMEM((4, 3 * both, PHASE), bf16),
            pltpu.VMEM((8, 128), f32),
            pltpu.VMEM((3, 8, width), f32),
            pltpu.VMEM((both, width), bf16),
        ],
        compiler_params=params(20),
        cost_estimate=pl.CostEstimate(flops=1, bytes_accessed=1, transcendentals=0),
        name="attn_backward",
    )(lat, attn, cot, mix_own, mix_got, mod, conv_low, proj, att_t, lse, wcat, out_a, out_b)


def tail_kernel(
    idx_ref, lat_ref, attn_ref, fo_ref, fr_ref, co_ref, cr_ref, cot_ref, resid_ref, two_ref, mod_ref, k_ref,
    own_ref, send_ref, kg_ref, rows_ref,
    plain, shifted, grad, grad_shifted, out_low, sums,
):
    width = lat_ref.shape[1]
    zero_edges(plain, shifted, grad, grad_shifted)
    fill_shifted(lat_ref, mod_ref, plain, shifted)
    def grad_body(row, carry):
        padded = pl.ds(pl.multiple_of(HALF + row * HALF, HALF), HALF)
        for g in range(4):
            rows = pl.ds(pl.multiple_of(g * PHASE + row * HALF, HALF), HALF)
            values = co_ref[rows, :].astype(f32) + cr_ref[rows, :].astype(f32)
            grad[g, padded, :] = values
            grad_shifted[g, padded, :] = shift_columns(values, g)
        return carry

    lax.fori_loop(0, HALF, grad_body, 0, unroll=2)
    for first in range(0, width, LANES):
        lanes = slice(first, first + LANES)
        totals = kernel_sums(plain, shifted, grad, lanes)
        for t in range(9):
            kg_ref[t : t + 1, lanes] = jnp.sum(totals[t], 0, keepdims=True)
    for first in range(0, width, LANES):
        lanes = slice(first, first + LANES)
        flipped = spread_kernel(k_ref, lanes, True)

        def back_body(row, carry):
            padded = pl.ds(pl.multiple_of(HALF + row * HALF, HALF), HALF)
            for g in range(4):
                plain[g, padded, lanes] = conv_row(grad, grad_shifted, flipped, g, row, lanes)
            return carry

        lax.fori_loop(0, HALF, back_body, 0, unroll=2)
    sums[...] = jnp.zeros_like(sums)
    gate_one = mod_ref[2:3, :]
    gate_two = mod_ref[5:6, :]
    live = idx_ref[8].astype(f32)
    gain = 1.0 + mod_ref[1:2, :]

    def fold(values):
        return jnp.sum(values.reshape(ROWS // 8, 8, width), 0)

    for g in range(4):

        def body(j, carry):
            rows = pl.ds(pl.multiple_of(g * PHASE + j * ROWS, ROWS), ROWS)
            latent = lat_ref[rows, :].astype(f32)
            attn = attn_ref[rows, :].astype(f32)
            ffn_out = fo_ref[rows, :].astype(f32) + fr_ref[rows, :].astype(f32)
            out = live * (latent + gate_one * attn + gate_two * ffn_out)
            out_low[0, rows, :] = out.astype(bf16)
            sums[2] += fold(ffn_out * cot_ref[rows, :].astype(f32))
            normed, scale = norm_rows(latent)
            back = plain[g, pl.ds(pl.multiple_of(HALF + j * ROWS, HALF), ROWS), :]
            u = back * gain
            mean_u = jnp.mean(u, -1, keepdims=True)
            mean_un = jnp.mean(u * normed, -1, keepdims=True)
            result = resid_ref[rows, :] + scale * (u - mean_u - normed * mean_un)
            out_low[1, rows, :] = result.astype(bf16)
            sums[0] += fold(back)
            sums[1] += fold(back * normed)
            return carry

        lax.fori_loop(0, PHASE // ROWS, body, 0, unroll=UNROLL)
    for t, row in enumerate((0, 1, 5)):
        rows_ref[row : row + 1, :] = jnp.sum(sums[t], 0, keepdims=True)
    rows_ref[2:5, :] = two_ref[0:3, :]
    rows_ref[6:8, :] = jnp.zeros((2, width), f32)
    kg_ref[9:16, :] = jnp.zeros((7, width), f32)
    perm = grid_permutation(True)
    for i, target in ((0, own_ref), (1, send_ref)):
        block = idx_ref[i]
        for which in range(2):
            values = jnp.concatenate(
                [
                    out_low[which, pl.ds(pl.multiple_of(g * PHASE + block * 64, 64), 64), :]
                    for g in range(4)
                ],
                0,
            )
            target[which] = dot_nn(perm, values).astype(bf16)


def tail(midx, lat, attn, ffn_own, ffn_got, conv_own, conv_got, cot, resid, two, mod, kernel):
    width = lat.shape[1]
    share = jax.ShapeDtypeStruct((2, TOKENS // 4, width), bf16)
    padded = pltpu.VMEM((4, PADDED, width), f32)
    return pl.pallas_call(
        tail_kernel,
        out_shape=(
            share,
            share,
            jax.ShapeDtypeStruct((16, width), f32),
            jax.ShapeDtypeStruct((8, width), f32),
        ),
        in_specs=[SMEM] + [VMEM] * 11,
        out_specs=(VMEM,) * 4,
        scratch_shapes=[padded] * 4 + [pltpu.VMEM((2, TOKENS, width), bf16), pltpu.VMEM((3, 8, width), f32)],
        compiler_params=params(30),
        cost_estimate=pl.CostEstimate(flops=1, bytes_accessed=1, transcendentals=0),
        name="tail",
    )(midx, lat, attn, ffn_own, ffn_got, conv_own, conv_got, cot, resid, two, mod, kernel)


def split_rows(values):
    high = values.astype(bf16).astype(f32)
    return jnp.concatenate([high, values - high], 0).astype(bf16)


def thin(product, rows, matrix):
    both = split_rows(rows)
    if matrix.dtype == bf16:
        result = product(both, matrix)
        return result[0:8] + result[8:16]
    high = matrix.astype(bf16)
    low = (matrix - high.astype(f32)).astype(bf16)
    first, second = product(both, high), product(both, low)
    return (first[0:8] + first[8:16]) + (second[0:8] + second[8:16])


def merge_ffn_kernel(
    grads_ref, piece_ref, soon_ref, late_ref, err1_ref, err2_ref, start1_ref, start2_ref, merged_ref, left_ref
):
    width = err1_ref.shape[0]
    pieces = [piece_ref, soon_ref, late_ref]
    edges = [0, piece_ref.shape[0], piece_ref.shape[0] + soon_ref.shape[0], 2 * width]

    def got(first, count, lanes):
        parts = []
        for ref, low, high in zip(pieces, edges[:-1], edges[1:]):
            begin, end = max(first, low), min(first + count, high)
            if begin < end:
                parts.append(ref[begin - low : end - low, lanes])
        return (parts[0] if len(parts) == 1 else jnp.concatenate(parts, 0)).astype(f32)

    for block, first in enumerate(range(0, width, LANES)):
        rows = slice(first, first + LANES)
        folded = [got(2 * LANES * t + LANES, LANES, rows) for t in range(width // LANES)]
        one = grads_ref[rows, :] + jnp.concatenate(folded, 1) + err1_ref[rows, :]
        merged_ref[rows, :] = one
        left_ref[0:8, rows] = thin(dot_nt, start1_ref[...], one)
        below = slice(width + first, width + first + LANES)
        second = got(2 * LANES * block, LANES, slice(0, width))
        two = grads_ref[below, :] + second + err2_ref[rows, :]
        merged_ref[below, :] = two
        left_ref[8:16, rows] = thin(dot_nt, start2_ref[...], two)


def merge_ffn(grads, pieces, err1, err2, start1, start2):
    width = err1.shape[0]
    return pl.pallas_call(
        merge_ffn_kernel,
        out_shape=(
            jax.ShapeDtypeStruct(grads.shape, f32),
            jax.ShapeDtypeStruct((16, width), f32),
        ),
        in_specs=[VMEM] * 8,
        out_specs=(VMEM,) * 2,
        compiler_params=params(10),
        cost_estimate=FREE,
        name="merge_ffn",
    )(grads, *pieces, err1, err2, start1, start2)


def left_attn_kernel(
    mine_ref, send_ref, send_k_ref, send_v_ref, _, kg_one, kg_two, err_ref, err_out_ref, start_ref, start_b_ref, start_out_ref,
    merged_ref, left_ref, bulk_ref,
):
    local = err_out_ref.shape[0]
    width = mine_ref.shape[1]
    left, left_b = None, None
    for t in range(3):
        rows = slice(t * local, (t + 1) * local)
        start, start_b = start_ref[8 * t : 8 * t + 8, :], start_b_ref[8 * t : 8 * t + 8, :]
        total = mine_ref[rows, :] + err_ref[rows, :]
        merged_ref[rows, :] = total
        term = thin(dot_nn, start, total)
        other = (send_ref[local : 2 * local, :], send_k_ref[...], send_v_ref[...])[t]
        term_b = thin(dot_nn, start_b, other)
        left = term if left is None else left + term
        left_b = term_b if left_b is None else left_b + term_b
    rows = slice(3 * local, 4 * local)
    total = mine_ref[rows, :] + err_out_ref[...]
    merged_ref[rows, :] = total
    left_ref[0:8, :] = left
    left_ref[8:16, :] = jnp.zeros((8, width), f32)
    left_ref[8:16, 0:local] = thin(dot_nt, start_out_ref[...], total)
    left_out = thin(dot_nt, start_out_ref[...], send_ref[0:local, :])
    left_out = jnp.concatenate([left_out, jnp.zeros((8, width - local), f32)], 1)
    size = 2 * local
    tile = kg_one.shape[1]
    bulk_ref[0:size, :] = send_ref[...]
    bulk_ref[size : size + 16, :] = jnp.concatenate([left_b, left_out], 0).astype(bf16)
    bulk_ref[size + 16 : size + 32, 0:tile] = kg_one[...].astype(bf16)
    bulk_ref[size + 16 : size + 32, tile:width] = kg_two[:, tile:width].astype(bf16)


def left_attn(mine, send, send_k, send_v, late, kg_one, kg_two, err_qkv, err_out, start, start_b, start_out):
    width = mine.shape[1]
    piece = jax.ShapeDtypeStruct((16, width), f32)
    return pl.pallas_call(
        left_attn_kernel,
        out_shape=(
            jax.ShapeDtypeStruct(mine.shape, f32),
            piece,
            jax.ShapeDtypeStruct((send.shape[0] + 32, width), bf16),
        ),
        in_specs=[VMEM] * 4 + [ANYWHERE] + [VMEM] * 7,
        out_specs=(VMEM,) * 3,
        compiler_params=params(12),
        cost_estimate=cost(mine.size * 64, mine.size * 12),
        name="left_attn",
    )(mine, send, send_k, send_v, late, kg_one, kg_two, err_qkv, err_out, start, start_b, start_out)


def orthonormal(factor):
    place = lax.broadcasted_iota(jnp.int32, (8, 1), 0)
    for k in range(8):
        products = jnp.sum(factor * factor[k : k + 1, :], -1, keepdims=True)
        scale = lax.rsqrt(products[k : k + 1, :] + ORTHO_EPS)
        column = factor[k : k + 1, :] * scale
        weight = jnp.where(place > k, products * scale, 0.0)
        factor = jnp.where(place == k, column, factor - weight * column)
    return factor


def right_kernel(inverse, left_ref, part_ref, got_ref, got_k, got_v, ffn_ref, basis_ref, columns_ref, right_ref, merged_ref):
    local = part_ref.shape[0] // 4
    width = part_ref.shape[1]
    basis = [orthonormal(left_ref[8 * m : 8 * m + 8, :] * inverse) for m in range(4)]
    stack = []
    for m in range(4):
        high = basis[m].astype(bf16).astype(f32)
        stack += [high, high, basis[m] - high]
    stack.append(jnp.zeros((32, width), f32))
    columns_ref[...] = jnp.concatenate(stack, 0).T.astype(bf16)
    basis_ref[...] = basis[0]
    for t, got in enumerate((got_ref[local : 2 * local, :], got_k[...], got_v[...])):
        rows = slice(t * local, (t + 1) * local)
        merged_ref[rows, :] = part_ref[rows, :] + got.astype(f32)
    total = merged_ref[0 : 3 * local, :]
    total_out = part_ref[3 * local : 4 * local, :] + got_ref[0:local, :].astype(f32)
    merged_ref[3 * local : 4 * local, :] = total_out
    right_ref[0:8, :] = jnp.zeros((8, width), f32)
    right_ref[0:8, 0 : 3 * local] = thin(dot_nt, basis[0], total)
    right_ref[8:16, :] = thin(dot_nn, basis[1][:, 0:local], total_out)
    right_ref[16:24, :] = thin(dot_nn, basis[2], ffn_ref[0:width, :])
    right_ref[24:32, :] = thin(dot_nn, basis[3], ffn_ref[width : 2 * width, :])


def right_factors(left, part, got, ffn_merged, count):
    width = part.shape[1]
    return pl.pallas_call(
        functools.partial(right_kernel, 1.0 / count),
        out_shape=(
            jax.ShapeDtypeStruct((8, width), f32),
            jax.ShapeDtypeStruct((width, 128), bf16),
            jax.ShapeDtypeStruct((32, width), f32),
            jax.ShapeDtypeStruct(part.shape, f32),
        ),
        in_specs=[VMEM] * 6,
        out_specs=(VMEM,) * 4,
        compiler_params=params(20),
        cost_estimate=cost(part.size * 200, part.size * 30),
        name="right_factors",
    )(left, part, *got, ffn_merged)


def final_kernel(
    inverse, _, right_ref, basis_ref, columns_ref, conv_g, conv_w, conv_m, attn_ref, ffn_ref,
    wq, mq, wo, mo, w1, m1, w2, m2,
    q_w, q_m, q_e, o_w, o_m, o_e, f1_w, f1_m, f1_e, f2_w, f2_m, f2_e, conv_w_new, conv_m_new,
    factors, q_columns, staged, loaded, sems, load_sems,
):
    width = attn_ref.shape[1]
    size = staged.shape[2]
    blocks, at = [], 0
    for m, (sources, outs, columns, rate) in enumerate(
        (
            ((wq, mq), (q_w, q_m, q_e), q_columns, LEARN_RATE),
            ((wo, mo), (o_w, o_m, o_e), columns_ref, FAST_RATE),
            ((w1, m1), (f1_w, f1_m, f1_e), columns_ref, LEARN_RATE),
            ((w2, m2), (f2_w, f2_m, f2_e), columns_ref, LEARN_RATE),
        )
    ):
        for first in range(0, outs[0].shape[0], size):
            blocks.append((m, sources, outs, columns, rate, first, at + first))
        at += outs[0].shape[0]

    arriving = []
    for i, (_, sources, _, _, _, first, _) in enumerate(blocks):
        pairs = [(source.at[pl.ds(first, size), :], loaded.at[i, j]) for j, source in enumerate(sources)]
        arriving.append(start_copies(pairs, load_sems, 2 * i))
    factors[...] = jnp.zeros_like(factors)
    for m in range(4):
        right = right_ref[8 * m : 8 * m + 8, :] * inverse
        high = right.astype(bf16).astype(f32)
        if m == 0:
            stack = [high, right - high, high, jnp.zeros((104, width), f32)]
            q_columns[...] = jnp.concatenate(stack, 0).T.astype(bf16)
            near = basis_ref[...].astype(bf16).astype(f32)
            part = jnp.concatenate([near, near, basis_ref[...] - near], 0)
        else:
            part = jnp.concatenate([high, right - high, high], 0)
        at = 24 * m
        factors[m, at : at + 24, :] = part
    moment = MOMENTUM * conv_m[...] + conv_g[0:9, :] * inverse
    conv_m_new[...] = moment
    conv_w_new[...] = conv_w[...] - FAST_RATE * moment

    slots = staged.shape[0]
    flying = [[] for _ in range(slots)]
    for i, (m, sources, outs, columns, rate, first, at) in enumerate(blocks):
        slot = i % slots
        wait_all(arriving[i])
        wait_all(flying[slot])
        rows = slice(at, at + size)
        merged = attn_ref[rows, :] if m < 2 else ffn_ref[at - attn_ref.shape[0] : at - attn_ref.shape[0] + size, :]
        approx = dot_nn(columns[first : first + size, :], factors[m].astype(bf16))
        fresh = MOMENTUM * loaded[i, 1] + approx
        staged[slot, 0] = loaded[i, 0] - rate * fresh
        staged[slot, 1] = fresh
        staged[slot, 2] = merged - approx
        pairs = [(staged.at[slot, j], outs[j].at[pl.ds(first, size), :]) for j in range(3)]
        flying[slot] = start_copies(pairs, sems, 3 * slot)
    for copies in flying:
        wait_all(copies)


def final_update(token, right, basis, columns, conv, attn_merged, ffn_merged, weights, count):
    width = right.shape[1]
    sizes = [w.shape[0] for w in weights[::2]]
    outs = [jax.ShapeDtypeStruct((size, width), f32) for size in sizes for _ in range(3)]
    conv_out = jax.ShapeDtypeStruct(conv[1].shape, f32)
    return pl.pallas_call(
        functools.partial(final_kernel, 1.0 / count),
        out_shape=(*outs, conv_out, conv_out),
        in_specs=[ANYWHERE] + [VMEM] * 8 + [pl.BlockSpec(memory_space=pltpu.HBM)] * 8,
        out_specs=(ANYWHERE,) * len(outs) + (VMEM,) * 2,
        scratch_shapes=[
            pltpu.VMEM((4, 128, width), f32),
            pltpu.VMEM((width, 128), bf16),
            pltpu.VMEM((4, 3, 192, width), f32),
            pltpu.VMEM((sum(sizes) // 192, 2, 192, width), f32),
            pltpu.SemaphoreType.DMA((12,)),
            pltpu.SemaphoreType.DMA((2 * sum(sizes) // 192,)),
        ],
        compiler_params=params(54),
        cost_estimate=cost(6 * width * width * 256, 50 << 20),
        name="final_update",
    )(token, right, basis, columns, *conv, attn_merged, ffn_merged, *weights)


def mod_kernel(
    inverse, slot_ref, silu_ref, own_ref, got_ref, conv_w, conv_m, w_ref, m_ref,
    conv_w_new, conv_m_new, w_new, m_new, rows, weights, moments, load_sems, sems,
):
    width = own_ref.shape[1]
    arriving = []
    for j in range(6):
        lanes = pl.ds(j * width, width)
        pairs = [(w_ref.at[:, lanes], weights.at[:, lanes]), (m_ref.at[:, lanes], moments.at[:, lanes])]
        arriving.append(start_copies(pairs, load_sems, 2 * j))
    count = own_ref.shape[0] - 16
    mine = pl.multiple_of(slot_ref[0] * count, 16)
    rows[pl.ds(mine, count), :] = own_ref[16 : 16 + count, :]
    rows[pl.ds(count - mine, count), :] = got_ref[16 : 16 + count, :]
    gradient = own_ref[0:16, :].astype(f32) + got_ref[0:16, :].astype(f32)
    moment = MOMENTUM * conv_m[...] + gradient[0:9, :] * inverse
    conv_m_new[...] = moment
    conv_w_new[...] = conv_w[...] - LEARN_RATE * moment
    shape = (silu_ref.shape[0], 2 * count)
    row = lax.broadcasted_iota(jnp.int32, shape, 0)
    col = lax.broadcasted_iota(jnp.int32, shape, 1)
    leaving = []
    for j in range(6):
        pick = jnp.where(col == 8 * row + j, 1.0, 0.0).astype(bf16)
        silu = dot_tn(silu_ref[...], pick).astype(bf16)
        mean = dot_nn(silu, rows[...]) * inverse
        wait_all(arriving[j])
        here = slice(j * width, (j + 1) * width)
        moment = MOMENTUM * moments[:, here] + mean
        moments[:, here] = moment
        weights[:, here] = weights[:, here] - LEARN_RATE * moment
        lanes = pl.ds(j * width, width)
        pairs = [(weights.at[:, lanes], w_new.at[:, lanes]), (moments.at[:, lanes], m_new.at[:, lanes])]
        leaving += start_copies(pairs, sems, 2 * j)
    wait_all(leaving)


def mod_update(slot, silu, own, got, w_mod, mom_mod, conv, mom_conv, count):
    width = own.shape[1]
    hbm = pl.BlockSpec(memory_space=pltpu.HBM)
    conv_new, mom_conv_new, w_new, mom_new = pl.pallas_call(
        functools.partial(mod_kernel, 1.0 / count),
        out_shape=(jax.ShapeDtypeStruct(conv.shape, f32),) * 2 + (jax.ShapeDtypeStruct(w_mod.shape, f32),) * 2,
        in_specs=[SMEM] + [VMEM] * 5 + [hbm] * 2,
        out_specs=(VMEM, VMEM, ANYWHERE, ANYWHERE),
        scratch_shapes=[
            pltpu.VMEM((2 * own.shape[0] - 32, width), bf16),
            pltpu.VMEM(w_mod.shape, f32),
            pltpu.VMEM(w_mod.shape, f32),
            pltpu.SemaphoreType.DMA((12,)),
            pltpu.SemaphoreType.DMA((12,)),
        ],
        compiler_params=params(54),
        cost_estimate=cost(100 * w_mod.size, 16 * w_mod.size),
        name="mod_update",
    )(slot, silu, own, got, conv, mom_conv, w_mod, mom_mod)
    return w_new, mom_new, conv_new, mom_conv_new


def leave_kernel(slot_ref, own_ref, got_ref, out_ref, grad_ref):
    mine = slot_ref[0]
    for i, target in enumerate((out_ref, grad_ref)):
        target[mine] = own_ref[i]
        target[1 - mine] = got_ref[i]


def leave(slot, own, got):
    return pl.pallas_call(
        leave_kernel,
        out_shape=(jax.ShapeDtypeStruct(own.shape, bf16),) * 2,
        in_specs=[SMEM, VMEM, VMEM],
        out_specs=(VMEM, VMEM),
        compiler_params=params(4),
        cost_estimate=cost(0, 8 * own.size),
        name="leave",
    )(slot, own, got)


def per_device(
    latents, conditions, cotangent, counts, w_mod, mom_mod, conv_attn, mom_conv_attn,
    w_qkv, mom_qkv, err_qkv, start_qkv, w_out, mom_out, err_out, start_out,
    w_fc1, mom_fc1, err_fc1, start_fc1, conv_ffn, mom_conv_ffn, w_fc2, mom_fc2, err_fc2, start_fc2,
):
    slots, share, width = latents.shape
    local = w_out.shape[0]
    rank = start_out.shape[1]
    mp_count = lax.axis_size("mp")
    dp_count = lax.axis_size("dp")
    mp = lax.axis_index("mp")
    dp = lax.axis_index("dp")
    chip, core = mp // 2, mp % 2

    def swap_chip(values):
        return lax.ppermute(values, "mp", [(i, i ^ 2) for i in range(mp_count)])

    def swap_core(values):
        return lax.ppermute(values, "mp", [(i, i ^ 1) for i in range(mp_count)])

    def swap_dp(values, bit):
        return lax.ppermute(values, "dp", [(i, i ^ bit) for i in range(dp_count)])

    bits = [1 << b for b in range(dp_count.bit_length() - 1)]

    def sum_dp(values):
        for bit in bits:
            low = lax.optimization_barrier(values.astype(bf16))
            values = low.astype(f32) + swap_dp(low, bit).astype(f32)
        return values

    def after(values, earlier):
        return lax.optimization_barrier((values, earlier))[0]

    place = (dp ^ (dp >> 1)) & 1
    slot = jnp.reshape(chip, (1,)).astype(jnp.int32)
    idx = jnp.stack(
        [
            2 * chip + core, 2 * (1 - chip) + core, 2 * chip + 1 - core, 2 * (1 - chip) + 1 - core,
            core, place, dp & 3, chip, counts[0] > chip,
        ]
    ).astype(jnp.int32)

    w_qkv_t, mom_qkv_t, err_qkv_t = (
        jnp.swapaxes(a, -1, -2).reshape(3 * local, width) for a in (w_qkv, mom_qkv, err_qkv[0])
    )
    size = w_qkv_t.shape[0] // 4
    near_half = [
        lax.dynamic_slice_in_dim(w_qkv_t, (2 * place + i) * size, size, 0).astype(bf16) for i in range(2)
    ]
    qkv_near = [swap_chip(h) for h in near_half]

    size = w_fc1.shape[0] // 4
    ffn_q = jnp.concatenate(
        [lax.dynamic_slice_in_dim(w, (dp & 3) * size, size, 0).astype(bf16) for w in (w_fc1, w_fc2)], 0
    )
    ffn_near = swap_chip(ffn_q)

    silu_own = after(jax.nn.silu(conditions.astype(f32)).astype(bf16), ffn_q)
    silu_own = silu_own.reshape(slots, dp_count, -1).transpose(1, 0, 2)
    silu_all = lax.all_to_all(silu_own, "dp", split_axis=0, concat_axis=0, tiled=True)
    silu_slot = lax.dynamic_index_in_dim(silu_all, chip, 1, keepdims=False)

    sib_l = swap_core(latents)
    snd_l = lax.dynamic_index_in_dim(after(latents, silu_own), 1 - chip, 0, keepdims=False)
    got_l = swap_chip(snd_l)

    silu_slot = after(silu_slot, (qkv_near, snd_l))
    partial = modulation_part(silu_slot, w_mod, width)
    gathered = lax.all_to_all(partial, "dp", split_axis=0, concat_axis=0, tiled=True)
    out_a = after(w_out, partial).astype(bf16)
    starts_qkv = start_qkv.transpose(0, 2, 1).reshape(3 * rank, local)
    rows = [
        jnp.pad(conv_ffn, ((0, 16 - conv_ffn.shape[0]), (0, 0))),
        jnp.pad(starts_qkv, ((0, 32 - 3 * rank), (0, width - local))),
    ]
    parts = [out_a]
    for values in rows:
        high = lax.reduce_precision(values, 8, 7)
        parts += [high.astype(bf16), (values - high).astype(bf16)]
    out_b = swap_chip(jnp.concatenate(parts, 0))
    snd_c = lax.dynamic_index_in_dim(after(cotangent, out_a), 1 - chip, 0, keepdims=False)
    got_c = swap_chip(snd_c)
    sib_c = swap_core(after(cotangent, out_a))

    near = after(qkv_near, partial)
    qkv_b = near + [swap_dp(near[0], 1), swap_dp(near[1], 2)]
    ffn_near = after(ffn_near, partial)
    ffn_y, ffn_z = swap_dp(ffn_near, 1), swap_dp(ffn_near, 2)
    got_l = after(got_l, gathered)
    sib_got_l = swap_core(got_l)
    lat, conv_one = first_conv(idx, (latents, got_l, sib_l, sib_got_l), conv_attn)
    mod = jnp.sum(gathered, 0)
    wcat, conv_low, proj, att_t, lse, token = attn_forward(idx, conv_one, mod, conv_attn, w_qkv_t, qkv_b)
    att_sib = swap_core(att_t)
    ffn_y, ffn_z, out_b, got_c = after((ffn_y, ffn_z, out_b, got_c), token)
    ffn_pieces = (ffn_near, ffn_y, ffn_z, swap_dp(ffn_z[:size], 1), swap_dp(ffn_y[size:], 2))
    outs_sib = [swap_core(out_a), swap_core(out_b)]
    sib_got_c = swap_core(got_c)
    conv_ffn_b = (out_b[local : local + 16].astype(f32) + out_b[local + 16 : local + 32].astype(f32))[:9]
    starts_qkv_b = out_b[local + 32 : local + 64].astype(f32) + out_b[local + 64 : local + 96].astype(f32)
    starts_qkv_b = starts_qkv_b[: 3 * rank, :local]

    attn, mixed, mixed_t, fgl, cot = second_norm(
        idx, lat, att_t, att_sib, [out_a, out_b, *outs_sib], [cotangent, got_c, sib_c, sib_got_c], mod
    )
    w1_b, w2_b, act_b, hidden_b, snd_ffn, kgrad_b = ffn_first(idx, mixed, mixed_t, fgl, ffn_pieces, conv_ffn_b)
    got_ffn = swap_chip(snd_ffn)
    ffn_b, mix_b, snd_soon, snd_late, kgrad_c = ffn_second(
        mixed, mixed_t, fgl, w1_b, w2_b, act_b, hidden_b, conv_ffn_b
    )
    got_soon = swap_chip(snd_soon)
    ffn_part, mix_part, grad_ffn, kgrad_a = ffn_own(mixed, mixed_t, fgl, w_fc1, w_fc2, conv_ffn, (ffn_b, mix_b))
    mix_part, got_ffn, got_soon = lax.optimization_barrier((mix_part, got_ffn, got_soon))
    mix_got = swap_core(mix_part)
    got_late = swap_chip(after(snd_late, got_soon))
    conv_part, resid_grad, grad_attn, snd_attn, snd_k, snd_v, sums_two = attn_backward(
        lat, attn, cot, mix_part, mix_got, mod, conv_low, proj, att_t, lse, wcat, out_a, out_b
    )
    conv_got = swap_core(conv_part)
    ffn_got = swap_core(after(ffn_part, sums_two))

    part_attn, left_a, bulk = left_attn(
        grad_attn, snd_attn, snd_k, snd_v, got_late, kgrad_b, kgrad_c, err_qkv_t, err_out[0], starts_qkv, starts_qkv_b,
        start_out.T,
    )
    got_bulk = swap_chip(bulk)
    own_out, snd_out, kgrad_attn, mod_rows = tail(
        idx, lat, attn, ffn_part, ffn_got, conv_part, conv_got, cot, resid_grad, sums_two, mod, conv_attn
    )
    got_bulk = after(got_bulk, kgrad_attn)
    got_k = swap_chip(after(snd_k, got_bulk))
    got_v = None
    left_swap = got_bulk[2 * local :].astype(f32)
    merged_ffn, left_ffn = merge_ffn(
        grad_ffn, (got_ffn, got_soon, got_late), err_fc1[0], err_fc2[0], start_fc1.T, start_fc2.T
    )

    sums = jnp.concatenate(
        [left_a + left_swap[:16], left_ffn, kgrad_a + left_swap[16:], kgrad_attn], 0
    ).astype(bf16)
    mod_rows = mod_rows.astype(bf16)
    count = sums.shape[0]
    for bit in bits:
        sent = lax.optimization_barrier(jnp.concatenate([sums, mod_rows], 0))
        if bit == 2:
            sent, got_k = lax.optimization_barrier((sent, got_k))
            got_v = swap_chip(after(snd_v, got_k))
        if bit == 4:
            sent, got_v = lax.optimization_barrier((sent, got_v))
        got = swap_dp(sent, bit)
        total = sent[:count].astype(f32) + got[:count].astype(f32)
        sums = total.astype(bf16)
        mod_rows = jnp.concatenate([mod_rows, got[count:]], 0)

    basis, columns, rights, merged_attn = right_factors(
        total[:32], part_attn, (got_bulk, got_k, got_v), merged_ffn, dp_count
    )
    both = jnp.concatenate(after([sums[48:64], mod_rows], rights), 0)
    other = swap_chip(both)
    count = jnp.arange(dp_count)
    pick = ((dp ^ count)[:, None] == count[None, :]).astype(bf16)
    silu_order = jnp.dot(pick, silu_all.reshape(dp_count, -1)).reshape(silu_all.shape)
    silu_order = silu_order.transpose(1, 0, 2).reshape(dp_count * slots, -1)
    w_mod_new, mom_mod_new, conv_attn_new, mom_conv_attn_new = mod_update(
        slot, silu_order, both, other, w_mod, mom_mod, conv_attn, mom_conv_attn, dp_count
    )
    got_out = swap_chip(after(snd_out, rights))
    right_sum = sum_dp(rights)
    (
        w_qkv_new, mom_qkv_new, err_qkv_new, w_out_new, mom_out_new, err_out_new,
        w_fc1_new, mom_fc1_new, err_fc1_new, w_fc2_new, mom_fc2_new, err_fc2_new,
        conv_ffn_new, mom_conv_ffn_new,
    ) = final_update(
        mom_conv_ffn, right_sum, basis, columns, (total[32:48], conv_ffn, mom_conv_ffn), merged_attn,
        merged_ffn, (w_qkv_t, mom_qkv_t, w_out, mom_out, w_fc1, mom_fc1, w_fc2, mom_fc2), dp_count,
    )
    w_qkv_new, mom_qkv_new, err_qkv_new = (
        jnp.swapaxes(a.reshape(3, local, width), -1, -2) for a in (w_qkv_new, mom_qkv_new, err_qkv_new)
    )

    latents_out, latents_grad = leave(slot, own_out, got_out)
    return (
        latents_out, latents_grad, w_mod_new, mom_mod_new, conv_attn_new, mom_conv_attn_new,
        w_qkv_new, mom_qkv_new, err_qkv_new[None], w_out_new, mom_out_new, err_out_new[None],
        w_fc1_new, mom_fc1_new, err_fc1_new[None], conv_ffn_new, mom_conv_ffn_new,
        w_fc2_new, mom_fc2_new, err_fc2_new[None],
    )


def solution(mesh):
    token = P("dp", "mp", None)
    rows = P("mp", None)
    columns = P(None, "mp")
    placed = (
        token, P("dp", None), token, P("dp"), P("dp", None), P("dp", None), P(), P(),
        P(None, None, "mp"), P(None, None, "mp"), P("dp", None, None, "mp"), P(None, "mp", None),
        rows, rows, P("dp", "mp", None), P(),
        columns, columns, P("dp", None, "mp"), rows,
        columns, columns,
        rows, rows, P("dp", "mp", None), P(),
    )
    results = (
        token, token, P("dp", None), P("dp", None), P(), P(),
        P(None, None, "mp"), P(None, None, "mp"), P("dp", None, None, "mp"),
        rows, rows, P("dp", "mp", None),
        columns, columns, P("dp", None, "mp"),
        columns, columns,
        rows, rows, P("dp", "mp", None),
    )
    return jax.shard_map(per_device, mesh=mesh, in_specs=placed, out_specs=results, check_vma=False)
```
